32 devices in a mesh: seq: 2 (over y), head: 4 (over z), dp: 4 (over x, core).
Axes of the slice: x: 2, y: 2, z: 4, core: 2. Of those that a mesh axis runs over, the one named last changes fastest.
Arguments:
- queries: bfloat16 [2304, 8192], P(('dp', 'seq', 'head')), parts along dimension 0, may hold values from -20 to 20
- routed_keys: bfloat16 [2304, 1024], P(('dp', 'seq', 'head')), parts along dimension 0, may hold values from -4 to 4
- routed_values: bfloat16 [2304, 1024], P(('dp', 'seq', 'head')), parts along dimension 0, may hold values from -6 to 6
- output_gradient: bfloat16 [2304, 8192], P(('dp', 'seq', 'head')), parts along dimension 0, may hold values from -6 to 6
- positions: int32 [2304], P('dp'), parts along dimension 0, may hold values from 0 to 3071, as said below
- counts: int32 [8], P('dp'), parts along dimension 0, may hold values from 1 to 288, as said below
Outputs:
- attended: bfloat16 [2304, 8192], P(('dp', 'seq', 'head')), parts along dimension 0
- grad_query: bfloat16 [2304, 8192], P(('dp', 'seq', 'head')), parts along dimension 0
- key_state_gradient: bfloat16 [2304, 1024], P(('dp', 'seq', 'head')), parts along dimension 0
- value_state_gradient: bfloat16 [2304, 1024], P(('dp', 'seq', 'head')), parts along dimension 0
The draws below stay inside these ranges and needn't reach their ends.
There are 4 independent parts, one for each index of `dp`. The reference program is written for one: setup_inputs(seed, part) draws one part's arguments, and reference() takes and returns one part's arrays. A program takes and returns all parts, laid end to end along the dimension named above; each array names one. Nothing has to cross between parts.
Inputs may be any that keep to these rules, and one draw needn't show every extreme that they name: `counts`: one sequence shard has exactly 288; every other shard has 96 or more. Within shard s all positions lie in s * 1536 to (s + 1) * 1536 - 1 and are distinct; the live slots of a shard are strictly increasing.
All inputs are finite; a program needn't handle non-finite values.
Results may differ from the reference program's by a relative error of at most 0.018.
Values may be sent and summed in bfloat16 or wider, within the bound.
No kernel may reach another device: no remote copies, remote signals or barrier semaphores. Data moves between devices by JAX's collectives and lax.ppermute only.
A program may use at most 128 MiB of HBM per device.

```python
import jax
import jax.numpy as jnp
from jax import lax

QUERY_HEADS = 64
KEY_VALUE_HEADS = 8
HEAD_WIDTH = 128
TOK_SHARD = 1536
CAP = 288
ROUTED_SLOTS = 576
N_SEQ = 2


def routed_counts(key, part):
    shard_total = N_SEQ
    other_count = shard_total - 1
    low_count = CAP // 3
    spread_steps = (CAP - low_count) // 4
    first_step = jax.random.randint(jax.random.fold_in(key, 23), (), 0, spread_steps)
    first_share = low_count + jnp.asarray(part, jnp.int32) % 4 + 4 * first_step
    shares = jax.random.randint(jax.random.fold_in(key, 21), (other_count,), low_count, CAP + 1)
    shares = shares.at[0].set(first_share)
    big_shard = jax.random.randint(jax.random.fold_in(key, 22), (), 0, shard_total)
    every_index = jnp.arange(shard_total)
    source_index = jnp.clip(every_index - (every_index > big_shard).astype(jnp.int32), 0, other_count - 1)
    return jnp.where(every_index == big_shard, CAP, shares[source_index]).astype(jnp.int32)


def draw_counts(key, part):
    shared = routed_counts(key, part)
    return shared


def draw_positions(key, part):
    shard_counts = routed_counts(key, part)
    key = jax.random.fold_in(key, 7)
    shard_keys = jax.random.split(key, N_SEQ)
    orders = jax.vmap(lambda one_key: jax.random.permutation(one_key, TOK_SHARD))(shard_keys)
    picked_rows = orders[:, :CAP].astype(jnp.int32)
    slot_index = jnp.arange(CAP)
    is_live = slot_index[None, :] < shard_counts[:, None]
    order_key = jnp.where(is_live, picked_rows, picked_rows + TOK_SHARD)
    sorted_keys = jnp.sort(order_key, axis=1)
    within = jnp.where(sorted_keys >= TOK_SHARD, sorted_keys - TOK_SHARD, sorted_keys)
    placed = within + jnp.arange(N_SEQ, dtype=jnp.int32)[:, None] * TOK_SHARD
    return placed.reshape(ROUTED_SLOTS).astype(jnp.int32)


def draw_routed_keys(key, part):
    key = jax.random.fold_in(key, 3)
    unrotated_input = jax.random.truncated_normal(key, -4.0, 4.0, (ROUTED_SLOTS, KEY_VALUE_HEADS * HEAD_WIDTH), jnp.float32)
    return unrotated_input.astype(jnp.bfloat16)


def draw_queries(key, part):
    key = jax.random.fold_in(key, 4)
    unrotated_input = jax.random.truncated_normal(key, -4.0, 4.0, (ROUTED_SLOTS, QUERY_HEADS * HEAD_WIDTH), jnp.float32)
    return unrotated_input.astype(jnp.bfloat16)


def level_of(own_key, dims, cuts, low, high):
    def one(dim, shards_of):
        heights = jax.random.uniform(jax.random.fold_in(jax.random.fold_in(own_key, 6), dim), (shards_of,), jnp.float32, low / len(cuts), high / len(cuts))
        return jnp.repeat(jnp.exp(heights), dims[dim] // shards_of).reshape((-1,) + (1,) * (len(dims) - dim - 1))

    loudness = one(*cuts[0])
    for cut in cuts[1:]:
        loudness = loudness * one(*cut)
    return loudness


def gaussian(stream_key, extent, spread, most, shards=(), kind=jnp.bfloat16):
    values = jax.random.normal(stream_key, extent, jnp.float32) * spread
    if len(shards) > 0:
        values = level_of(stream_key, extent, shards, -0.22, 0.18) * values
    return jnp.clip(values, min=-most, max=most).astype(kind)


def setup_inputs(seed: int = 0, part: int = 0) -> dict:
    arg_keys = jax.random.split(jax.random.key(seed), 7)
    own_keys = jax.random.split(jax.random.fold_in(arg_keys[6], part), 7)
    return {
        "queries": draw_queries(jax.random.fold_in(jax.random.fold_in(arg_keys[6], part), 71), part),
        "routed_keys": draw_routed_keys(jax.random.fold_in(jax.random.fold_in(arg_keys[6], part), 71), part),
        "routed_values": gaussian(own_keys[2], (ROUTED_SLOTS, KEY_VALUE_HEADS * HEAD_WIDTH), 1.0, 6.0, ((0, 8),)),
        "output_gradient": gaussian(own_keys[3], (ROUTED_SLOTS, QUERY_HEADS * HEAD_WIDTH), 1.0, 6.0, ((0, 8),)),
        "positions": draw_positions(jax.random.fold_in(jax.random.fold_in(arg_keys[6], part), 71), part),
        "counts": draw_counts(jax.random.fold_in(jax.random.fold_in(arg_keys[6], part), 71), part),
    }


ROPE_BASE = 500000.0

def rope_angles(position):
    inverse_freq = jnp.float32(ROPE_BASE) ** (-(jnp.arange(HEAD_WIDTH // 2, dtype=jnp.float32) * 2.0 / HEAD_WIDTH))
    angle_table = position.astype(jnp.float32)[:, None] * inverse_freq[None, :]
    return (jnp.cos(angle_table), jnp.sin(angle_table))

def apply_rotary(vectors, cosine_table, sine_values):
    half_size = vectors.shape[-1] // 2
    lower_half = vectors[..., :half_size]
    upper_half = vectors[..., half_size:]
    cosine_table = cosine_table[:, None, :]
    sine_values = sine_values[:, None, :]
    return jnp.concatenate([lower_half * cosine_table - upper_half * sine_values, upper_half * cosine_table + lower_half * sine_values], -1)

def invert_rotary(vectors, cosine_table, sine_values):
    half_size = vectors.shape[-1] // 2
    lower_half = vectors[..., :half_size]
    upper_half = vectors[..., half_size:]
    cosine_table = cosine_table[:, None, :]
    sine_values = sine_values[:, None, :]
    return jnp.concatenate([lower_half * cosine_table + upper_half * sine_values, upper_half * cosine_table - lower_half * sine_values], -1)

def round_trip(values_in):
    return lax.optimization_barrier(values_in.astype(jnp.bfloat16)).astype(jnp.float32)

def reference(queries, routed_keys, routed_values, output_gradient, positions, counts):
    routed_count = positions.shape[0]
    capacity = routed_count // N_SEQ
    heads_per_group = QUERY_HEADS // KEY_VALUE_HEADS
    score_scale = 1.0 / jnp.sqrt(jnp.float32(HEAD_WIDTH))
    is_valid = jnp.arange(routed_count) % capacity < jnp.repeat(counts, capacity, total_repeat_length=routed_count)
    query_live = is_valid.astype(jnp.float32)
    cosine_table, sine_values = rope_angles(positions)
    query_rotated = apply_rotary(queries.astype(jnp.float32).reshape(routed_count, QUERY_HEADS, HEAD_WIDTH), cosine_table, sine_values).astype(jnp.bfloat16)
    key_rotated = apply_rotary(routed_keys.astype(jnp.float32).reshape(routed_count, KEY_VALUE_HEADS, HEAD_WIDTH), cosine_table, sine_values).astype(jnp.bfloat16)
    allowed = (positions[None, :] <= positions[:, None]) & is_valid[None, :]

    def attend_group(pieces):
        query_group, key_group, value_group, grad_group = pieces
        query_f = query_group.astype(jnp.float32)
        key_f = key_group.astype(jnp.float32)
        value_f = value_group.astype(jnp.float32)
        grad_f = grad_group.astype(jnp.float32)
        scores = jnp.einsum('qhd,kd->hqk', query_f, key_f) * score_scale
        scores = jnp.where(allowed[None], scores, -1e+30)
        row_max = lax.optimization_barrier(jnp.max(scores, -1, keepdims=True))
        weights = jnp.exp(scores - row_max)
        probs = weights / lax.optimization_barrier(jnp.sum(weights, -1, keepdims=True)) * query_live[None, :, None]
        probs_low = round_trip(probs)
        attended = jnp.einsum('hqk,kd->qhd', probs_low, value_f).astype(jnp.bfloat16)
        dprob = jnp.einsum('qhd,kd->hqk', grad_f, value_f)
        delta = lax.optimization_barrier(jnp.sum(grad_f * lax.optimization_barrier(attended).astype(jnp.float32), -1)).T
        dscore = round_trip(probs * (dprob - delta[:, :, None]))
        grad_q = jnp.einsum('hqk,kd->qhd', dscore, key_f) * score_scale
        key_gradient = jnp.einsum('hqk,qhd->kd', dscore, query_f) * score_scale
        value_gradient = jnp.einsum('hqk,qhd->kd', probs_low, grad_f)
        return (attended, grad_q, key_gradient, value_gradient)
    grouped_queries = query_rotated.reshape(routed_count, KEY_VALUE_HEADS, heads_per_group, HEAD_WIDTH).transpose(1, 0, 2, 3)
    gradient_groups = output_gradient.reshape(routed_count, KEY_VALUE_HEADS, heads_per_group, HEAD_WIDTH).transpose(1, 0, 2, 3)
    key_groups = key_rotated.transpose(1, 0, 2)
    grouped_values = routed_values.reshape(routed_count, KEY_VALUE_HEADS, HEAD_WIDTH).transpose(1, 0, 2)
    attended, grad_q, key_gradient, value_gradient = lax.map(attend_group, (grouped_queries, key_groups, grouped_values, gradient_groups))
    attended = attended.transpose(1, 0, 2, 3).reshape(routed_count, QUERY_HEADS * HEAD_WIDTH)
    grad_q = grad_q.transpose(1, 0, 2, 3).reshape(routed_count, QUERY_HEADS, HEAD_WIDTH)
    grad_query = invert_rotary(grad_q, cosine_table, sine_values).astype(jnp.bfloat16).reshape(routed_count, QUERY_HEADS * HEAD_WIDTH)
    key_state_gradient = invert_rotary(key_gradient.transpose(1, 0, 2), cosine_table, sine_values).astype(jnp.bfloat16).reshape(routed_count, KEY_VALUE_HEADS * HEAD_WIDTH)
    value_state_gradient = value_gradient.transpose(1, 0, 2).reshape(routed_count, KEY_VALUE_HEADS * HEAD_WIDTH).astype(jnp.bfloat16)
    return (attended, grad_query, key_state_gradient, value_state_gradient)
```

```python
import functools

import jax
import jax.numpy as jnp
import numpy as np
from jax import lax
from jax.experimental import pallas as pl
from jax.experimental.pallas import tpu as pltpu
from jax.sharding import PartitionSpec as P

QUERY_HEADS = 64
KEY_VALUE_HEADS = 8
HEAD_WIDTH = 128
GROUP = QUERY_HEADS // KEY_VALUE_HEADS
ROPE_BASE = 500000.0
SCORE_SCALE = 1.0 / float(np.sqrt(HEAD_WIDTH))
LOG2_E = 1.4426950408889634
CHUNKS = 2
HEADS_PER_CHUNK = KEY_VALUE_HEADS // CHUNKS
CHUNK_COLS = HEADS_PER_CHUNK * HEAD_WIDTH
VMEM = pl.BlockSpec(memory_space=pltpu.VMEM)
SMEM = pl.BlockSpec(memory_space=pltpu.SMEM)


def inverse_freq_row():
    half = HEAD_WIDTH // 2
    place = lax.rem(lax.broadcasted_iota(jnp.int32, (8, HEAD_WIDTH), 1), half)
    row = jnp.ones((8, HEAD_WIDTH), jnp.float32)
    for i in range(1, half):
        row = jnp.where(place == i, np.float32(ROPE_BASE ** (-2.0 * i / HEAD_WIDTH)), row)
    return row[0:1]


def rope(vectors, cosine, sine):
    return vectors * cosine + pltpu.roll(vectors, HEAD_WIDTH // 2, 1) * sine


def rope_back(vectors, cosine, sine):
    return vectors * cosine - pltpu.roll(vectors, HEAD_WIDTH // 2, 1) * sine


def head_cols(index):
    return slice(index * HEAD_WIDTH, (index + 1) * HEAD_WIDTH)


def prepare_keys(rows, pos_ref, key_ref, value_ref, *out_refs):
    kv_refs, (cos_ref, sin_ref) = out_refs[:CHUNKS], out_refs[CHUNKS:]
    padded = key_ref.shape[0]
    start = (lax.axis_index("seq") * lax.axis_size("head") + lax.axis_index("head")) * rows
    sublane = lax.broadcasted_iota(jnp.int32, (8, HEAD_WIDTH), 0)
    pieces = []
    for base in range(0, padded, 8):
        piece = jnp.zeros((8, HEAD_WIDTH), jnp.int32)
        for offset in range(min(8, rows - base)):
            piece = jnp.where(sublane == offset, pos_ref[start + (base + offset)], piece)
        pieces.append(piece)
    angle = jnp.concatenate(pieces, 0).astype(jnp.float32) * inverse_freq_row()
    lane = lax.broadcasted_iota(jnp.int32, angle.shape, 1)
    cosine = jnp.cos(angle)
    sine = jnp.sin(angle) * jnp.where(lane < HEAD_WIDTH // 2, -1.0, 1.0)
    cos_ref[...] = cosine
    sin_ref[...] = sine
    for head in range(KEY_VALUE_HEADS):
        chunk, place = divmod(head, HEADS_PER_CHUNK)
        rotated = rope(key_ref[:, head_cols(head)].astype(jnp.float32), cosine, sine)
        kv_refs[chunk][:, head_cols(place)] = rotated.astype(jnp.bfloat16)
        kv_refs[chunk][:, head_cols(HEADS_PER_CHUNK + place)] = value_ref[:, head_cols(head)]


def prepare_queries(query_ref, grad_ref, cos_ref, sin_ref, q_ref, qt_ref, g_ref, gt_ref, table_ref):
    cosine, sine = cos_ref[...], sin_ref[...]
    queries = jnp.concatenate(
        [
            rope(query_ref[:, head_cols(h)].astype(jnp.float32), cosine, sine)
            for h in range(GROUP)
        ],
        0,
    )
    grads = jnp.concatenate(
        [grad_ref[:, head_cols(h)].astype(jnp.float32) for h in range(GROUP)], 0
    )
    q_ref[0] = queries.astype(jnp.bfloat16)
    qt_ref[0] = queries.T.astype(jnp.bfloat16)
    g_ref[0] = grads.astype(jnp.bfloat16)
    gt_ref[0] = grads.T.astype(jnp.bfloat16)
    table_ref[...] = cosine


def dot(left, right):
    return jnp.dot(left, right, preferred_element_type=jnp.float32)


def attend(seq_count, head_count, rows, has_alias, counts_ref, *refs):
    blocks = seq_count * head_count
    kv_refs = refs[:blocks]
    q_ref, qt_ref, g_ref, gt_ref, cos_ref, sin_ref = refs[blocks : blocks + 6]
    outs = refs[blocks + 6 + 2 * has_alias :]
    out_ref, grad_ref = outs[:2]
    part_refs = outs[2 : 2 + seq_count]
    bias_ref, live_ref = outs[2 + seq_count :]
    padded = kv_refs[0].shape[0]
    query_rows = GROUP * padded
    step = pl.program_id(0)
    seq_index, head_index = lax.axis_index("seq"), lax.axis_index("head")
    my_rank = seq_index * head_count + head_index

    @pl.when(step == 0)
    def _():
        key_row = lax.broadcasted_iota(jnp.int32, (padded, query_rows), 0)
        query_row = lax.rem(lax.broadcasted_iota(jnp.int32, (padded, query_rows), 1), padded)
        for block in range(blocks):
            seq_offset, head_offset = divmod(block, head_count)
            seq_from = jnp.bitwise_xor(seq_index, seq_offset)
            head_from = jnp.bitwise_xor(head_index, head_offset)
            rank = seq_from * head_count + head_from
            limit = jnp.minimum(counts_ref[seq_from] - head_from * rows, rows)
            limit = jnp.where(rank <= my_rank, limit, 0)
            allowed = key_row < limit
            if block == 0:
                allowed = allowed & (key_row <= query_row)
                live_ref[...] = (query_row[:8] < limit).astype(jnp.float32)
            bias_ref[block * padded : (block + 1) * padded, :] = jnp.where(allowed, 0.0, -1e30)

    cols = pl.ds(pl.multiple_of(step * HEAD_WIDTH, HEAD_WIDTH), HEAD_WIDTH)
    far_cols = pl.ds(pl.multiple_of(CHUNK_COLS + step * HEAD_WIDTH, HEAD_WIDTH), HEAD_WIDTH)
    keys_wide = jnp.concatenate([ref[:, cols].astype(jnp.float32) for ref in kv_refs], 0)
    values_wide = jnp.concatenate([ref[:, far_cols].astype(jnp.float32) for ref in kv_refs], 0)
    keys, keys_t = keys_wide.astype(jnp.bfloat16), keys_wide.T.astype(jnp.bfloat16)
    values, values_t = values_wide.astype(jnp.bfloat16), values_wide.T.astype(jnp.bfloat16)
    queries, queries_t = q_ref[0], qt_ref[0]
    grads, grads_t = g_ref[0], gt_ref[0]

    scores = dot(keys, queries_t) * (SCORE_SCALE * LOG2_E) + bias_ref[...]
    weights = jnp.exp2(scores - jnp.max(scores, 0, keepdims=True))
    row_total = jnp.sum(weights, 0, keepdims=True)
    probs = weights * (live_ref[0:1, :] / row_total)
    probs_low = probs.astype(jnp.bfloat16)
    out_t = dot(values_t, probs_low)
    delta = jnp.sum(
        grads_t.astype(jnp.float32) * out_t.astype(jnp.bfloat16).astype(jnp.float32),
        0,
        keepdims=True,
    )
    dscore = (probs * (dot(values, grads_t) - delta)).astype(jnp.bfloat16)
    grad_t = dot(keys_t, dscore) * SCORE_SCALE
    key_part = dot(dscore, queries) * SCORE_SCALE
    value_part = dot(probs_low, grads)

    cosine, sine = cos_ref[...], sin_ref[...]
    out_heads, grad_heads = out_t.T, grad_t.T
    for h in range(GROUP):
        piece = slice(h * padded, (h + 1) * padded)
        out_ref[:, head_cols(h)] = out_heads[piece].astype(jnp.bfloat16)
        grad_ref[:, head_cols(h)] = rope_back(grad_heads[piece], cosine, sine).astype(jnp.bfloat16)
    for block in range(blocks):
        seq_offset, head_offset = divmod(block, head_count)
        piece = slice(block * padded, (block + 1) * padded)
        part_refs[seq_offset][head_offset, :, cols] = key_part[piece].astype(jnp.bfloat16)
        part_refs[seq_offset][head_offset, :, far_cols] = value_part[piece].astype(jnp.bfloat16)


def combine(seq_count, head_count, *refs):
    part_refs, base_ref, send_refs = refs[:seq_count], refs[seq_count], refs[seq_count + 1 :]
    for offset in range(head_count):
        total = part_refs[0][offset].astype(jnp.float32)
        for ref in part_refs[1:]:
            total = total + ref[offset].astype(jnp.float32)
        if offset == 0:
            base_ref[...] = total
        else:
            send_refs[offset - 1][...] = total.astype(jnp.bfloat16)


def finish(head_count, *refs):
    cosine, sine = refs[0][...], refs[1][...]
    key_ref, value_ref = refs[-2:]
    for chunk in range(CHUNKS):
        mine = refs[2 + chunk * head_count : 2 + (chunk + 1) * head_count]
        for place in range(HEADS_PER_CHUNK):
            here, there = head_cols(place), head_cols(HEADS_PER_CHUNK + place)
            key_total, value_total = mine[0][:, here], mine[0][:, there]
            for ref in mine[1:]:
                key_total = key_total + ref[:, here].astype(jnp.float32)
                value_total = value_total + ref[:, there].astype(jnp.float32)
            cols = head_cols(chunk * HEADS_PER_CHUNK + place)
            key_ref[:, cols] = rope_back(key_total, cosine, sine).astype(jnp.bfloat16)
            value_ref[:, cols] = value_total.astype(jnp.bfloat16)


def params(mebibytes):
    return pltpu.CompilerParams(vmem_limit_bytes=mebibytes << 20)


def cost(microseconds):
    return pl.CostEstimate(
        flops=microseconds * 1153 * 10**6,
        bytes_accessed=microseconds * 3690 * 10**3,
        transcendentals=0,
    )


def shards(queries, routed_keys, routed_values, output_gradient, positions, counts):
    seq_count = lax.axis_size("seq")
    head_count = lax.axis_size("head")
    blocks = seq_count * head_count
    rows = queries.shape[0]
    padded = -(-rows // 8) * 8
    if padded != rows:
        extra = ((0, padded - rows), (0, 0))
        queries, routed_keys, routed_values, output_gradient = (
            jnp.pad(x, extra) for x in (queries, routed_keys, routed_values, output_gradient)
        )
    query_rows = GROUP * padded
    shape = jax.ShapeDtypeStruct
    bf16, f32 = jnp.bfloat16, jnp.float32
    ranks = [(s, z) for s in range(seq_count) for z in range(head_count)]

    def rank_of(s, z):
        return s * head_count + z

    def along_head(x, offset, upward, held=0):
        pairs = []
        for s, z in ranks:
            other = z ^ offset
            if s < seq_count - 1 or ((z ^ held) < other) == upward:
                pairs.append((rank_of(s, z), rank_of(s, other)))
        return lax.ppermute(x, ("seq", "head"), pairs)

    def along_seq(x, offset, upward):
        pairs = [
            (rank_of(s, z), rank_of(s ^ offset, z))
            for s, z in ranks
            if (s < (s ^ offset)) == upward
        ]
        return lax.ppermute(x, ("seq", "head"), pairs)

    table = shape((padded, HEAD_WIDTH), f32)
    piece = shape((padded, 2 * CHUNK_COLS), bf16)
    *own, cosine, sine = pl.pallas_call(
        functools.partial(prepare_keys, rows),
        out_shape=[piece] * CHUNKS + [table, table],
        in_specs=[SMEM, VMEM, VMEM],
        out_specs=[VMEM] * (CHUNKS + 2),
        compiler_params=params(56),
        name="prepare_keys",
    )(positions, routed_keys, routed_values)

    wide = GROUP * HEAD_WIDTH
    row_block = pl.BlockSpec((padded, wide), lambda g: (0, g))
    table_block = pl.BlockSpec((padded, HEAD_WIDTH), lambda g: (0, 0))
    tall_block = pl.BlockSpec((1, query_rows, HEAD_WIDTH), lambda g: (g, 0, 0))
    flat_block = pl.BlockSpec((1, HEAD_WIDTH, query_rows), lambda g: (g, 0, 0))
    tall = shape((KEY_VALUE_HEADS, query_rows, HEAD_WIDTH), bf16)
    flat = shape((KEY_VALUE_HEADS, HEAD_WIDTH, query_rows), bf16)
    *stacked, cosine_later = pl.pallas_call(
        prepare_queries,
        grid=(KEY_VALUE_HEADS,),
        out_shape=[tall, flat, tall, flat, table],
        in_specs=[row_block, row_block, table_block, table_block],
        out_specs=[tall_block, flat_block, tall_block, flat_block]
        + [table_block],
        cost_estimate=cost(7),
        compiler_params=params(16),
        name="prepare_queries",
    )(queries, output_gradient, cosine, sine)

    bits = [1 << b for b in reversed(range((head_count - 1).bit_length()))]
    far = [[[along_seq(x, a, True)] for a in range(1, seq_count)] for x in own]
    gathered = []
    for chunk in range(CHUNKS):
        near = {0: own[chunk]}
        for bit in bits:
            near.update({j ^ bit: along_head(x, bit, True, j) for j, x in near.items()})
            if bit == bits[0] and chunk == 0:
                near[bit], cosine_later, far = lax.optimization_barrier(
                    (near[bit], cosine_later, far)
                )
            if bit == bits[0] and chunk + 1 < CHUNKS:
                own[chunk + 1], near[bit] = lax.optimization_barrier((own[chunk + 1], near[bit]))
        near = [near[j] for j in range(head_count)]
        for a in range(1, seq_count):
            far[chunk][a - 1] += [along_seq(x, a, True) for x in near[1:]]
        gathered.append(near + [x for group in far[chunk] for x in group])

    wide_outs = ()
    summed = []
    for chunk in range(CHUNKS):
        first = chunk * HEADS_PER_CHUNK
        has_alias = int(chunk > 0)
        tall_part = pl.BlockSpec((1, query_rows, HEAD_WIDTH), lambda g, f=first: (f + g, 0, 0))
        flat_part = pl.BlockSpec((1, HEAD_WIDTH, query_rows), lambda g, f=first: (f + g, 0, 0))
        row_part = pl.BlockSpec((padded, wide), lambda g, f=first: (0, f + g))
        kv_block = pl.BlockSpec((padded, 2 * CHUNK_COLS), lambda g: (0, 0))
        part_block = pl.BlockSpec((head_count, padded, 2 * CHUNK_COLS), lambda g: (0, 0, 0))
        out = pl.pallas_call(
            functools.partial(attend, seq_count, head_count, rows, has_alias),
            grid=(HEADS_PER_CHUNK,),
            out_shape=[shape((padded, QUERY_HEADS * HEAD_WIDTH), bf16)] * 2
            + [shape((head_count, padded, 2 * CHUNK_COLS), bf16)] * seq_count,
            in_specs=[SMEM]
            + [kv_block] * blocks
            + [tall_part, flat_part, tall_part, flat_part, table_block, table_block]
            + [pl.BlockSpec(memory_space=pl.ANY)] * (2 * has_alias),
            out_specs=[row_part, row_part] + [part_block] * seq_count,
            scratch_shapes=[
                pltpu.VMEM((blocks * padded, query_rows), f32),
                pltpu.VMEM((8, query_rows), f32),
            ],
            input_output_aliases={blocks + 7: 0, blocks + 8: 1} if has_alias else {},
            cost_estimate=cost(10),
            compiler_params=params(32),
            name="attend",
        )(counts, *gathered[chunk], *stacked, cosine_later, sine, *wide_outs)
        wide_outs = out[:2]
        parts = [out[2]] + [along_seq(out[2 + a], a, False) for a in range(1, seq_count)]
        base, *sends = pl.pallas_call(
            functools.partial(combine, seq_count, head_count),
            out_shape=[shape((padded, 2 * CHUNK_COLS), f32)] + [piece] * (head_count - 1),
            in_specs=[VMEM] * seq_count,
            out_specs=[VMEM] * head_count,
            cost_estimate=cost(2),
            compiler_params=params(8),
            name="combine",
        )(*parts)
        summed += [base] + [along_head(x, j + 1, False) for j, x in enumerate(sends)]

    narrow = shape((padded, KEY_VALUE_HEADS * HEAD_WIDTH), bf16)
    key_grad, value_grad = pl.pallas_call(
        functools.partial(finish, head_count),
        out_shape=[narrow, narrow],
        in_specs=[VMEM] * (2 + CHUNKS * head_count),
        out_specs=[VMEM, VMEM],
        cost_estimate=cost(2),
        compiler_params=params(8),
        name="finish",
    )(cosine, sine, *summed)
    results = (*wide_outs, key_grad, value_grad)
    if padded != rows:
        results = tuple(x[:rows] for x in results)
    return results


def solution(mesh):
    rows = P(("dp", "seq", "head"), None)
    return jax.shard_map(
        shards,
        mesh=mesh,
        in_specs=(rows, rows, rows, rows, P("dp"), P("dp")),
        out_specs=(rows, rows, rows, rows),
        check_vma=False,
    )
```

```python
import functools

import jax
import jax.numpy as jnp
import numpy as np
from jax import lax
from jax.experimental import pallas as pl
from jax.experimental.pallas import tpu as pltpu
from jax.sharding import PartitionSpec as P

QUERY_HEADS = 64
KEY_VALUE_HEADS = 8
HEAD_WIDTH = 128
GROUP = QUERY_HEADS // KEY_VALUE_HEADS
ROPE_BASE = 500000.0
SCORE_SCALE = 1.0 / float(np.sqrt(HEAD_WIDTH))
LOG2_E = 1.4426950408889634
CHUNKS = 2
HEADS_PER_CHUNK = KEY_VALUE_HEADS // CHUNKS
CHUNK_COLS = HEADS_PER_CHUNK * HEAD_WIDTH
VMEM = pl.BlockSpec(memory_space=pltpu.VMEM)
SMEM = pl.BlockSpec(memory_space=pltpu.SMEM)


def inverse_freq_row():
    half = HEAD_WIDTH // 2
    place = lax.rem(lax.broadcasted_iota(jnp.int32, (8, HEAD_WIDTH), 1), half)
    row = jnp.ones((8, HEAD_WIDTH), jnp.float32)
    for i in range(1, half):
        row = jnp.where(place == i, np.float32(ROPE_BASE ** (-2.0 * i / HEAD_WIDTH)), row)
    return row[0:1]


def rope(vectors, cosine, sine):
    return vectors * cosine + pltpu.roll(vectors, HEAD_WIDTH // 2, 1) * sine


def rope_back(vectors, cosine, sine):
    return vectors * cosine - pltpu.roll(vectors, HEAD_WIDTH // 2, 1) * sine


def head_cols(index):
    return slice(index * HEAD_WIDTH, (index + 1) * HEAD_WIDTH)


def prepare_keys(rows, pos_ref, key_ref, value_ref, kv_ref, cos_ref, sin_ref):
    padded = key_ref.shape[0]
    start = (lax.axis_index("seq") * lax.axis_size("head") + lax.axis_index("head")) * rows
    sublane = lax.broadcasted_iota(jnp.int32, (8, HEAD_WIDTH), 0)
    pieces = []
    for base in range(0, padded, 8):
        piece = jnp.zeros((8, HEAD_WIDTH), jnp.int32)
        for offset in range(min(8, rows - base)):
            piece = jnp.where(sublane == offset, pos_ref[start + (base + offset)], piece)
        pieces.append(piece)
    angle = jnp.concatenate(pieces, 0).astype(jnp.float32) * inverse_freq_row()
    lane = lax.broadcasted_iota(jnp.int32, angle.shape, 1)
    cosine = jnp.cos(angle)
    sine = jnp.sin(angle) * jnp.where(lane < HEAD_WIDTH // 2, -1.0, 1.0)
    cos_ref[...] = cosine
    sin_ref[...] = sine
    for head in range(KEY_VALUE_HEADS):
        chunk, place = divmod(head, HEADS_PER_CHUNK)
        place += 2 * chunk * HEADS_PER_CHUNK
        rotated = rope(key_ref[:, head_cols(head)].astype(jnp.float32), cosine, sine)
        kv_ref[:, head_cols(place)] = rotated.astype(jnp.bfloat16)
        kv_ref[:, head_cols(HEADS_PER_CHUNK + place)] = value_ref[:, head_cols(head)]


def prepare_queries(query_ref, grad_ref, cos_ref, sin_ref, q_ref, qt_ref, g_ref, gt_ref, table_ref):
    cosine, sine = cos_ref[...], sin_ref[...]
    queries = jnp.concatenate(
        [
            rope(query_ref[:, head_cols(h)].astype(jnp.float32), cosine, sine)
            for h in range(GROUP)
        ],
        0,
    )
    grads = jnp.concatenate(
        [grad_ref[:, head_cols(h)].astype(jnp.float32) for h in range(GROUP)], 0
    )
    q_ref[0] = queries.astype(jnp.bfloat16)
    qt_ref[0] = queries.T.astype(jnp.bfloat16)
    g_ref[0] = grads.astype(jnp.bfloat16)
    gt_ref[0] = grads.T.astype(jnp.bfloat16)
    table_ref[...] = cosine


def dot(left, right):
    return jnp.dot(left, right, preferred_element_type=jnp.float32)


def attend(seq_count, head_count, rows, has_alias, counts_ref, *refs):
    blocks = seq_count * head_count
    kv_refs = refs[:blocks]
    q_ref, qt_ref, g_ref, gt_ref, cos_ref, sin_ref = refs[blocks : blocks + 6]
    outs = refs[blocks + 6 + 2 * has_alias :]
    out_ref, grad_ref = outs[:2]
    part_refs = outs[2 : 2 + seq_count]
    bias_ref, live_ref = outs[2 + seq_count :]
    padded = kv_refs[0].shape[0]
    query_rows = GROUP * padded
    step = pl.program_id(0)
    seq_index, head_index = lax.axis_index("seq"), lax.axis_index("head")
    my_rank = seq_index * head_count + head_index

    @pl.when(step == 0)
    def _():
        key_row = lax.broadcasted_iota(jnp.int32, (padded, query_rows), 0)
        query_row = lax.rem(lax.broadcasted_iota(jnp.int32, (padded, query_rows), 1), padded)
        for block in range(blocks):
            seq_offset, head_offset = divmod(block, head_count)
            seq_from = jnp.bitwise_xor(seq_index, seq_offset)
            head_from = jnp.bitwise_xor(head_index, head_offset)
            rank = seq_from * head_count + head_from
            limit = jnp.minimum(counts_ref[seq_from] - head_from * rows, rows)
            limit = jnp.where(rank <= my_rank, limit, 0)
            allowed = key_row < limit
            if block == 0:
                allowed = allowed & (key_row <= query_row)
                live_ref[...] = (query_row[:8] < limit).astype(jnp.float32)
            bias_ref[block * padded : (block + 1) * padded, :] = jnp.where(allowed, 0.0, -1e30)

    cols = pl.ds(pl.multiple_of(step * HEAD_WIDTH, HEAD_WIDTH), HEAD_WIDTH)
    far_cols = pl.ds(pl.multiple_of(CHUNK_COLS + step * HEAD_WIDTH, HEAD_WIDTH), HEAD_WIDTH)
    keys_wide = jnp.concatenate([ref[:, cols].astype(jnp.float32) for ref in kv_refs], 0)
    values_wide = jnp.concatenate([ref[:, far_cols].astype(jnp.float32) for ref in kv_refs], 0)
    keys, keys_t = keys_wide.astype(jnp.bfloat16), keys_wide.T.astype(jnp.bfloat16)
    values, values_t = values_wide.astype(jnp.bfloat16), values_wide.T.astype(jnp.bfloat16)
    queries, queries_t = q_ref[0], qt_ref[0]
    grads, grads_t = g_ref[0], gt_ref[0]

    scores = dot(keys, queries_t) * (SCORE_SCALE * LOG2_E) + bias_ref[...]
    weights = jnp.exp2(scores - jnp.max(scores, 0, keepdims=True))
    row_total = jnp.sum(weights, 0, keepdims=True)
    probs = weights * (live_ref[0:1, :] / row_total)
    probs_low = probs.astype(jnp.bfloat16)
    out_t = dot(values_t, probs_low)
    delta = jnp.sum(
        grads_t.astype(jnp.float32) * out_t.astype(jnp.bfloat16).astype(jnp.float32),
        0,
        keepdims=True,
    )
    dscore = (probs * (dot(values, grads_t) - delta)).astype(jnp.bfloat16)
    grad_t = dot(keys_t, dscore) * SCORE_SCALE
    key_part = dot(dscore, queries) * SCORE_SCALE
    value_part = dot(probs_low, grads)

    cosine, sine = cos_ref[...], sin_ref[...]
    out_heads, grad_heads = out_t.T, grad_t.T
    for h in range(GROUP):
        piece = slice(h * padded, (h + 1) * padded)
        out_ref[:, head_cols(h)] = out_heads[piece].astype(jnp.bfloat16)
        grad_ref[:, head_cols(h)] = rope_back(grad_heads[piece], cosine, sine).astype(jnp.bfloat16)
    for block in range(blocks):
        seq_offset, head_offset = divmod(block, head_count)
        piece = slice(block * padded, (block + 1) * padded)
        part_refs[seq_offset][head_offset, :, cols] = key_part[piece].astype(jnp.bfloat16)
        part_refs[seq_offset][head_offset, :, far_cols] = value_part[piece].astype(jnp.bfloat16)


def combine(*refs):
    *part_refs, send_ref = refs
    for offset in range(send_ref.shape[0]):
        total = part_refs[0][offset].astype(jnp.float32)
        for ref in part_refs[1:]:
            total = total + ref[offset].astype(jnp.float32)
        send_ref[jnp.bitwise_xor(lax.axis_index("head"), offset)] = total.astype(jnp.bfloat16)


def finish(cos_ref, sin_ref, *refs):
    cosine, sine = cos_ref[...], sin_ref[...]
    *sum_refs, key_ref, value_ref = refs

    def total(ref, place):
        return sum(ref[z, :, head_cols(place)].astype(jnp.float32) for z in range(ref.shape[0]))

    for chunk, ref in enumerate(sum_refs):
        for place in range(HEADS_PER_CHUNK):
            cols = head_cols(chunk * HEADS_PER_CHUNK + place)
            key_ref[:, cols] = rope_back(total(ref, place), cosine, sine).astype(jnp.bfloat16)
            value_ref[:, cols] = total(ref, HEADS_PER_CHUNK + place).astype(jnp.bfloat16)


def params(mebibytes):
    return pltpu.CompilerParams(vmem_limit_bytes=mebibytes << 20)


def cost(microseconds):
    return pl.CostEstimate(
        flops=microseconds * 1153 * 10**6,
        bytes_accessed=microseconds * 3690 * 10**3,
        transcendentals=0,
    )


def shards(queries, routed_keys, routed_values, output_gradient, positions, counts):
    seq_count = lax.axis_size("seq")
    head_count = lax.axis_size("head")
    blocks = seq_count * head_count
    rows = queries.shape[0]
    padded = -(-rows // 8) * 8
    if padded != rows:
        extra = ((0, padded - rows), (0, 0))
        queries, routed_keys, routed_values, output_gradient = (
            jnp.pad(x, extra) for x in (queries, routed_keys, routed_values, output_gradient)
        )
    query_rows = GROUP * padded
    shape = jax.ShapeDtypeStruct
    bf16, f32 = jnp.bfloat16, jnp.float32
    ranks = [(s, z) for s in range(seq_count) for z in range(head_count)]

    def rank_of(s, z):
        return s * head_count + z

    def along_head(x, offset, upward, held=0):
        pairs = []
        for s, z in ranks:
            other = z ^ offset
            if s < seq_count - 1 or ((z ^ held) < other) == upward:
                pairs.append((rank_of(s, z), rank_of(s, other)))
        return lax.ppermute(x, ("seq", "head"), pairs)

    def along_seq(x, offset, upward):
        pairs = [
            (rank_of(s, z), rank_of(s ^ offset, z))
            for s, z in ranks
            if (s < (s ^ offset)) == upward
        ]
        return lax.ppermute(x, ("seq", "head"), pairs)

    table = shape((padded, HEAD_WIDTH), f32)
    own, cosine, sine = pl.pallas_call(
        functools.partial(prepare_keys, rows),
        out_shape=[shape((padded, 2 * KEY_VALUE_HEADS * HEAD_WIDTH), bf16), table, table],
        in_specs=[SMEM, VMEM, VMEM],
        out_specs=[VMEM] * 3,
        compiler_params=params(56),
        name="prepare_keys",
    )(positions, routed_keys, routed_values)

    wide = GROUP * HEAD_WIDTH
    row_block = pl.BlockSpec((padded, wide), lambda g: (0, g))
    table_block = pl.BlockSpec((padded, HEAD_WIDTH), lambda g: (0, 0))
    tall_block = pl.BlockSpec((1, query_rows, HEAD_WIDTH), lambda g: (g, 0, 0))
    flat_block = pl.BlockSpec((1, HEAD_WIDTH, query_rows), lambda g: (g, 0, 0))
    tall = shape((KEY_VALUE_HEADS, query_rows, HEAD_WIDTH), bf16)
    flat = shape((KEY_VALUE_HEADS, HEAD_WIDTH, query_rows), bf16)
    *stacked, cosine_later = pl.pallas_call(
        prepare_queries,
        grid=(KEY_VALUE_HEADS,),
        out_shape=[tall, flat, tall, flat, table],
        in_specs=[row_block, row_block, table_block, table_block],
        out_specs=[tall_block, flat_block, tall_block, flat_block]
        + [table_block],
        cost_estimate=cost(7),
        compiler_params=params(16),
        name="prepare_queries",
    )(queries, output_gradient, cosine, sine)

    bits = [1 << b for b in reversed(range((head_count - 1).bit_length()))]
    later = range(1, seq_count)
    whole = {0: own, **{bit: along_head(own, bit, True) for bit in {bits[0], 1}}}
    far = {(a, 0): along_seq(own, a, True) for a in later}
    whole[1], cosine_later, far = lax.optimization_barrier((whole[1], cosine_later, far))
    far.update({(a, 1): along_seq(whole[1], a, True) for a in later})
    chunked = [
        {j: x[:, 2 * c * CHUNK_COLS : 2 * (c + 1) * CHUNK_COLS] for j, x in whole.items()}
        for c in range(CHUNKS)
    ]
    gathered = []
    for c, near in enumerate(chunked):
        for bit in bits[1:]:
            near.update(
                {j ^ bit: along_head(x, bit, True, j) for j, x in near.items() if j ^ bit not in near}
            )
        if c + 1 < CHUNKS:
            chunked[c + 1][bits[0]], near[head_count - 1], far = lax.optimization_barrier(
                (chunked[c + 1][bits[0]], near[head_count - 1], far)
            )
        blocks_here = [whole[0], whole[1]] + [near[j] for j in range(2, head_count)]
        for a in later:
            blocks_here += [far[a, 0], far[a, 1]]
            blocks_here += [along_seq(near[j], a, True) for j in range(2, head_count)]
        gathered.append(blocks_here)

    wide_outs = ()
    summed = []
    for chunk in range(CHUNKS):
        first = chunk * HEADS_PER_CHUNK
        has_alias = int(chunk > 0)
        tall_part = pl.BlockSpec((1, query_rows, HEAD_WIDTH), lambda g, f=first: (f + g, 0, 0))
        flat_part = pl.BlockSpec((1, HEAD_WIDTH, query_rows), lambda g, f=first: (f + g, 0, 0))
        row_part = pl.BlockSpec((padded, wide), lambda g, f=first: (0, f + g))
        kv_whole = pl.BlockSpec((padded, 2 * CHUNK_COLS), lambda g, c=chunk: (0, c))
        kv_chunk = pl.BlockSpec((padded, 2 * CHUNK_COLS), lambda g: (0, 0))
        part_block = pl.BlockSpec((head_count, padded, 2 * CHUNK_COLS), lambda g: (0, 0, 0))
        out = pl.pallas_call(
            functools.partial(attend, seq_count, head_count, rows, has_alias),
            grid=(HEADS_PER_CHUNK,),
            out_shape=[shape((padded, QUERY_HEADS * HEAD_WIDTH), bf16)] * 2
            + [shape((head_count, padded, 2 * CHUNK_COLS), bf16)] * seq_count,
            in_specs=[SMEM]
            + ([kv_whole] * 2 + [kv_chunk] * (head_count - 2)) * seq_count
            + [tall_part, flat_part, tall_part, flat_part, table_block, table_block]
            + [pl.BlockSpec(memory_space=pl.ANY)] * (2 * has_alias),
            out_specs=[row_part, row_part] + [part_block] * seq_count,
            scratch_shapes=[
                pltpu.VMEM((blocks * padded, query_rows), f32),
                pltpu.VMEM((8, query_rows), f32),
            ],
            input_output_aliases={blocks + 7: 0, blocks + 8: 1} if has_alias else {},
            cost_estimate=cost(10),
            compiler_params=params(32),
            name="attend",
        )(counts, *gathered[chunk], *stacked, cosine_later, sine, *wide_outs)
        wide_outs = out[:2]
        parts = [out[2]] + [along_seq(out[2 + a], a, False) for a in range(1, seq_count)]
        if chunk:
            parts[-1], sums = lax.optimization_barrier((parts[-1], sums))
        sums = pl.pallas_call(
            combine,
            out_shape=shape((head_count, padded, 2 * CHUNK_COLS), bf16),
            in_specs=[VMEM] * seq_count,
            out_specs=VMEM,
            cost_estimate=cost(2),
            compiler_params=params(8),
            name="combine",
        )(*parts)
        summed.append(lax.all_to_all(sums, "head", split_axis=0, concat_axis=0, tiled=True))

    narrow = shape((padded, KEY_VALUE_HEADS * HEAD_WIDTH), bf16)
    key_grad, value_grad = pl.pallas_call(
        finish,
        out_shape=[narrow, narrow],
        in_specs=[VMEM] * (2 + CHUNKS),
        out_specs=[VMEM, VMEM],
        cost_estimate=cost(2),
        compiler_params=params(8),
        name="finish",
    )(cosine, sine, *summed)
    results = (*wide_outs, key_grad, value_grad)
    if padded != rows:
        results = tuple(x[:rows] for x in results)
    return results


def solution(mesh):
    rows = P(("dp", "seq", "head"), None)
    return jax.shard_map(
        shards,
        mesh=mesh,
        in_specs=(rows, rows, rows, rows, P("dp"), P("dp")),
        out_specs=(rows, rows, rows, rows),
        check_vma=False,
    )
```

```python
import functools

import jax
import jax.numpy as jnp
import numpy as np
from jax import lax
from jax.experimental import pallas as pl
from jax.experimental.pallas import tpu as pltpu
from jax.sharding import PartitionSpec as P

QUERY_HEADS = 64
KEY_VALUE_HEADS = 8
HEAD_WIDTH = 128
GROUP = QUERY_HEADS // KEY_VALUE_HEADS
ROPE_BASE = 500000.0
SCORE_SCALE = 1.0 / float(np.sqrt(HEAD_WIDTH))
LOG2_E = 1.4426950408889634
CHUNKS = 2
HEADS_PER_CHUNK = KEY_VALUE_HEADS // CHUNKS
CHUNK_COLS = HEADS_PER_CHUNK * HEAD_WIDTH
STEP_HEADS = 2
VMEM = pl.BlockSpec(memory_space=pltpu.VMEM)
SMEM = pl.BlockSpec(memory_space=pltpu.SMEM)


def inverse_freq_row():
    half = HEAD_WIDTH // 2
    place = lax.rem(lax.broadcasted_iota(jnp.int32, (8, HEAD_WIDTH), 1), half)
    row = jnp.ones((8, HEAD_WIDTH), jnp.float32)
    for i in range(1, half):
        row = jnp.where(place == i, np.float32(ROPE_BASE ** (-2.0 * i / HEAD_WIDTH)), row)
    return row[0:1]


def rope(vectors, cosine, sine):
    return vectors * cosine + pltpu.roll(vectors, HEAD_WIDTH // 2, 1) * sine


def rope_back(vectors, cosine, sine):
    return vectors * cosine - pltpu.roll(vectors, HEAD_WIDTH // 2, 1) * sine


def head_cols(index):
    return slice(index * HEAD_WIDTH, (index + 1) * HEAD_WIDTH)


def prepare_keys(rows, pos_ref, key_ref, value_ref, whole_ref, *out_refs):
    kv_refs, (cos_ref, sin_ref) = out_refs[:CHUNKS], out_refs[CHUNKS:]
    padded = key_ref.shape[0]
    start = (lax.axis_index("seq") * lax.axis_size("head") + lax.axis_index("head")) * rows
    sublane = lax.broadcasted_iota(jnp.int32, (8, HEAD_WIDTH), 0)
    pieces = []
    for base in range(0, padded, 8):
        piece = jnp.zeros((8, HEAD_WIDTH), jnp.int32)
        for offset in range(min(8, rows - base)):
            piece = jnp.where(sublane == offset, pos_ref[start + (base + offset)], piece)
        pieces.append(piece)
    angle = jnp.concatenate(pieces, 0).astype(jnp.float32) * inverse_freq_row()
    lane = lax.broadcasted_iota(jnp.int32, angle.shape, 1)
    cosine = jnp.cos(angle)
    sine = jnp.sin(angle) * jnp.where(lane < HEAD_WIDTH // 2, -1.0, 1.0)
    cos_ref[...] = cosine
    sin_ref[...] = sine
    for head in range(KEY_VALUE_HEADS):
        chunk, place = divmod(head, HEADS_PER_CHUNK)
        rotated = rope(key_ref[:, head_cols(head)].astype(jnp.float32), cosine, sine)
        columns = {
            place: rotated.astype(jnp.bfloat16),
            HEADS_PER_CHUNK + place: value_ref[:, head_cols(head)],
        }
        for column, x in columns.items():
            kv_refs[chunk][:, head_cols(column)] = x
            whole_ref[:, head_cols(2 * chunk * HEADS_PER_CHUNK + column)] = x


def prepare_queries(query_ref, grad_ref, cos_ref, sin_ref, q_ref, qt_ref, g_ref, gt_ref, table_ref):
    cosine, sine = cos_ref[...], sin_ref[...]
    queries = jnp.concatenate(
        [
            rope(query_ref[:, head_cols(h)].astype(jnp.float32), cosine, sine)
            for h in range(GROUP)
        ],
        0,
    )
    grads = jnp.concatenate(
        [grad_ref[:, head_cols(h)].astype(jnp.float32) for h in range(GROUP)], 0
    )
    q_ref[0] = queries.astype(jnp.bfloat16)
    qt_ref[0] = queries.T.astype(jnp.bfloat16)
    g_ref[0] = grads.astype(jnp.bfloat16)
    gt_ref[0] = grads.T.astype(jnp.bfloat16)
    table_ref[...] = cosine


def dot(left, right):
    return jnp.dot(left, right, preferred_element_type=jnp.float32)


def attend(seq_count, head_count, rows, has_alias, counts_ref, *refs):
    blocks = seq_count * head_count
    kv_refs = refs[:blocks]
    q_ref, qt_ref, g_ref, gt_ref, cos_ref, sin_ref = refs[blocks : blocks + 6]
    outs = refs[blocks + 6 + 2 * has_alias :]
    out_ref, grad_ref = outs[:2]
    part_refs = outs[2 : 2 + seq_count]
    bias_ref, live_ref = outs[2 + seq_count :]
    padded = kv_refs[0].shape[0]
    query_rows = GROUP * padded
    step = pl.program_id(0)
    seq_index, head_index = lax.axis_index("seq"), lax.axis_index("head")
    my_rank = seq_index * head_count + head_index

    @pl.when(step == 0)
    def _():
        key_row = lax.broadcasted_iota(jnp.int32, (padded, query_rows), 0)
        query_row = lax.rem(lax.broadcasted_iota(jnp.int32, (padded, query_rows), 1), padded)
        for block in range(blocks):
            seq_offset, head_offset = divmod(block, head_count)
            seq_from = jnp.bitwise_xor(seq_index, seq_offset)
            head_from = jnp.bitwise_xor(head_index, head_offset)
            rank = seq_from * head_count + head_from
            limit = jnp.minimum(counts_ref[seq_from] - head_from * rows, rows)
            limit = jnp.where(rank <= my_rank, limit, 0)
            allowed = key_row < limit
            if block == 0:
                allowed = allowed & (key_row <= query_row)
                live_ref[...] = (query_row[:8] < limit).astype(jnp.float32)
            bias_ref[block * padded : (block + 1) * padded, :] = jnp.where(allowed, 0.0, -1e30)

    def lanes(first, place):
        start = pl.multiple_of((first + step * STEP_HEADS + place) * HEAD_WIDTH, HEAD_WIDTH)
        return pl.ds(start, HEAD_WIDTH)

    def gathered(first, place):
        cols = lanes(first, place)
        wide = jnp.concatenate([ref[:, cols].astype(jnp.float32) for ref in kv_refs], 0)
        return wide.astype(jnp.bfloat16), wide.T.astype(jnp.bfloat16)

    heads = range(STEP_HEADS)
    keys, values = [gathered(0, p) for p in heads], [gathered(HEADS_PER_CHUNK, p) for p in heads]
    bias, live = bias_ref[...], live_ref[0:1, :]
    scores = [dot(keys[p][0], qt_ref[p]) * (SCORE_SCALE * LOG2_E) + bias for p in heads]
    dprobs, probs, probs_low = [], [], []
    for p in heads:
        weights = jnp.exp2(scores[p] - jnp.max(scores[p], 0, keepdims=True))
        probs.append(weights * (live / jnp.sum(weights, 0, keepdims=True)))
        probs_low.append(probs[p].astype(jnp.bfloat16))
        dprobs.append(dot(values[p][0], gt_ref[p]))
    outs_t, value_parts, dscores = [], [], []
    for p in heads:
        outs_t.append(dot(values[p][1], probs_low[p]))
        value_parts.append(dot(probs_low[p], g_ref[p]))
        out_low = outs_t[p].astype(jnp.bfloat16).astype(jnp.float32)
        delta = jnp.sum(gt_ref[p].astype(jnp.float32) * out_low, 0, keepdims=True)
        dscores.append((probs[p] * (dprobs[p] - delta)).astype(jnp.bfloat16))
    grads_t = [dot(keys[p][1], dscores[p]) * SCORE_SCALE for p in heads]
    key_parts = [dot(dscores[p], q_ref[p]) * SCORE_SCALE for p in heads]

    cosine, sine = cos_ref[...], sin_ref[...]
    for p in heads:
        out_heads, grad_heads = outs_t[p].T, grads_t[p].T
        for h in range(GROUP):
            piece, cols = slice(h * padded, (h + 1) * padded), head_cols(p * GROUP + h)
            out_ref[:, cols] = out_heads[piece].astype(jnp.bfloat16)
            grad_ref[:, cols] = rope_back(grad_heads[piece], cosine, sine).astype(jnp.bfloat16)
        for block in range(blocks):
            seq_offset, head_offset = divmod(block, head_count)
            piece = slice(block * padded, (block + 1) * padded)
            part_ref = part_refs[seq_offset]
            part_ref[head_offset, :, lanes(0, p)] = key_parts[p][piece].astype(jnp.bfloat16)
            part_ref[head_offset, :, lanes(HEADS_PER_CHUNK, p)] = value_parts[p][piece].astype(
                jnp.bfloat16
            )


def combine(seq_count, head_count, *refs):
    part_refs, base_ref, send_refs = refs[:seq_count], refs[seq_count], refs[seq_count + 1 :]
    for offset in range(head_count):
        total = part_refs[0][offset].astype(jnp.float32)
        for ref in part_refs[1:]:
            total = total + ref[offset].astype(jnp.float32)
        if offset == 0:
            base_ref[...] = total
        else:
            send_refs[offset - 1][...] = total.astype(jnp.bfloat16)


def finish(head_count, *refs):
    cosine, sine = refs[0][...], refs[1][...]
    key_ref, value_ref = refs[-2:]
    for chunk in range(CHUNKS):
        mine = refs[2 + chunk * head_count : 2 + (chunk + 1) * head_count]
        for place in range(HEADS_PER_CHUNK):
            here, there = head_cols(place), head_cols(HEADS_PER_CHUNK + place)
            key_total, value_total = mine[0][:, here], mine[0][:, there]
            for ref in mine[1:]:
                key_total = key_total + ref[:, here].astype(jnp.float32)
                value_total = value_total + ref[:, there].astype(jnp.float32)
            cols = head_cols(chunk * HEADS_PER_CHUNK + place)
            key_ref[:, cols] = rope_back(key_total, cosine, sine).astype(jnp.bfloat16)
            value_ref[:, cols] = value_total.astype(jnp.bfloat16)


def params(mebibytes):
    return pltpu.CompilerParams(vmem_limit_bytes=mebibytes << 20)


def cost(microseconds):
    return pl.CostEstimate(
        flops=microseconds * 1153 * 10**6,
        bytes_accessed=microseconds * 3690 * 10**3,
        transcendentals=0,
    )


def shards(queries, routed_keys, routed_values, output_gradient, positions, counts):
    seq_count = lax.axis_size("seq")
    head_count = lax.axis_size("head")
    blocks = seq_count * head_count
    rows = queries.shape[0]
    padded = -(-rows // 8) * 8
    if padded != rows:
        extra = ((0, padded - rows), (0, 0))
        queries, routed_keys, routed_values, output_gradient = (
            jnp.pad(x, extra) for x in (queries, routed_keys, routed_values, output_gradient)
        )
    query_rows = GROUP * padded
    shape = jax.ShapeDtypeStruct
    bf16, f32 = jnp.bfloat16, jnp.float32
    ranks = [(s, z) for s in range(seq_count) for z in range(head_count)]

    def rank_of(s, z):
        return s * head_count + z

    def along_head(x, offset, upward, held=0):
        pairs = []
        for s, z in ranks:
            other = z ^ offset
            if s < seq_count - 1 or ((z ^ held) < other) == upward:
                pairs.append((rank_of(s, z), rank_of(s, other)))
        return lax.ppermute(x, ("seq", "head"), pairs)

    def along_seq(x, offset, upward):
        pairs = [
            (rank_of(s, z), rank_of(s ^ offset, z))
            for s, z in ranks
            if (s < (s ^ offset)) == upward
        ]
        return lax.ppermute(x, ("seq", "head"), pairs)

    table = shape((padded, HEAD_WIDTH), f32)
    piece = shape((padded, 2 * CHUNK_COLS), bf16)
    whole, *own, cosine, sine = pl.pallas_call(
        functools.partial(prepare_keys, rows),
        out_shape=[shape((padded, CHUNKS * 2 * CHUNK_COLS), bf16)]
        + [piece] * CHUNKS
        + [table, table],
        in_specs=[SMEM, VMEM, VMEM],
        out_specs=[VMEM] * (CHUNKS + 3),
        compiler_params=params(56),
        name="prepare_keys",
    )(positions, routed_keys, routed_values)

    wide = GROUP * HEAD_WIDTH
    row_block = pl.BlockSpec((padded, wide), lambda g: (0, g))
    table_block = pl.BlockSpec((padded, HEAD_WIDTH), lambda g: (0, 0))
    tall_block = pl.BlockSpec((1, query_rows, HEAD_WIDTH), lambda g: (g, 0, 0))
    flat_block = pl.BlockSpec((1, HEAD_WIDTH, query_rows), lambda g: (g, 0, 0))
    tall = shape((KEY_VALUE_HEADS, query_rows, HEAD_WIDTH), bf16)
    flat = shape((KEY_VALUE_HEADS, HEAD_WIDTH, query_rows), bf16)
    *stacked, cosine_later = pl.pallas_call(
        prepare_queries,
        grid=(KEY_VALUE_HEADS,),
        out_shape=[tall, flat, tall, flat, table],
        in_specs=[row_block, row_block, table_block, table_block],
        out_specs=[tall_block, flat_block, tall_block, flat_block]
        + [table_block],
        cost_estimate=cost(7),
        compiler_params=params(16),
        name="prepare_queries",
    )(queries, output_gradient, cosine, sine)

    bits = [1 << b for b in reversed(range((head_count - 1).bit_length()))]
    later = range(1, seq_count)
    chunked = [{bits[0]: along_head(own[0], bits[0], True)}]
    far = {(a, 0): along_seq(whole, a, True) for a in later}
    nearest = along_head(whole, 1, True)
    chunked[0][bits[0]], own[1:], cosine_later, far = lax.optimization_barrier(
        (chunked[0][bits[0]], own[1:], cosine_later, far)
    )
    chunked += [{bits[0]: along_head(x, bits[0], True)} for x in own[1:]]
    far.update({(a, 1): along_seq(nearest, a, True) for a in later})
    gathered = []
    for c, near in enumerate(chunked):
        near[0] = own[c]
        for bit in bits[1:]:
            near.update(
                {j ^ bit: along_head(x, bit, True, j) for j, x in near.items() if j ^ bit > 1}
            )
        blocks_here = [whole, nearest] + [near[j] for j in range(2, head_count)]
        for a in later:
            blocks_here += [far[a, 0], far[a, 1]]
            blocks_here += [along_seq(near[j], a, True) for j in range(2, head_count)]
        gathered.append(blocks_here)

    wide_outs = ()
    summed = []
    for chunk in range(CHUNKS):
        first = chunk * HEADS_PER_CHUNK // STEP_HEADS
        has_alias = int(chunk > 0)
        tall_part = pl.BlockSpec((STEP_HEADS, query_rows, HEAD_WIDTH), lambda g, f=first: (f + g, 0, 0))
        flat_part = pl.BlockSpec((STEP_HEADS, HEAD_WIDTH, query_rows), lambda g, f=first: (f + g, 0, 0))
        row_part = pl.BlockSpec((padded, STEP_HEADS * wide), lambda g, f=first: (0, f + g))
        kv_whole = pl.BlockSpec((padded, 2 * CHUNK_COLS), lambda g, c=chunk: (0, c))
        kv_chunk = pl.BlockSpec((padded, 2 * CHUNK_COLS), lambda g: (0, 0))
        part_block = pl.BlockSpec((head_count, padded, 2 * CHUNK_COLS), lambda g: (0, 0, 0))
        out = pl.pallas_call(
            functools.partial(attend, seq_count, head_count, rows, has_alias),
            grid=(HEADS_PER_CHUNK // STEP_HEADS,),
            out_shape=[shape((padded, QUERY_HEADS * HEAD_WIDTH), bf16)] * 2
            + [shape((head_count, padded, 2 * CHUNK_COLS), bf16)] * seq_count,
            in_specs=[SMEM]
            + ([kv_whole] * 2 + [kv_chunk] * (head_count - 2)) * seq_count
            + [tall_part, flat_part, tall_part, flat_part, table_block, table_block]
            + [pl.BlockSpec(memory_space=pl.ANY)] * (2 * has_alias),
            out_specs=[row_part, row_part] + [part_block] * seq_count,
            scratch_shapes=[
                pltpu.VMEM((blocks * padded, query_rows), f32),
                pltpu.VMEM((8, query_rows), f32),
            ],
            input_output_aliases={blocks + 7: 0, blocks + 8: 1} if has_alias else {},
            cost_estimate=cost(10),
            compiler_params=params(32),
            name="attend",
        )(counts, *gathered[chunk], *stacked, cosine_later, sine, *wide_outs)
        wide_outs = out[:2]
        parts = [out[2]] + [along_seq(out[2 + a], a, False) for a in range(1, seq_count)]
        base, *sends = pl.pallas_call(
            functools.partial(combine, seq_count, head_count),
            out_shape=[shape((padded, 2 * CHUNK_COLS), f32)] + [piece] * (head_count - 1),
            in_specs=[VMEM] * seq_count,
            out_specs=[VMEM] * head_count,
            cost_estimate=cost(2),
            compiler_params=params(8),
            name="combine",
        )(*parts)
        summed += [base] + [along_head(x, j + 1, False) for j, x in enumerate(sends)]

    narrow = shape((padded, KEY_VALUE_HEADS * HEAD_WIDTH), bf16)
    key_grad, value_grad = pl.pallas_call(
        functools.partial(finish, head_count),
        out_shape=[narrow, narrow],
        in_specs=[VMEM] * (2 + CHUNKS * head_count),
        out_specs=[VMEM, VMEM],
        cost_estimate=cost(2),
        compiler_params=params(8),
        name="finish",
    )(cosine, sine, *summed)
    results = (*wide_outs, key_grad, value_grad)
    if padded != rows:
        results = tuple(x[:rows] for x in results)
    return results


def solution(mesh):
    rows = P(("dp", "seq", "head"), None)
    return jax.shard_map(
        shards,
        mesh=mesh,
        in_specs=(rows, rows, rows, rows, P("dp"), P("dp")),
        out_specs=(rows, rows, rows, rows),
        check_vma=False,
    )
```

```python
import functools

import jax
import jax.numpy as jnp
import numpy as np
from jax import lax
from jax.experimental import pallas as pl
from jax.experimental.pallas import tpu as pltpu
from jax.sharding import PartitionSpec as P

QUERY_HEADS = 64
KEY_VALUE_HEADS = 8
HEAD_WIDTH = 128
GROUP = QUERY_HEADS // KEY_VALUE_HEADS
ROPE_BASE = 500000.0
SCORE_SCALE = 1.0 / float(np.sqrt(HEAD_WIDTH))
SCORE_TO_LOG2 = SCORE_SCALE * 1.4426950408889634
MASK_ROWS = 128
CHUNKS = 2
HEADS_PER_CHUNK = KEY_VALUE_HEADS // CHUNKS
CHUNK_COLS = HEADS_PER_CHUNK * HEAD_WIDTH
STEP_HEADS = 2
VMEM = pl.BlockSpec(memory_space=pltpu.VMEM)
SMEM = pl.BlockSpec(memory_space=pltpu.SMEM)


def inverse_freq_row():
    half = HEAD_WIDTH // 2
    place = lax.rem(lax.broadcasted_iota(jnp.int32, (8, HEAD_WIDTH), 1), half)
    row = jnp.ones((8, HEAD_WIDTH), jnp.float32)
    for i in range(1, half):
        row = jnp.where(place == i, np.float32(ROPE_BASE ** (-2.0 * i / HEAD_WIDTH)), row)
    return row[0:1]


def rope(vectors, cosine, sine):
    return vectors * cosine + pltpu.roll(vectors, HEAD_WIDTH // 2, 1) * sine


def rope_back(vectors, cosine, sine):
    return vectors * cosine - pltpu.roll(vectors, HEAD_WIDTH // 2, 1) * sine


def head_cols(index):
    return slice(index * HEAD_WIDTH, (index + 1) * HEAD_WIDTH)


def prepare_keys(rows, pos_ref, key_ref, value_ref, whole_ref, *out_refs):
    kv_refs, (cos_ref, sin_ref) = out_refs[:CHUNKS], out_refs[CHUNKS:]
    padded = key_ref.shape[0]
    start = (lax.axis_index("seq") * lax.axis_size("head") + lax.axis_index("head")) * rows
    sublane = lax.broadcasted_iota(jnp.int32, (8, HEAD_WIDTH), 0)
    pieces = []
    for base in range(0, padded, 8):
        piece = jnp.zeros((8, HEAD_WIDTH), jnp.int32)
        for offset in range(min(8, rows - base)):
            piece = jnp.where(sublane == offset, pos_ref[start + (base + offset)], piece)
        pieces.append(piece)
    angle = jnp.concatenate(pieces, 0).astype(jnp.float32) * inverse_freq_row()
    lane = lax.broadcasted_iota(jnp.int32, angle.shape, 1)
    cosine = jnp.cos(angle)
    sine = jnp.sin(angle) * jnp.where(lane < HEAD_WIDTH // 2, -1.0, 1.0)
    cos_ref[...] = cosine
    sin_ref[...] = sine
    for head in range(KEY_VALUE_HEADS):
        chunk, place = divmod(head, HEADS_PER_CHUNK)
        rotated = rope(key_ref[:, head_cols(head)].astype(jnp.float32), cosine, sine)
        columns = {
            place: rotated.astype(jnp.bfloat16),
            HEADS_PER_CHUNK + place: value_ref[:, head_cols(head)],
        }
        for column, x in columns.items():
            kv_refs[chunk][:, head_cols(column)] = x
            whole_ref[:, head_cols(2 * chunk * HEADS_PER_CHUNK + column)] = x


def prepare_queries(query_ref, grad_ref, cos_ref, sin_ref, q_ref, qt_ref, g_ref, gt_ref, table_ref):
    cosine, sine = cos_ref[...], sin_ref[...]
    queries = jnp.concatenate(
        [
            rope(query_ref[:, head_cols(h)].astype(jnp.float32), cosine, sine)
            for h in range(GROUP)
        ],
        0,
    )
    grads = jnp.concatenate(
        [grad_ref[:, head_cols(h)].astype(jnp.float32) for h in range(GROUP)], 0
    )
    q_ref[0] = queries.astype(jnp.bfloat16)
    qt_ref[0] = queries.T.astype(jnp.bfloat16)
    g_ref[0] = grads.astype(jnp.bfloat16)
    gt_ref[0] = grads.T.astype(jnp.bfloat16)
    table_ref[...] = cosine


def dot(left, right):
    return jnp.dot(left, right, preferred_element_type=jnp.float32)


def attend(seq_count, head_count, rows, has_alias, counts_ref, *refs):
    blocks = seq_count * head_count
    kv_refs = refs[:blocks]
    q_ref, qt_ref, g_ref, gt_ref, cos_ref, sin_ref = refs[blocks : blocks + 6]
    outs = refs[blocks + 6 + 2 * has_alias :]
    out_ref, grad_ref = outs[:2]
    part_refs = outs[2 : 2 + seq_count]
    key_mask_ref, query_mask_ref, live_ref = outs[2 + seq_count :]
    padded = kv_refs[0].shape[0]
    query_rows = GROUP * padded
    step = pl.program_id(0)
    seq_index, head_index = lax.axis_index("seq"), lax.axis_index("head")
    my_rank = seq_index * head_count + head_index

    @pl.when(step == 0)
    def _():
        shape = (padded, MASK_ROWS)
        key_row = lax.broadcasted_iota(jnp.int32, shape, 0)
        mask_row = lax.broadcasted_iota(jnp.int32, shape, 1)
        for block in range(blocks):
            seq_offset, head_offset = divmod(block, head_count)
            seq_from = jnp.bitwise_xor(seq_index, seq_offset)
            head_from = jnp.bitwise_xor(head_index, head_offset)
            rank = seq_from * head_count + head_from
            limit = jnp.minimum(counts_ref[seq_from] - head_from * rows, rows)
            limit = jnp.where(rank <= my_rank, limit, 0)
            barred = (mask_row == MASK_ROWS - 1) & (key_row >= limit)
            if block == 0:
                barred = barred | ((mask_row < padded) & (key_row > mask_row))
            piece = slice(block * padded, (block + 1) * padded)
            key_mask_ref[piece, :] = jnp.where(barred, -1e30, 0.0)
        shape = (MASK_ROWS, query_rows)
        query_row = lax.rem(lax.broadcasted_iota(jnp.int32, shape, 1), padded)
        mask_row = lax.broadcasted_iota(jnp.int32, shape, 0)
        met = (mask_row == query_row) | (mask_row == MASK_ROWS - 1)
        query_mask_ref[...] = jnp.where(met, 1.0, 0.0).astype(jnp.bfloat16)
        limit = jnp.minimum(counts_ref[seq_index] - head_index * rows, rows)
        live_ref[...] = (query_row[:8] < limit).astype(jnp.float32)

    def lanes(first, place):
        start = pl.multiple_of((first + step * STEP_HEADS + place) * HEAD_WIDTH, HEAD_WIDTH)
        return pl.ds(start, HEAD_WIDTH)

    def gathered(first, place):
        cols = lanes(first, place)
        wide = jnp.concatenate([ref[:, cols].astype(jnp.float32) for ref in kv_refs], 0)
        return wide.astype(jnp.bfloat16), wide.T.astype(jnp.bfloat16)

    heads = range(STEP_HEADS)
    keys, values = [gathered(0, p) for p in heads], [gathered(HEADS_PER_CHUNK, p) for p in heads]
    key_mask, query_mask = key_mask_ref[...].astype(jnp.bfloat16), query_mask_ref[...]
    scores = [
        dot(
            jnp.concatenate([keys[p][0], key_mask], 1), jnp.concatenate([qt_ref[p], query_mask], 0)
        )
        for p in heads
    ]
    inverse, weights, dprobs = [], [], []
    for p in heads:
        top = jnp.max(scores[p], 0, keepdims=True) * SCORE_TO_LOG2
        wide = jnp.exp2(scores[p] * SCORE_TO_LOG2 - top)
        inverse.append(live_ref[...] / jnp.sum(wide, 0, keepdims=True))
        weights.append(wide.astype(jnp.bfloat16))
        dprobs.append(dot(values[p][0], gt_ref[p]))
    outs_t, value_parts, dscores = [], [], []
    for p in heads:
        factor = inverse[p][0:1]
        outs_t.append(dot(values[p][1], weights[p]) * factor)
        scaled = (g_ref[p].astype(jnp.float32) * inverse[p].T[:, 0:1]).astype(jnp.bfloat16)
        value_parts.append(dot(weights[p], scaled))
        out_low = outs_t[p].astype(jnp.bfloat16).astype(jnp.float32)
        delta = jnp.sum(gt_ref[p].astype(jnp.float32) * out_low, 0, keepdims=True) * factor
        dscores.append(
            (weights[p].astype(jnp.float32) * (dprobs[p] * factor - delta)).astype(jnp.bfloat16)
        )
    grads_t = [dot(keys[p][1], dscores[p]) * SCORE_SCALE for p in heads]
    key_parts = [dot(dscores[p], q_ref[p]) * SCORE_SCALE for p in heads]

    cosine, sine = cos_ref[...], sin_ref[...]
    for p in heads:
        out_heads, grad_heads = outs_t[p].T, grads_t[p].T
        for h in range(GROUP):
            piece, cols = slice(h * padded, (h + 1) * padded), head_cols(p * GROUP + h)
            out_ref[:, cols] = out_heads[piece].astype(jnp.bfloat16)
            grad_ref[:, cols] = rope_back(grad_heads[piece], cosine, sine).astype(jnp.bfloat16)
        for block in range(blocks):
            seq_offset, head_offset = divmod(block, head_count)
            piece = slice(block * padded, (block + 1) * padded)
            part_ref = part_refs[seq_offset]
            part_ref[head_offset, :, lanes(0, p)] = key_parts[p][piece].astype(jnp.bfloat16)
            part_ref[head_offset, :, lanes(HEADS_PER_CHUNK, p)] = value_parts[p][piece].astype(
                jnp.bfloat16
            )


def combine(*refs):
    *sum_refs, keep_ref, send_ref = refs
    for place in range(keep_ref.shape[0]):
        for offset, ref in ((2 * place, keep_ref), (2 * place + 1, send_ref)):
            total = sum(sum_ref[offset].astype(jnp.float32) for sum_ref in sum_refs)
            ref[place] = total.astype(ref.dtype)


def finish(cos_ref, sin_ref, *refs):
    cosine, sine = cos_ref[...], sin_ref[...]
    *sum_refs, key_ref, value_ref = refs
    for chunk in range(CHUNKS):
        mine = sum_refs[2 * chunk : 2 * chunk + 2]
        for place in range(HEADS_PER_CHUNK):
            cols = head_cols(chunk * HEADS_PER_CHUNK + place)
            here, there = head_cols(place), head_cols(HEADS_PER_CHUNK + place)
            key_total = sum(ref[0, :, here].astype(jnp.float32) for ref in mine)
            value_total = sum(ref[0, :, there].astype(jnp.float32) for ref in mine)
            key_ref[:, cols] = rope_back(key_total, cosine, sine).astype(jnp.bfloat16)
            value_ref[:, cols] = value_total.astype(jnp.bfloat16)


def params(mebibytes):
    return pltpu.CompilerParams(vmem_limit_bytes=mebibytes << 20)


def cost(microseconds):
    return pl.CostEstimate(
        flops=microseconds * 1153 * 10**6,
        bytes_accessed=microseconds * 3690 * 10**3,
        transcendentals=0,
    )


def shards(queries, routed_keys, routed_values, output_gradient, positions, counts):
    seq_count = lax.axis_size("seq")
    head_count = lax.axis_size("head")
    blocks = seq_count * head_count
    rows = queries.shape[0]
    padded = -(-rows // 8) * 8
    if padded != rows:
        extra = ((0, padded - rows), (0, 0))
        queries, routed_keys, routed_values, output_gradient = (
            jnp.pad(x, extra) for x in (queries, routed_keys, routed_values, output_gradient)
        )
    query_rows = GROUP * padded
    shape = jax.ShapeDtypeStruct
    bf16, f32 = jnp.bfloat16, jnp.float32
    ranks = [(s, z) for s in range(seq_count) for z in range(head_count)]

    def rank_of(s, z):
        return s * head_count + z

    def along_head(x, offset, wanted):
        pairs = [
            (rank_of(s, z), rank_of(s, z ^ offset))
            for s, z in ranks
            if s < seq_count - 1 or wanted(z, z ^ offset)
        ]
        return lax.ppermute(x, ("seq", "head"), pairs)

    def gather_step(x, offset, held):
        return along_head(x, offset, lambda z, other: z ^ held < other)

    def halving_step(x, bit):
        def wanted(z, other):
            return max(z ^ m for m in range(bit)) >= min(
                other ^ m for m in range(0, head_count, 2 * bit)
            )

        return along_head(x, bit, wanted)

    def along_seq(x, offset, upward):
        pairs = [
            (rank_of(s, z), rank_of(s ^ offset, z))
            for s, z in ranks
            if (s < (s ^ offset)) == upward
        ]
        return lax.ppermute(x, ("seq", "head"), pairs)

    table = shape((padded, HEAD_WIDTH), f32)
    piece = shape((padded, 2 * CHUNK_COLS), bf16)
    whole, *own, cosine, sine = pl.pallas_call(
        functools.partial(prepare_keys, rows),
        out_shape=[shape((padded, CHUNKS * 2 * CHUNK_COLS), bf16)]
        + [piece] * CHUNKS
        + [table, table],
        in_specs=[SMEM, VMEM, VMEM],
        out_specs=[VMEM] * (CHUNKS + 3),
        compiler_params=params(56),
        name="prepare_keys",
    )(positions, routed_keys, routed_values)

    wide = GROUP * HEAD_WIDTH
    row_block = pl.BlockSpec((padded, wide), lambda g: (0, g))
    table_block = pl.BlockSpec((padded, HEAD_WIDTH), lambda g: (0, 0))
    tall_block = pl.BlockSpec((1, query_rows, HEAD_WIDTH), lambda g: (g, 0, 0))
    flat_block = pl.BlockSpec((1, HEAD_WIDTH, query_rows), lambda g: (g, 0, 0))
    tall = shape((KEY_VALUE_HEADS, query_rows, HEAD_WIDTH), bf16)
    flat = shape((KEY_VALUE_HEADS, HEAD_WIDTH, query_rows), bf16)
    *stacked, cosine_later = pl.pallas_call(
        prepare_queries,
        grid=(KEY_VALUE_HEADS,),
        out_shape=[tall, flat, tall, flat, table],
        in_specs=[row_block, row_block, table_block, table_block],
        out_specs=[tall_block, flat_block, tall_block, flat_block]
        + [table_block],
        cost_estimate=cost(7),
        compiler_params=params(16),
        name="prepare_queries",
    )(queries, output_gradient, cosine, sine)

    bits = [1 << b for b in reversed(range((head_count - 1).bit_length()))]
    later = range(1, seq_count)
    chunked = [{bits[0]: gather_step(own[0], bits[0], 0)}]
    far = {(a, 0): along_seq(whole, a, True) for a in later}
    nearest = gather_step(whole, 1, 0)
    chunked[0][bits[0]], own[1:], cosine_later, far = lax.optimization_barrier(
        (chunked[0][bits[0]], own[1:], cosine_later, far)
    )
    chunked += [{bits[0]: gather_step(x, bits[0], 0)} for x in own[1:]]
    far.update({(a, 1): along_seq(nearest, a, True) for a in later})
    top = {}
    for c, near in enumerate(chunked):
        near[bits[0]], top = lax.optimization_barrier((near[bits[0]], top))
        top.update({(a, c): along_seq(near[bits[0]], a, True) for a in later})
    gathered = []
    for c, near in enumerate(chunked):
        near[0] = own[c]
        for bit in bits[1:]:
            near.update(
                {j ^ bit: gather_step(x, bit, j) for j, x in near.items() if j ^ bit > 1}
            )
        blocks_here = [whole, nearest] + [near[j] for j in range(2, head_count)]
        for a in later:
            blocks_here += [far[a, 0], far[a, 1]]
            blocks_here += [
                top[a, c] if j == bits[0] else along_seq(near[j], a, True)
                for j in range(2, head_count)
            ]
        gathered.append(blocks_here)

    wide_outs = ()
    summed = []
    for chunk in range(CHUNKS):
        first = chunk * HEADS_PER_CHUNK // STEP_HEADS
        has_alias = int(chunk > 0)
        tall_part = pl.BlockSpec((STEP_HEADS, query_rows, HEAD_WIDTH), lambda g, f=first: (f + g, 0, 0))
        flat_part = pl.BlockSpec((STEP_HEADS, HEAD_WIDTH, query_rows), lambda g, f=first: (f + g, 0, 0))
        row_part = pl.BlockSpec((padded, STEP_HEADS * wide), lambda g, f=first: (0, f + g))
        kv_whole = pl.BlockSpec((padded, 2 * CHUNK_COLS), lambda g, c=chunk: (0, c))
        kv_chunk = pl.BlockSpec((padded, 2 * CHUNK_COLS), lambda g: (0, 0))
        part_block = pl.BlockSpec((head_count, padded, 2 * CHUNK_COLS), lambda g: (0, 0, 0))
        out = pl.pallas_call(
            functools.partial(attend, seq_count, head_count, rows, has_alias),
            grid=(HEADS_PER_CHUNK // STEP_HEADS,),
            out_shape=[shape((padded, QUERY_HEADS * HEAD_WIDTH), bf16)] * 2
            + [shape((head_count, padded, 2 * CHUNK_COLS), bf16)] * seq_count,
            in_specs=[SMEM]
            + ([kv_whole] * 2 + [kv_chunk] * (head_count - 2)) * seq_count
            + [tall_part, flat_part, tall_part, flat_part, table_block, table_block]
            + [pl.BlockSpec(memory_space=pl.ANY)] * (2 * has_alias),
            out_specs=[row_part, row_part] + [part_block] * seq_count,
            scratch_shapes=[
                pltpu.VMEM((blocks * padded, MASK_ROWS), f32),
                pltpu.VMEM((MASK_ROWS, query_rows), bf16),
                pltpu.VMEM((8, query_rows), f32),
            ],
            input_output_aliases={blocks + 7: 0, blocks + 8: 1} if has_alias else {},
            cost_estimate=cost(10),
            compiler_params=params(32),
            name="attend",
        )(counts, *gathered[chunk], *stacked, cosine_later, sine, *wide_outs)
        wide_outs = out[:2]
        parts = [out[2]] + [along_seq(out[2 + a], a, False) for a in range(1, seq_count)]
        if chunk:
            parts[-1], send = lax.optimization_barrier((parts[-1], send))
            summed.append(halving_step(send, head_count // 2))
        bit = 1
        while bit < head_count:
            left = (head_count // (2 * bit), padded, 2 * CHUNK_COLS)
            keep, send = pl.pallas_call(
                combine,
                out_shape=[shape(left, f32), shape(left, bf16)],
                in_specs=[VMEM] * len(parts),
                out_specs=[VMEM] * 2,
                cost_estimate=cost(2),
                compiler_params=params(8),
                name="combine",
            )(*parts)
            if 2 * bit < head_count:
                parts = [keep, halving_step(send, bit)]
            bit *= 2
        summed.append(keep)
    summed.append(halving_step(send, head_count // 2))

    narrow = shape((padded, KEY_VALUE_HEADS * HEAD_WIDTH), bf16)
    key_grad, value_grad = pl.pallas_call(
        finish,
        out_shape=[narrow, narrow],
        in_specs=[VMEM] * (2 + CHUNKS * 2),
        out_specs=[VMEM, VMEM],
        cost_estimate=cost(2),
        compiler_params=params(8),
        name="finish",
    )(cosine, sine, *summed)
    results = (*wide_outs, key_grad, value_grad)
    if padded != rows:
        results = tuple(x[:rows] for x in results)
    return results


def solution(mesh):
    rows = P(("dp", "seq", "head"), None)
    return jax.shard_map(
        shards,
        mesh=mesh,
        in_specs=(rows, rows, rows, rows, P("dp"), P("dp")),
        out_specs=(rows, rows, rows, rows),
        check_vma=False,
    )
```

```python
import functools

import jax
import jax.numpy as jnp
import numpy as np
from jax import lax
from jax.experimental import pallas as pl
from jax.experimental.pallas import tpu as pltpu
from jax.sharding import PartitionSpec as P

QUERY_HEADS = 64
KEY_VALUE_HEADS = 8
HEAD_WIDTH = 128
GROUP = QUERY_HEADS // KEY_VALUE_HEADS
ROPE_BASE = 500000.0
SCORE_SCALE = 1.0 / float(np.sqrt(HEAD_WIDTH))
LOG2_E = 1.4426950408889634
CHUNKS = 2
HEADS_PER_CHUNK = KEY_VALUE_HEADS // CHUNKS
CHUNK_COLS = HEADS_PER_CHUNK * HEAD_WIDTH
STEP_HEADS = 2
VMEM = pl.BlockSpec(memory_space=pltpu.VMEM)
SMEM = pl.BlockSpec(memory_space=pltpu.SMEM)


def inverse_freq_row():
    half = HEAD_WIDTH // 2
    place = lax.rem(lax.broadcasted_iota(jnp.int32, (8, HEAD_WIDTH), 1), half)
    row = jnp.ones((8, HEAD_WIDTH), jnp.float32)
    for i in range(1, half):
        row = jnp.where(place == i, np.float32(ROPE_BASE ** (-2.0 * i / HEAD_WIDTH)), row)
    return row[0:1]


def angle_tables(rows, padded, pos_ref):
    start = (lax.axis_index("seq") * lax.axis_size("head") + lax.axis_index("head")) * rows
    sublane = lax.broadcasted_iota(jnp.int32, (8, HEAD_WIDTH), 0)
    pieces = []
    for base in range(0, padded, 8):
        piece = jnp.zeros((8, HEAD_WIDTH), jnp.int32)
        for offset in range(min(8, rows - base)):
            piece = jnp.where(sublane == offset, pos_ref[start + (base + offset)], piece)
        pieces.append(piece)
    angle = jnp.concatenate(pieces, 0).astype(jnp.float32) * inverse_freq_row()
    lane = lax.broadcasted_iota(jnp.int32, angle.shape, 1)
    return jnp.cos(angle), jnp.sin(angle) * jnp.where(lane < HEAD_WIDTH // 2, -1.0, 1.0)


def rope(vectors, cosine, sine):
    return vectors * cosine + pltpu.roll(vectors, HEAD_WIDTH // 2, 1) * sine


def rope_back(vectors, cosine, sine):
    return vectors * cosine - pltpu.roll(vectors, HEAD_WIDTH // 2, 1) * sine


def head_cols(index):
    return slice(index * HEAD_WIDTH, (index + 1) * HEAD_WIDTH)


def prepare_keys(rows, pos_ref, key_ref, value_ref, whole_ref, *kv_refs):
    cosine, sine = angle_tables(rows, key_ref.shape[0], pos_ref)
    for head in range(KEY_VALUE_HEADS):
        chunk, place = divmod(head, HEADS_PER_CHUNK)
        rotated = rope(key_ref[:, head_cols(head)].astype(jnp.float32), cosine, sine)
        columns = {
            place: rotated.astype(jnp.bfloat16),
            HEADS_PER_CHUNK + place: value_ref[:, head_cols(head)],
        }
        for column, x in columns.items():
            kv_refs[chunk][:, head_cols(column)] = x
            whole_ref[:, head_cols(2 * chunk * HEADS_PER_CHUNK + column)] = x


def prepare_queries(rows, pos_ref, query_ref, grad_ref, *out_refs):
    q_ref, qt_ref, g_ref, gt_ref, cos_ref, sin_ref, cos_t_ref, sin_t_ref = out_refs

    @pl.when(pl.program_id(0) == 0)
    def _():
        cosine, sine = angle_tables(rows, query_ref.shape[0], pos_ref)
        cos_ref[...] = cosine
        sin_ref[...] = sine
        half = HEAD_WIDTH // 2
        cos_t_ref[...] = jnp.concatenate([cosine] * GROUP, 0).T[half:] * SCORE_SCALE
        sin_t_ref[...] = jnp.concatenate([sine] * GROUP, 0).T[half:] * SCORE_SCALE

    cosine, sine = cos_ref[...], sin_ref[...]
    queries = jnp.concatenate(
        [
            rope(query_ref[:, head_cols(h)].astype(jnp.float32), cosine, sine)
            for h in range(GROUP)
        ],
        0,
    )
    grads = jnp.concatenate(
        [grad_ref[:, head_cols(h)].astype(jnp.float32) for h in range(GROUP)], 0
    )
    q_ref[0] = queries.astype(jnp.bfloat16)
    qt_ref[0] = queries.T.astype(jnp.bfloat16)
    g_ref[0] = grads.astype(jnp.bfloat16)
    gt_ref[0] = grads.T.astype(jnp.bfloat16)


def dot(left, right):
    return jnp.dot(left, right, preferred_element_type=jnp.float32)


def attend(seq_count, head_count, rows, has_alias, counts_ref, *refs):
    blocks = seq_count * head_count
    kv_refs = refs[:blocks]
    q_ref, qt_ref, g_ref, gt_ref, cos_ref, sin_ref = refs[blocks : blocks + 6]
    outs = refs[blocks + 6 + 2 * has_alias :]
    out_ref, grad_ref = outs[:2]
    part_refs = outs[2 : 2 + seq_count]
    bias_ref, live_ref = outs[2 + seq_count :]
    padded = kv_refs[0].shape[0]
    query_rows = GROUP * padded
    step = pl.program_id(0)
    seq_index, head_index = lax.axis_index("seq"), lax.axis_index("head")
    my_rank = seq_index * head_count + head_index

    @pl.when(step == 0)
    def _():
        key_row = lax.broadcasted_iota(jnp.int32, (padded, query_rows), 0)
        query_row = lax.rem(lax.broadcasted_iota(jnp.int32, (padded, query_rows), 1), padded)
        for block in range(blocks):
            seq_offset, head_offset = divmod(block, head_count)
            seq_from = jnp.bitwise_xor(seq_index, seq_offset)
            head_from = jnp.bitwise_xor(head_index, head_offset)
            rank = seq_from * head_count + head_from
            limit = jnp.minimum(counts_ref[seq_from] - head_from * rows, rows)
            limit = jnp.where(rank <= my_rank, limit, 0)
            allowed = key_row < limit
            if block == 0:
                allowed = allowed & (key_row <= query_row)
                live_ref[...] = (query_row[:8] < limit).astype(jnp.float32)
            bias_ref[block * padded : (block + 1) * padded, :] = jnp.where(allowed, 0.0, -1e30)

    def lanes(first, place):
        start = pl.multiple_of((first + step * STEP_HEADS + place) * HEAD_WIDTH, HEAD_WIDTH)
        return pl.ds(start, HEAD_WIDTH)

    def gathered(first, place):
        cols = lanes(first, place)
        wide = jnp.concatenate([ref[:, cols].astype(jnp.float32) for ref in kv_refs], 0)
        low = wide.astype(jnp.bfloat16)
        return low, low.T

    heads = range(STEP_HEADS)
    keys, values = [gathered(0, p) for p in heads], [gathered(HEADS_PER_CHUNK, p) for p in heads]
    bias, live = bias_ref[...], live_ref[0:1, :]
    scores = [dot(keys[p][0], qt_ref[p]) * (SCORE_SCALE * LOG2_E) + bias for p in heads]
    dprobs, probs, probs_low = [], [], []
    for p in heads:
        weights = jnp.exp2(scores[p] - jnp.max(scores[p], 0, keepdims=True))
        probs.append(weights * (live / jnp.sum(weights, 0, keepdims=True)))
        probs_low.append(probs[p].astype(jnp.bfloat16))
        dprobs.append(dot(values[p][0], gt_ref[p]))
    outs_t, value_parts, dscores = [], [], []
    for p in heads:
        outs_t.append(dot(values[p][1], probs_low[p]))
        value_parts.append(dot(probs_low[p], g_ref[p]))
        out_low = outs_t[p].astype(jnp.bfloat16).astype(jnp.float32)
        delta = jnp.sum(gt_ref[p].astype(jnp.float32) * out_low, 0, keepdims=True)
        dscores.append((probs[p] * (dprobs[p] - delta)).astype(jnp.bfloat16))
    grads_t = [dot(keys[p][1], dscores[p]) for p in heads]
    key_parts = [dot(dscores[p], q_ref[p]) * SCORE_SCALE for p in heads]

    cosine, sine = cos_ref[...], sin_ref[...]
    half = HEAD_WIDTH // 2
    for p in heads:
        first, second = grads_t[p][:half], grads_t[p][half:]
        turned = [first * cosine + second * sine, second * cosine - first * sine]
        grad_low = jnp.concatenate(turned, 0).astype(jnp.bfloat16)
        out_heads = outs_t[p].astype(jnp.bfloat16).T.astype(jnp.float32)
        grad_heads = grad_low.T.astype(jnp.float32)
        for h in range(GROUP):
            piece, cols = slice(h * padded, (h + 1) * padded), head_cols(p * GROUP + h)
            out_ref[:, cols] = out_heads[piece].astype(jnp.bfloat16)
            grad_ref[:, cols] = grad_heads[piece].astype(jnp.bfloat16)
        for block in range(blocks):
            seq_offset, head_offset = divmod(block, head_count)
            piece = slice(block * padded, (block + 1) * padded)
            part_ref = part_refs[seq_offset]
            part_ref[head_offset, :, lanes(0, p)] = key_parts[p][piece].astype(jnp.bfloat16)
            part_ref[head_offset, :, lanes(HEADS_PER_CHUNK, p)] = value_parts[p][piece].astype(
                jnp.bfloat16
            )


def combine(seq_count, head_count, *refs):
    part_refs, base_ref, send_refs = refs[:seq_count], refs[seq_count], refs[seq_count + 1 :]
    for offset in range(head_count):
        total = part_refs[0][offset].astype(jnp.float32)
        for ref in part_refs[1:]:
            total = total + ref[offset].astype(jnp.float32)
        if offset == 0:
            base_ref[...] = total
        else:
            send_refs[offset - 1][...] = total.astype(jnp.bfloat16)


def finish(head_count, *refs):
    cosine, sine = refs[0][...], refs[1][...]
    key_ref, value_ref = refs[-2:]
    for chunk in range(CHUNKS):
        mine = refs[2 + chunk * head_count : 2 + (chunk + 1) * head_count]
        for place in range(HEADS_PER_CHUNK):
            here, there = head_cols(place), head_cols(HEADS_PER_CHUNK + place)
            key_total, value_total = mine[0][:, here], mine[0][:, there]
            for ref in mine[1:]:
                key_total = key_total + ref[:, here].astype(jnp.float32)
                value_total = value_total + ref[:, there].astype(jnp.float32)
            cols = head_cols(chunk * HEADS_PER_CHUNK + place)
            key_ref[:, cols] = rope_back(key_total, cosine, sine).astype(jnp.bfloat16)
            value_ref[:, cols] = value_total.astype(jnp.bfloat16)


def params(mebibytes):
    return pltpu.CompilerParams(vmem_limit_bytes=mebibytes << 20)


def cost(microseconds):
    return pl.CostEstimate(
        flops=microseconds * 1153 * 10**6,
        bytes_accessed=microseconds * 3690 * 10**3,
        transcendentals=0,
    )


def shards(queries, routed_keys, routed_values, output_gradient, positions, counts):
    seq_count = lax.axis_size("seq")
    head_count = lax.axis_size("head")
    blocks = seq_count * head_count
    rows = queries.shape[0]
    padded = -(-rows // 8) * 8
    if padded != rows:
        extra = ((0, padded - rows), (0, 0))
        queries, routed_keys, routed_values, output_gradient = (
            jnp.pad(x, extra) for x in (queries, routed_keys, routed_values, output_gradient)
        )
    query_rows = GROUP * padded
    shape = jax.ShapeDtypeStruct
    bf16, f32 = jnp.bfloat16, jnp.float32
    ranks = [(s, z) for s in range(seq_count) for z in range(head_count)]

    def rank_of(s, z):
        return s * head_count + z

    def along_head(x, offset, upward, held=0):
        pairs = []
        for s, z in ranks:
            other = z ^ offset
            if s < seq_count - 1 or ((z ^ held) < other) == upward:
                pairs.append((rank_of(s, z), rank_of(s, other)))
        return lax.ppermute(x, ("seq", "head"), pairs)

    def along_seq(x, offset, upward):
        pairs = [
            (rank_of(s, z), rank_of(s ^ offset, z))
            for s, z in ranks
            if (s < (s ^ offset)) == upward
        ]
        return lax.ppermute(x, ("seq", "head"), pairs)

    table = shape((padded, HEAD_WIDTH), f32)
    table_t = shape((HEAD_WIDTH // 2, query_rows), f32)
    piece = shape((padded, 2 * CHUNK_COLS), bf16)
    whole, *own = pl.pallas_call(
        functools.partial(prepare_keys, rows),
        out_shape=[shape((padded, CHUNKS * 2 * CHUNK_COLS), bf16)] + [piece] * CHUNKS,
        in_specs=[SMEM, VMEM, VMEM],
        out_specs=[VMEM] * (CHUNKS + 1),
        compiler_params=params(56),
        name="prepare_keys",
    )(positions, routed_keys, routed_values)

    wide = GROUP * HEAD_WIDTH
    row_block = pl.BlockSpec((padded, wide), lambda g: (0, g))
    table_block = pl.BlockSpec((padded, HEAD_WIDTH), lambda g: (0, 0))
    tall_block = pl.BlockSpec((1, query_rows, HEAD_WIDTH), lambda g: (g, 0, 0))
    flat_block = pl.BlockSpec((1, HEAD_WIDTH, query_rows), lambda g: (g, 0, 0))
    tall = shape((KEY_VALUE_HEADS, query_rows, HEAD_WIDTH), bf16)
    flat = shape((KEY_VALUE_HEADS, HEAD_WIDTH, query_rows), bf16)
    table_t_block = pl.BlockSpec(table_t.shape, lambda g: (0, 0))
    *stacked, cosine, sine, cosine_t, sine_t = pl.pallas_call(
        functools.partial(prepare_queries, rows),
        grid=(KEY_VALUE_HEADS,),
        out_shape=[tall, flat, tall, flat, table, table, table_t, table_t],
        in_specs=[SMEM, row_block, row_block],
        out_specs=[tall_block, flat_block, tall_block, flat_block]
        + [table_block, table_block, table_t_block, table_t_block],
        cost_estimate=cost(7),
        compiler_params=params(16),
        name="prepare_queries",
    )(positions, queries, output_gradient)

    bits = [1 << b for b in reversed(range((head_count - 1).bit_length()))]
    later = range(1, seq_count)
    firsts = sorted({bits[0], 1})
    far = {a: along_seq(whole, a, True) for a in later}
    near = {0: own[0], **{j: along_head(own[0], j, True) for j in firsts}}
    near, cosine_t, far = lax.optimization_barrier((near, cosine_t, far))

    def gather(near):
        for bit in bits[1:]:
            near.update(
                {j ^ bit: along_head(x, bit, True, j) for j, x in near.items() if j ^ bit not in near}
            )
        crossed = {
            (a, j): along_seq(near[j], a, True) for j in range(1, head_count) for a in later
        }
        blocks_here = [near[j] for j in range(head_count)]
        for a in later:
            blocks_here += [far[a]] + [crossed[a, j] for j in range(1, head_count)]
        return blocks_here

    wide_outs = ()
    parts = []
    for chunk in range(CHUNKS):
        first = chunk * HEADS_PER_CHUNK // STEP_HEADS
        has_alias = int(chunk > 0)
        tall_part, flat_part = (
            pl.BlockSpec((STEP_HEADS, *x.shape[1:]), lambda g, f=first: (f + g, 0, 0))
            for x in (tall, flat)
        )
        row_part = pl.BlockSpec((padded, STEP_HEADS * wide), lambda g, f=first: (0, f + g))
        if chunk:
            near = {0: own[chunk], **{j: along_head(own[chunk], j, True) for j in firsts}}
            near, parts[-1][0] = lax.optimization_barrier((near, parts[-1][0]))
        gathered = gather(near)
        if chunk + 1 < CHUNKS:
            last = head_count - 1
            own[chunk + 1], gathered[last] = lax.optimization_barrier(
                (own[chunk + 1], gathered[last])
            )
        kv_whole = pl.BlockSpec((padded, 2 * CHUNK_COLS), lambda g, c=chunk: (0, c))
        kv_chunk = pl.BlockSpec((padded, 2 * CHUNK_COLS), lambda g: (0, 0))
        part_block = pl.BlockSpec((head_count, padded, 2 * CHUNK_COLS), lambda g: (0, 0, 0))
        out = pl.pallas_call(
            functools.partial(attend, seq_count, head_count, rows, has_alias),
            grid=(HEADS_PER_CHUNK // STEP_HEADS,),
            out_shape=[shape((padded, QUERY_HEADS * HEAD_WIDTH), bf16)] * 2
            + [shape((head_count, padded, 2 * CHUNK_COLS), bf16)] * seq_count,
            in_specs=[SMEM]
            + [kv_chunk] * head_count
            + ([kv_whole] + [kv_chunk] * (head_count - 1)) * (seq_count - 1)
            + [tall_part, flat_part, tall_part, flat_part, table_t_block, table_t_block]
            + [pl.BlockSpec(memory_space=pl.ANY)] * (2 * has_alias),
            out_specs=[row_part, row_part] + [part_block] * seq_count,
            scratch_shapes=[
                pltpu.VMEM((blocks * padded, query_rows), f32),
                pltpu.VMEM((8, query_rows), f32),
            ],
            input_output_aliases={blocks + 7: 0, blocks + 8: 1} if has_alias else {},
            cost_estimate=cost(10),
            compiler_params=params(32),
            name="attend",
        )(counts, *gathered, *stacked, cosine_t, sine_t, *wide_outs)
        wide_outs = out[:2]
        parts.append([out[2]] + [along_seq(out[2 + a], a, False) for a in later])

    summed = []
    for mine in parts:
        if summed:
            mine[-1], summed[-head_count] = lax.optimization_barrier(
                (mine[-1], summed[-head_count])
            )
        base, *sends = pl.pallas_call(
            functools.partial(combine, seq_count, head_count),
            out_shape=[shape((padded, 2 * CHUNK_COLS), f32)] + [piece] * (head_count - 1),
            in_specs=[VMEM] * seq_count,
            out_specs=[VMEM] * head_count,
            cost_estimate=cost(2),
            compiler_params=params(8),
            name="combine",
        )(*mine)
        summed += [base] + [along_head(x, j + 1, False) for j, x in enumerate(sends)]

    narrow = shape((padded, KEY_VALUE_HEADS * HEAD_WIDTH), bf16)
    key_grad, value_grad = pl.pallas_call(
        functools.partial(finish, head_count),
        out_shape=[narrow, narrow],
        in_specs=[VMEM] * (2 + CHUNKS * head_count),
        out_specs=[VMEM, VMEM],
        cost_estimate=cost(2),
        compiler_params=params(8),
        name="finish",
    )(cosine, sine, *summed)
    results = (*wide_outs, key_grad, value_grad)
    if padded != rows:
        results = tuple(x[:rows] for x in results)
    return results


def solution(mesh):
    rows = P(("dp", "seq", "head"), None)
    return jax.shard_map(
        shards,
        mesh=mesh,
        in_specs=(rows, rows, rows, rows, P("dp"), P("dp")),
        out_specs=(rows, rows, rows, rows),
        check_vma=False,
    )
```

```python
import functools

import jax
import jax.numpy as jnp
import numpy as np
from jax import lax
from jax.experimental import pallas as pl
from jax.experimental.pallas import tpu as pltpu
from jax.sharding import PartitionSpec as P

QUERY_HEADS = 64
KEY_VALUE_HEADS = 8
HEAD_WIDTH = 128
GROUP = QUERY_HEADS // KEY_VALUE_HEADS
ROPE_BASE = 500000.0
SCORE_SCALE = 1.0 / float(np.sqrt(HEAD_WIDTH))
LOG2_E = 1.4426950408889634
CHUNKS = 2
HEADS_PER_CHUNK = KEY_VALUE_HEADS // CHUNKS
CHUNK_COLS = HEADS_PER_CHUNK * HEAD_WIDTH
STEP_HEADS = 2
VMEM = pl.BlockSpec(memory_space=pltpu.VMEM)
SMEM = pl.BlockSpec(memory_space=pltpu.SMEM)


def inverse_freq_row():
    half = HEAD_WIDTH // 2
    place = lax.rem(lax.broadcasted_iota(jnp.int32, (8, HEAD_WIDTH), 1), half)
    row = jnp.ones((8, HEAD_WIDTH), jnp.float32)
    for i in range(1, half):
        row = jnp.where(place == i, np.float32(ROPE_BASE ** (-2.0 * i / HEAD_WIDTH)), row)
    return row[0:1]


def angle_tables(rows, padded, pos_ref):
    start = (lax.axis_index("seq") * lax.axis_size("head") + lax.axis_index("head")) * rows
    sublane = lax.broadcasted_iota(jnp.int32, (8, HEAD_WIDTH), 0)
    pieces = []
    for base in range(0, padded, 8):
        piece = jnp.zeros((8, HEAD_WIDTH), jnp.int32)
        for offset in range(min(8, rows - base)):
            piece = jnp.where(sublane == offset, pos_ref[start + (base + offset)], piece)
        pieces.append(piece)
    angle = jnp.concatenate(pieces, 0).astype(jnp.float32) * inverse_freq_row()
    lane = lax.broadcasted_iota(jnp.int32, angle.shape, 1)
    return jnp.cos(angle), jnp.sin(angle) * jnp.where(lane < HEAD_WIDTH // 2, -1.0, 1.0)


def rope(vectors, cosine, sine):
    return vectors * cosine + pltpu.roll(vectors, HEAD_WIDTH // 2, 1) * sine


def rope_back(vectors, cosine, sine):
    return vectors * cosine - pltpu.roll(vectors, HEAD_WIDTH // 2, 1) * sine


def head_cols(index):
    return slice(index * HEAD_WIDTH, (index + 1) * HEAD_WIDTH)


def prepare_keys(rows, pos_ref, key_ref, value_ref, whole_ref, *kv_refs):
    cosine, sine = angle_tables(rows, key_ref.shape[0], pos_ref)
    for head in range(KEY_VALUE_HEADS):
        chunk, place = divmod(head, HEADS_PER_CHUNK)
        rotated = rope(key_ref[:, head_cols(head)].astype(jnp.float32), cosine, sine)
        columns = {
            place: rotated.astype(jnp.bfloat16),
            HEADS_PER_CHUNK + place: value_ref[:, head_cols(head)],
        }
        for column, x in columns.items():
            kv_refs[chunk][:, head_cols(column)] = x
            whole_ref[:, head_cols(2 * chunk * HEADS_PER_CHUNK + column)] = x


def prepare_queries(rows, pos_ref, query_ref, grad_ref, *out_refs):
    q_ref, qt_ref, g_ref, gt_ref, cos_ref, sin_ref = out_refs

    @pl.when(pl.program_id(0) == 0)
    def _():
        cosine, sine = angle_tables(rows, query_ref.shape[0], pos_ref)
        cos_ref[...] = cosine
        sin_ref[...] = sine

    cosine, sine = cos_ref[...], sin_ref[...]
    queries = jnp.concatenate(
        [
            rope(query_ref[:, head_cols(h)].astype(jnp.float32), cosine, sine)
            for h in range(GROUP)
        ],
        0,
    )
    grads = jnp.concatenate(
        [grad_ref[:, head_cols(h)].astype(jnp.float32) for h in range(GROUP)], 0
    )
    q_ref[0] = queries.astype(jnp.bfloat16)
    qt_ref[0] = queries.T.astype(jnp.bfloat16)
    g_ref[0] = grads.astype(jnp.bfloat16)
    gt_ref[0] = grads.T.astype(jnp.bfloat16)


def dot(left, right):
    return jnp.dot(left, right, preferred_element_type=jnp.float32)


def attend(seq_count, head_count, rows, has_alias, counts_ref, *refs):
    blocks = seq_count * head_count
    kv_refs = refs[:blocks]
    q_ref, qt_ref, g_ref, gt_ref, cos_ref, sin_ref = refs[blocks : blocks + 6]
    outs = refs[blocks + 6 + 2 * has_alias :]
    out_ref, grad_ref = outs[:2]
    part_refs = outs[2 : 2 + seq_count]
    bias_ref, live_ref = outs[2 + seq_count :]
    padded = kv_refs[0].shape[0]
    query_rows = GROUP * padded
    step = pl.program_id(0)
    seq_index, head_index = lax.axis_index("seq"), lax.axis_index("head")
    my_rank = seq_index * head_count + head_index

    @pl.when(step == 0)
    def _():
        key_row = lax.broadcasted_iota(jnp.int32, (padded, query_rows), 0)
        query_row = lax.rem(lax.broadcasted_iota(jnp.int32, (padded, query_rows), 1), padded)
        for block in range(blocks):
            seq_offset, head_offset = divmod(block, head_count)
            seq_from = jnp.bitwise_xor(seq_index, seq_offset)
            head_from = jnp.bitwise_xor(head_index, head_offset)
            rank = seq_from * head_count + head_from
            limit = jnp.minimum(counts_ref[seq_from] - head_from * rows, rows)
            limit = jnp.where(rank <= my_rank, limit, 0)
            allowed = key_row < limit
            if block == 0:
                allowed = allowed & (key_row <= query_row)
                live_ref[...] = (query_row[:8] < limit).astype(jnp.float32)
            bias_ref[block * padded : (block + 1) * padded, :] = jnp.where(allowed, 0.0, -1e30)

    def lanes(first, place):
        start = pl.multiple_of((first + step * STEP_HEADS + place) * HEAD_WIDTH, HEAD_WIDTH)
        return pl.ds(start, HEAD_WIDTH)

    def gathered(first, place):
        cols = lanes(first, place)
        wide = jnp.concatenate([ref[:, cols].astype(jnp.float32) for ref in kv_refs], 0)
        return wide.astype(jnp.bfloat16)

    heads = range(STEP_HEADS)
    keys, values = [gathered(0, p) for p in heads], [gathered(HEADS_PER_CHUNK, p) for p in heads]
    bias, live = bias_ref[...], live_ref[0:1, :]
    scores = [dot(keys[p], qt_ref[p]) * (SCORE_SCALE * LOG2_E) + bias for p in heads]
    probs, probs_low, dscores = [], [], []
    for p in heads:
        weights = jnp.exp2(scores[p] - jnp.max(scores[p], 0, keepdims=True))
        probs.append(weights * (live / jnp.sum(weights, 0, keepdims=True)))
        probs_low.append(probs[p].astype(jnp.bfloat16))
    for p in heads:
        weighted = probs[p] * dot(values[p], gt_ref[p])
        delta = jnp.sum(weighted, 0, keepdims=True)
        dscores.append((weighted - probs[p] * delta).astype(jnp.bfloat16))
    outs = [dot(probs_low[p].T, values[p]) for p in heads]
    value_parts = [dot(probs_low[p], g_ref[p]) for p in heads]
    grads = [dot(dscores[p].T, keys[p]) * SCORE_SCALE for p in heads]
    key_parts = [dot(dscores[p], q_ref[p]) * SCORE_SCALE for p in heads]

    cosine, sine = cos_ref[...], sin_ref[...]
    for p in heads:
        for h in range(GROUP):
            piece, cols = slice(h * padded, (h + 1) * padded), head_cols(p * GROUP + h)
            out_ref[:, cols] = outs[p][piece].astype(jnp.bfloat16)
            grad_ref[:, cols] = rope_back(grads[p][piece], cosine, sine).astype(jnp.bfloat16)
        for block in range(blocks):
            seq_offset, head_offset = divmod(block, head_count)
            piece = slice(block * padded, (block + 1) * padded)
            part_ref = part_refs[seq_offset]
            part_ref[head_offset, :, lanes(0, p)] = key_parts[p][piece].astype(jnp.bfloat16)
            part_ref[head_offset, :, lanes(HEADS_PER_CHUNK, p)] = value_parts[p][piece].astype(
                jnp.bfloat16
            )


def combine(seq_count, head_count, *refs):
    part_refs, base_ref, send_refs = refs[:seq_count], refs[seq_count], refs[seq_count + 1 :]
    for offset in range(head_count):
        total = part_refs[0][offset].astype(jnp.float32)
        for ref in part_refs[1:]:
            total = total + ref[offset].astype(jnp.float32)
        if offset == 0:
            base_ref[...] = total
        else:
            send_refs[offset - 1][...] = total.astype(jnp.bfloat16)


def finish(head_count, *refs):
    cosine, sine = refs[0][...], refs[1][...]
    key_ref, value_ref = refs[-2:]
    for chunk in range(CHUNKS):
        mine = refs[2 + chunk * head_count : 2 + (chunk + 1) * head_count]
        for place in range(HEADS_PER_CHUNK):
            here, there = head_cols(place), head_cols(HEADS_PER_CHUNK + place)
            key_total, value_total = mine[0][:, here], mine[0][:, there]
            for ref in mine[1:]:
                key_total = key_total + ref[:, here].astype(jnp.float32)
                value_total = value_total + ref[:, there].astype(jnp.float32)
            cols = head_cols(chunk * HEADS_PER_CHUNK + place)
            key_ref[:, cols] = rope_back(key_total, cosine, sine).astype(jnp.bfloat16)
            value_ref[:, cols] = value_total.astype(jnp.bfloat16)


def params(mebibytes):
    return pltpu.CompilerParams(vmem_limit_bytes=mebibytes << 20)


def cost(microseconds):
    return pl.CostEstimate(
        flops=microseconds * 1153 * 10**6,
        bytes_accessed=microseconds * 3690 * 10**3,
        transcendentals=0,
    )


def shards(queries, routed_keys, routed_values, output_gradient, positions, counts):
    seq_count = lax.axis_size("seq")
    head_count = lax.axis_size("head")
    blocks = seq_count * head_count
    rows = queries.shape[0]
    padded = -(-rows // 8) * 8
    if padded != rows:
        extra = ((0, padded - rows), (0, 0))
        queries, routed_keys, routed_values, output_gradient = (
            jnp.pad(x, extra) for x in (queries, routed_keys, routed_values, output_gradient)
        )
    query_rows = GROUP * padded
    shape = jax.ShapeDtypeStruct
    bf16, f32 = jnp.bfloat16, jnp.float32
    ranks = [(s, z) for s in range(seq_count) for z in range(head_count)]

    def rank_of(s, z):
        return s * head_count + z

    def along_head(x, offset, upward, held=0):
        pairs = []
        for s, z in ranks:
            other = z ^ offset
            if s < seq_count - 1 or ((z ^ held) < other) == upward:
                pairs.append((rank_of(s, z), rank_of(s, other)))
        return lax.ppermute(x, ("seq", "head"), pairs)

    def along_seq(x, offset, upward):
        pairs = [
            (rank_of(s, z), rank_of(s ^ offset, z))
            for s, z in ranks
            if (s < (s ^ offset)) == upward
        ]
        return lax.ppermute(x, ("seq", "head"), pairs)

    table = shape((padded, HEAD_WIDTH), f32)
    piece = shape((padded, 2 * CHUNK_COLS), bf16)
    whole, *own = pl.pallas_call(
        functools.partial(prepare_keys, rows),
        out_shape=[shape((padded, CHUNKS * 2 * CHUNK_COLS), bf16)] + [piece] * CHUNKS,
        in_specs=[SMEM, VMEM, VMEM],
        out_specs=[VMEM] * (CHUNKS + 1),
        compiler_params=params(56),
        name="prepare_keys",
    )(positions, routed_keys, routed_values)

    wide = GROUP * HEAD_WIDTH
    row_block = pl.BlockSpec((padded, wide), lambda g: (0, g))
    table_block = pl.BlockSpec((padded, HEAD_WIDTH), lambda g: (0, 0))
    tall_block = pl.BlockSpec((1, query_rows, HEAD_WIDTH), lambda g: (g, 0, 0))
    flat_block = pl.BlockSpec((1, HEAD_WIDTH, query_rows), lambda g: (g, 0, 0))
    tall = shape((KEY_VALUE_HEADS, query_rows, HEAD_WIDTH), bf16)
    flat = shape((KEY_VALUE_HEADS, HEAD_WIDTH, query_rows), bf16)
    *stacked, cosine, sine = pl.pallas_call(
        functools.partial(prepare_queries, rows),
        grid=(KEY_VALUE_HEADS,),
        out_shape=[tall, flat, tall, flat, table, table],
        in_specs=[SMEM, row_block, row_block],
        out_specs=[tall_block, flat_block, tall_block, flat_block]
        + [table_block, table_block],
        cost_estimate=cost(7),
        compiler_params=params(16),
        name="prepare_queries",
    )(positions, queries, output_gradient)

    bits = [1 << b for b in reversed(range((head_count - 1).bit_length()))]
    later = range(1, seq_count)
    firsts = sorted({bits[0], 1})
    far = {a: along_seq(whole, a, True) for a in later}
    near = {0: own[0], **{j: along_head(own[0], j, True) for j in firsts}}
    near, own[1:], cosine, far = lax.optimization_barrier((near, own[1:], cosine, far))

    def exchange(near):
        for bit in bits[1:]:
            near.update(
                {j ^ bit: along_head(x, bit, True, j) for j, x in near.items() if j ^ bit not in near}
            )

    def cross(near, offsets):
        return {(a, j): along_seq(near[j], a, True) for j in offsets for a in later}

    gathered = []
    for chunk in range(CHUNKS):
        if chunk:
            near = {0: own[chunk], **{j: along_head(own[chunk], j, True) for j in firsts}}
            near, crossed = lax.optimization_barrier((near, crossed))
            gathered[-1].update(crossed)
        crossed = cross(near, firsts)
        exchange(near)
        gathered.append(
            near | crossed | cross(near, [j for j in near if j not in (0, *firsts)])
        )
    far_own = [(a, 0) for a in later]
    order = list(range(head_count)) + [(a, j) for a in later for j in range(head_count)]

    wide_outs = ()
    parts = []
    for chunk in range(CHUNKS):
        first = chunk * HEADS_PER_CHUNK // STEP_HEADS
        has_alias = int(chunk > 0)
        tall_part, flat_part = (
            pl.BlockSpec((STEP_HEADS, *x.shape[1:]), lambda g, f=first: (f + g, 0, 0))
            for x in (tall, flat)
        )
        row_part = pl.BlockSpec((padded, STEP_HEADS * wide), lambda g, f=first: (0, f + g))
        kv_whole = pl.BlockSpec((padded, 2 * CHUNK_COLS), lambda g, c=chunk: (0, c))
        kv_chunk = pl.BlockSpec((padded, 2 * CHUNK_COLS), lambda g: (0, 0))
        part_block = pl.BlockSpec((head_count, padded, 2 * CHUNK_COLS), lambda g: (0, 0, 0))
        out = pl.pallas_call(
            functools.partial(attend, seq_count, head_count, rows, has_alias),
            grid=(HEADS_PER_CHUNK // STEP_HEADS,),
            out_shape=[shape((padded, QUERY_HEADS * HEAD_WIDTH), bf16)] * 2
            + [shape((head_count, padded, 2 * CHUNK_COLS), bf16)] * seq_count,
            in_specs=[SMEM]
            + [kv_chunk] * head_count
            + ([kv_whole] + [kv_chunk] * (head_count - 1)) * (seq_count - 1)
            + [tall_part, flat_part, tall_part, flat_part, table_block, table_block]
            + [pl.BlockSpec(memory_space=pl.ANY)] * (2 * has_alias),
            out_specs=[row_part, row_part] + [part_block] * seq_count,
            scratch_shapes=[
                pltpu.VMEM((blocks * padded, query_rows), f32),
                pltpu.VMEM((8, query_rows), f32),
            ],
            input_output_aliases={blocks + 7: 0, blocks + 8: 1} if has_alias else {},
            cost_estimate=cost(10),
            compiler_params=params(32),
            name="attend",
        )(
            counts,
            *(far[k[0]] if k in far_own else gathered[chunk][k] for k in order),
            *stacked,
            cosine,
            sine,
            *wide_outs,
        )
        wide_outs = out[:2]
        parts.append([out[2]] + [along_seq(out[2 + a], a, False) for a in later])

    summed = []
    for mine in parts:
        if summed:
            mine[-1], summed[-head_count] = lax.optimization_barrier(
                (mine[-1], summed[-head_count])
            )
        base, *sends = pl.pallas_call(
            functools.partial(combine, seq_count, head_count),
            out_shape=[shape((padded, 2 * CHUNK_COLS), f32)] + [piece] * (head_count - 1),
            in_specs=[VMEM] * seq_count,
            out_specs=[VMEM] * head_count,
            cost_estimate=cost(2),
            compiler_params=params(8),
            name="combine",
        )(*mine)
        summed += [base] + [along_head(x, j + 1, False) for j, x in enumerate(sends)]

    narrow = shape((padded, KEY_VALUE_HEADS * HEAD_WIDTH), bf16)
    key_grad, value_grad = pl.pallas_call(
        functools.partial(finish, head_count),
        out_shape=[narrow, narrow],
        in_specs=[VMEM] * (2 + CHUNKS * head_count),
        out_specs=[VMEM, VMEM],
        cost_estimate=cost(2),
        compiler_params=params(8),
        name="finish",
    )(cosine, sine, *summed)
    results = (*wide_outs, key_grad, value_grad)
    if padded != rows:
        results = tuple(x[:rows] for x in results)
    return results


def solution(mesh):
    rows = P(("dp", "seq", "head"), None)
    return jax.shard_map(
        shards,
        mesh=mesh,
        in_specs=(rows, rows, rows, rows, P("dp"), P("dp")),
        out_specs=(rows, rows, rows, rows),
        check_vma=False,
    )
```

```python
import functools

import jax
import jax.numpy as jnp
import numpy as np
from jax import lax
from jax.experimental import pallas as pl
from jax.experimental.pallas import tpu as pltpu
from jax.sharding import PartitionSpec as P

QUERY_HEADS = 64
KEY_VALUE_HEADS = 8
HEAD_WIDTH = 128
GROUP = QUERY_HEADS // KEY_VALUE_HEADS
ROPE_BASE = 500000.0
SCORE_SCALE = 1.0 / float(np.sqrt(HEAD_WIDTH))
CHUNKS = 2
HEADS_PER_CHUNK = KEY_VALUE_HEADS // CHUNKS
CHUNK_COLS = HEADS_PER_CHUNK * HEAD_WIDTH
STEP_HEADS = 2
VMEM = pl.BlockSpec(memory_space=pltpu.VMEM)
SMEM = pl.BlockSpec(memory_space=pltpu.SMEM)


def inverse_freq_row():
    half = HEAD_WIDTH // 2
    place = lax.rem(lax.broadcasted_iota(jnp.int32, (8, HEAD_WIDTH), 1), half)
    row = jnp.ones((8, HEAD_WIDTH), jnp.float32)
    for i in range(1, half):
        row = jnp.where(place == i, np.float32(ROPE_BASE ** (-2.0 * i / HEAD_WIDTH)), row)
    return row[0:1]


def angle_tables(rows, padded, pos_ref):
    start = (lax.axis_index("seq") * lax.axis_size("head") + lax.axis_index("head")) * rows
    sublane = lax.broadcasted_iota(jnp.int32, (8, HEAD_WIDTH), 0)
    pieces = []
    for base in range(0, padded, 8):
        piece = jnp.zeros((8, HEAD_WIDTH), jnp.int32)
        for offset in range(min(8, rows - base)):
            piece = jnp.where(sublane == offset, pos_ref[start + (base + offset)], piece)
        pieces.append(piece)
    angle = jnp.concatenate(pieces, 0).astype(jnp.float32) * inverse_freq_row()
    lane = lax.broadcasted_iota(jnp.int32, angle.shape, 1)
    return jnp.cos(angle), jnp.sin(angle) * jnp.where(lane < HEAD_WIDTH // 2, -1.0, 1.0)


def rope(vectors, cosine, sine):
    return vectors * cosine + pltpu.roll(vectors, HEAD_WIDTH // 2, 1) * sine


def rope_back(vectors, cosine, sine):
    return vectors * cosine - pltpu.roll(vectors, HEAD_WIDTH // 2, 1) * sine


def head_cols(index):
    return slice(index * HEAD_WIDTH, (index + 1) * HEAD_WIDTH)


def prepare_keys(rows, pos_ref, key_ref, value_ref, kv_ref):
    cosine, sine = angle_tables(rows, key_ref.shape[0], pos_ref)
    for head in range(KEY_VALUE_HEADS):
        chunk, place = divmod(head, HEADS_PER_CHUNK)
        place += 2 * chunk * HEADS_PER_CHUNK
        rotated = rope(key_ref[:, head_cols(head)].astype(jnp.float32), cosine, sine)
        kv_ref[:, head_cols(place)] = rotated.astype(jnp.bfloat16)
        kv_ref[:, head_cols(HEADS_PER_CHUNK + place)] = value_ref[:, head_cols(head)]


def stack(chunk, *refs):
    *block_refs, stack_ref = refs
    for place, ref in enumerate(block_refs):
        stack_ref[place] = ref[:, 2 * chunk * CHUNK_COLS : 2 * (chunk + 1) * CHUNK_COLS]


def prepare_queries(rows, pos_ref, query_ref, grad_ref, *out_refs):
    q_ref, qt_ref, g_ref, gt_ref, cos_ref, sin_ref, cos_t_ref, sin_t_ref = out_refs

    @pl.when(pl.program_id(0) == 0)
    def _():
        cosine, sine = angle_tables(rows, query_ref.shape[0], pos_ref)
        cos_ref[...] = cosine
        sin_ref[...] = sine
        half = HEAD_WIDTH // 2
        cos_t_ref[...] = jnp.concatenate([cosine] * GROUP, 0).T[half:] * SCORE_SCALE
        sin_t_ref[...] = jnp.concatenate([sine] * GROUP, 0).T[half:] * SCORE_SCALE

    cosine, sine = cos_ref[...], sin_ref[...]
    queries = jnp.concatenate(
        [
            rope(query_ref[:, head_cols(h)].astype(jnp.float32), cosine, sine)
            for h in range(GROUP)
        ],
        0,
    )
    grads = jnp.concatenate(
        [grad_ref[:, head_cols(h)].astype(jnp.float32) for h in range(GROUP)], 0
    )
    q_ref[0] = queries.astype(jnp.bfloat16)
    qt_ref[0] = queries.T.astype(jnp.bfloat16)
    g_ref[0] = grads.astype(jnp.bfloat16)
    gt_ref[0] = grads.T.astype(jnp.bfloat16)


def dot(left, right):
    return jnp.dot(left, right, preferred_element_type=jnp.float32)


def attend(seq_count, head_count, rows, pieces, has_alias, counts_ref, *refs):
    blocks = seq_count * head_count
    kv_refs = []
    for ref in refs[:pieces]:
        kv_refs += [ref] if len(ref.shape) == 2 else [ref.at[i] for i in range(ref.shape[0])]
    q_ref, qt_ref, g_ref, gt_ref, cos_ref, sin_ref = refs[pieces : pieces + 6]
    outs = refs[pieces + 6 + 2 * has_alias :]
    out_ref, grad_ref = outs[:2]
    part_refs = outs[2 : 2 + seq_count]
    bias_ref, live_ref = outs[2 + seq_count :]
    padded = kv_refs[0].shape[0]
    query_rows = GROUP * padded
    step = pl.program_id(0)
    seq_index, head_index = lax.axis_index("seq"), lax.axis_index("head")
    my_rank = seq_index * head_count + head_index

    @pl.when(step == 0)
    def _():
        key_row = lax.broadcasted_iota(jnp.int32, (padded, query_rows), 0)
        query_row = lax.rem(lax.broadcasted_iota(jnp.int32, (padded, query_rows), 1), padded)
        for block in range(blocks):
            seq_offset, head_offset = divmod(block, head_count)
            seq_from = jnp.bitwise_xor(seq_index, seq_offset)
            head_from = jnp.bitwise_xor(head_index, head_offset)
            rank = seq_from * head_count + head_from
            limit = jnp.minimum(counts_ref[seq_from] - head_from * rows, rows)
            limit = jnp.where(rank <= my_rank, limit, 0)
            allowed = key_row < limit
            if block == 0:
                allowed = allowed & (key_row <= query_row)
                live_ref[...] = (query_row[:8] < limit).astype(jnp.float32)
            bias_ref[block * padded : (block + 1) * padded, :] = jnp.where(allowed, 0.0, -1e30)

    def lanes(first, place):
        start = pl.multiple_of((first + step * STEP_HEADS + place) * HEAD_WIDTH, HEAD_WIDTH)
        return pl.ds(start, HEAD_WIDTH)

    def gathered(first, place):
        cols = lanes(first, place)
        wide = jnp.concatenate([ref[:, cols].astype(jnp.float32) for ref in kv_refs], 0)
        low = wide.astype(jnp.bfloat16)
        return low, low.T

    heads = range(STEP_HEADS)
    keys, values = [gathered(0, p) for p in heads], [gathered(HEADS_PER_CHUNK, p) for p in heads]
    bias, live = bias_ref[...], live_ref[0:1, :]
    scores = [dot(keys[p][0], qt_ref[p]) * SCORE_SCALE + bias for p in heads]
    dprobs, probs, probs_low = [], [], []
    for p in heads:
        weights = jnp.exp(scores[p] - jnp.max(scores[p], 0, keepdims=True))
        probs.append(weights * (live / jnp.sum(weights, 0, keepdims=True)))
        probs_low.append(probs[p].astype(jnp.bfloat16))
        dprobs.append(dot(values[p][0], gt_ref[p]))
    outs_t, value_parts, dscores = [], [], []
    for p in heads:
        outs_t.append(dot(values[p][1], probs_low[p]))
        value_parts.append(dot(probs_low[p], g_ref[p]))
        out_low = outs_t[p].astype(jnp.bfloat16).astype(jnp.float32)
        delta = jnp.sum(gt_ref[p].astype(jnp.float32) * out_low, 0, keepdims=True)
        dscores.append((probs[p] * (dprobs[p] - delta)).astype(jnp.bfloat16))
    grads_t = [dot(keys[p][1], dscores[p]) for p in heads]
    key_parts = [dot(dscores[p], q_ref[p]) * SCORE_SCALE for p in heads]

    cosine, sine = cos_ref[...], sin_ref[...]
    half = HEAD_WIDTH // 2
    for p in heads:
        first, second = grads_t[p][:half], grads_t[p][half:]
        turned = [first * cosine + second * sine, second * cosine - first * sine]
        grad_low = jnp.concatenate(turned, 0).astype(jnp.bfloat16)
        out_heads = outs_t[p].astype(jnp.bfloat16).T.astype(jnp.float32)
        grad_heads = grad_low.T.astype(jnp.float32)
        for h in range(GROUP):
            piece, cols = slice(h * padded, (h + 1) * padded), head_cols(p * GROUP + h)
            out_ref[:, cols] = out_heads[piece].astype(jnp.bfloat16)
            grad_ref[:, cols] = grad_heads[piece].astype(jnp.bfloat16)
        for block in range(blocks):
            seq_offset, head_offset = divmod(block, head_count)
            piece = slice(block * padded, (block + 1) * padded)
            part_ref = part_refs[seq_offset]
            part_ref[head_offset, :, lanes(0, p)] = key_parts[p][piece].astype(jnp.bfloat16)
            part_ref[head_offset, :, lanes(HEADS_PER_CHUNK, p)] = value_parts[p][piece].astype(
                jnp.bfloat16
            )


def combine(seq_count, head_count, *refs):
    part_refs, base_ref, send_refs = refs[:seq_count], refs[seq_count], refs[seq_count + 1 :]
    for offset in range(head_count):
        total = part_refs[0][offset].astype(jnp.float32)
        for ref in part_refs[1:]:
            total = total + ref[offset].astype(jnp.float32)
        if offset == 0:
            base_ref[...] = total
        else:
            send_refs[offset - 1][...] = total.astype(jnp.bfloat16)


def finish(head_count, *refs):
    cosine, sine = refs[0][...], refs[1][...]
    key_ref, value_ref = refs[-2:]
    for chunk in range(CHUNKS):
        mine = refs[2 + chunk * head_count : 2 + (chunk + 1) * head_count]
        for place in range(HEADS_PER_CHUNK):
            here, there = head_cols(place), head_cols(HEADS_PER_CHUNK + place)
            key_total, value_total = mine[0][:, here], mine[0][:, there]
            for ref in mine[1:]:
                key_total = key_total + ref[:, here].astype(jnp.float32)
                value_total = value_total + ref[:, there].astype(jnp.float32)
            cols = head_cols(chunk * HEADS_PER_CHUNK + place)
            key_ref[:, cols] = rope_back(key_total, cosine, sine).astype(jnp.bfloat16)
            value_ref[:, cols] = value_total.astype(jnp.bfloat16)


def params(mebibytes):
    return pltpu.CompilerParams(vmem_limit_bytes=mebibytes << 20)


def cost(microseconds):
    return pl.CostEstimate(
        flops=microseconds * 1153 * 10**6,
        bytes_accessed=microseconds * 3690 * 10**3,
        transcendentals=0,
    )


def shards(queries, routed_keys, routed_values, output_gradient, positions, counts):
    seq_count = lax.axis_size("seq")
    head_count = lax.axis_size("head")
    blocks = seq_count * head_count
    rows = queries.shape[0]
    padded = -(-rows // 8) * 8
    if padded != rows:
        extra = ((0, padded - rows), (0, 0))
        queries, routed_keys, routed_values, output_gradient = (
            jnp.pad(x, extra) for x in (queries, routed_keys, routed_values, output_gradient)
        )
    query_rows = GROUP * padded
    shape = jax.ShapeDtypeStruct
    bf16, f32 = jnp.bfloat16, jnp.float32
    ranks = [(s, z) for s in range(seq_count) for z in range(head_count)]

    def rank_of(s, z):
        return s * head_count + z

    def along_head(x, offset, upward, held=0):
        pairs = []
        for s, z in ranks:
            other = z ^ offset
            if s < seq_count - 1 or ((z ^ held) < other) == upward:
                pairs.append((rank_of(s, z), rank_of(s, other)))
        return lax.ppermute(x, ("seq", "head"), pairs)

    def along_seq(x, offset, upward):
        pairs = [
            (rank_of(s, z), rank_of(s ^ offset, z))
            for s, z in ranks
            if (s < (s ^ offset)) == upward
        ]
        return lax.ppermute(x, ("seq", "head"), pairs)

    table = shape((padded, HEAD_WIDTH), f32)
    table_t = shape((HEAD_WIDTH // 2, query_rows), f32)
    piece = shape((padded, 2 * CHUNK_COLS), bf16)
    own = pl.pallas_call(
        functools.partial(prepare_keys, rows),
        out_shape=shape((padded, CHUNKS * 2 * CHUNK_COLS), bf16),
        in_specs=[SMEM, VMEM, VMEM],
        out_specs=VMEM,
        compiler_params=params(56),
        name="prepare_keys",
    )(positions, routed_keys, routed_values)

    wide = GROUP * HEAD_WIDTH
    row_block = pl.BlockSpec((padded, wide), lambda g: (0, g))
    table_block = pl.BlockSpec((padded, HEAD_WIDTH), lambda g: (0, 0))
    tall_block = pl.BlockSpec((1, query_rows, HEAD_WIDTH), lambda g: (g, 0, 0))
    flat_block = pl.BlockSpec((1, HEAD_WIDTH, query_rows), lambda g: (g, 0, 0))
    tall = shape((KEY_VALUE_HEADS, query_rows, HEAD_WIDTH), bf16)
    flat = shape((KEY_VALUE_HEADS, HEAD_WIDTH, query_rows), bf16)
    table_t_block = pl.BlockSpec(table_t.shape, lambda g: (0, 0))
    *stacked, cosine, sine, cosine_t, sine_t = pl.pallas_call(
        functools.partial(prepare_queries, rows),
        grid=(KEY_VALUE_HEADS,),
        out_shape=[tall, flat, tall, flat, table, table, table_t, table_t],
        in_specs=[SMEM, row_block, row_block],
        out_specs=[tall_block, flat_block, tall_block, flat_block]
        + [table_block, table_block, table_t_block, table_t_block],
        cost_estimate=cost(7),
        compiler_params=params(16),
        name="prepare_queries",
    )(positions, queries, output_gradient)

    bits = [1 << b for b in reversed(range((head_count - 1).bit_length()))]
    later = range(1, seq_count)
    last = head_count - 1
    near = {0: own, **{j: along_head(own, j, True) for j in sorted({bits[0], 1}, reverse=True)}}
    far = {a: along_seq(own, a, True) for a in later}
    near, cosine_t, far = lax.optimization_barrier((near, cosine_t, far))
    for bit in bits[1:]:
        near.update(
            {j ^ bit: along_head(x, bit, True, j) for j, x in near.items() if j ^ bit not in near}
        )

    def cross(chunk, offsets):
        held = pl.pallas_call(
            functools.partial(stack, chunk),
            out_shape=shape((len(offsets), padded, 2 * CHUNK_COLS), bf16),
            in_specs=[VMEM] * len(offsets),
            out_specs=VMEM,
            compiler_params=params(8),
            name="stack",
        )(*(near[j] for j in offsets))
        return {a: along_seq(held, a, True) for a in later}

    crossed = [[cross(0, range(1, last)), cross(0, [last])]]
    near[last], crossed[0][0] = lax.optimization_barrier((near[last], crossed[0][0]))
    crossed += [[cross(chunk, range(1, head_count))] for chunk in range(1, CHUNKS)]

    wide_outs = ()
    parts = []
    for chunk in range(CHUNKS):
        first = chunk * HEADS_PER_CHUNK // STEP_HEADS
        has_alias = int(chunk > 0)
        tall_part, flat_part = (
            pl.BlockSpec((STEP_HEADS, *x.shape[1:]), lambda g, f=first: (f + g, 0, 0))
            for x in (tall, flat)
        )
        row_part = pl.BlockSpec((padded, STEP_HEADS * wide), lambda g, f=first: (0, f + g))
        gathered = [near[j] for j in range(head_count)]
        for a in later:
            gathered += [far[a]] + [part[a] for part in crossed[chunk]]
        inputs = len(gathered)
        kv_whole = pl.BlockSpec((padded, 2 * CHUNK_COLS), lambda g, c=chunk: (0, c))
        kv_specs = [
            kv_whole if len(x.shape) == 2 else pl.BlockSpec(x.shape, lambda g: (0, 0, 0))
            for x in gathered
        ]
        part_block = pl.BlockSpec((head_count, padded, 2 * CHUNK_COLS), lambda g: (0, 0, 0))
        out = pl.pallas_call(
            functools.partial(attend, seq_count, head_count, rows, inputs, has_alias),
            grid=(HEADS_PER_CHUNK // STEP_HEADS,),
            out_shape=[shape((padded, QUERY_HEADS * HEAD_WIDTH), bf16)] * 2
            + [shape((head_count, padded, 2 * CHUNK_COLS), bf16)] * seq_count,
            in_specs=[SMEM]
            + kv_specs
            + [tall_part, flat_part, tall_part, flat_part, table_t_block, table_t_block]
            + [pl.BlockSpec(memory_space=pl.ANY)] * (2 * has_alias),
            out_specs=[row_part, row_part] + [part_block] * seq_count,
            scratch_shapes=[
                pltpu.VMEM((blocks * padded, query_rows), f32),
                pltpu.VMEM((8, query_rows), f32),
            ],
            input_output_aliases={inputs + 7: 0, inputs + 8: 1} if has_alias else {},
            cost_estimate=cost(10),
            compiler_params=params(32),
            name="attend",
        )(counts, *gathered, *stacked, cosine_t, sine_t, *wide_outs)
        wide_outs = out[:2]
        parts.append([out[2]] + [along_seq(out[2 + a], a, False) for a in later])

    summed = []
    for mine in parts:
        if summed:
            mine[-1], summed[-head_count] = lax.optimization_barrier(
                (mine[-1], summed[-head_count])
            )
        base, *sends = pl.pallas_call(
            functools.partial(combine, seq_count, head_count),
            out_shape=[shape((padded, 2 * CHUNK_COLS), f32)] + [piece] * (head_count - 1),
            in_specs=[VMEM] * seq_count,
            out_specs=[VMEM] * head_count,
            cost_estimate=cost(2),
            compiler_params=params(8),
            name="combine",
        )(*mine)
        summed += [base] + [along_head(x, j + 1, False) for j, x in enumerate(sends)]

    narrow = shape((padded, KEY_VALUE_HEADS * HEAD_WIDTH), bf16)
    key_grad, value_grad = pl.pallas_call(
        functools.partial(finish, head_count),
        out_shape=[narrow, narrow],
        in_specs=[VMEM] * (2 + CHUNKS * head_count),
        out_specs=[VMEM, VMEM],
        cost_estimate=cost(2),
        compiler_params=params(8),
        name="finish",
    )(cosine, sine, *summed)
    results = (*wide_outs, key_grad, value_grad)
    if padded != rows:
        results = tuple(x[:rows] for x in results)
    return results


def solution(mesh):
    rows = P(("dp", "seq", "head"), None)
    return jax.shard_map(
        shards,
        mesh=mesh,
        in_specs=(rows, rows, rows, rows, P("dp"), P("dp")),
        out_specs=(rows, rows, rows, rows),
        check_vma=False,
    )
```

```python
import functools

import jax
import jax.numpy as jnp
import numpy as np
from jax import lax
from jax.experimental import pallas as pl
from jax.experimental.pallas import tpu as pltpu
from jax.sharding import PartitionSpec as P

QUERY_HEADS = 64
KEY_VALUE_HEADS = 8
HEAD_WIDTH = 128
GROUP = QUERY_HEADS // KEY_VALUE_HEADS
ROPE_BASE = 500000.0
SCORE_SCALE = 1.0 / float(np.sqrt(HEAD_WIDTH))
CHUNKS = 2
HEADS_PER_CHUNK = KEY_VALUE_HEADS // CHUNKS
CHUNK_COLS = HEADS_PER_CHUNK * HEAD_WIDTH
STEP_HEADS = 2
VMEM = pl.BlockSpec(memory_space=pltpu.VMEM)
SMEM = pl.BlockSpec(memory_space=pltpu.SMEM)


def inverse_freq_row():
    half = HEAD_WIDTH // 2
    place = lax.rem(lax.broadcasted_iota(jnp.int32, (8, HEAD_WIDTH), 1), half)
    row = jnp.ones((8, HEAD_WIDTH), jnp.float32)
    for i in range(1, half):
        row = jnp.where(place == i, np.float32(ROPE_BASE ** (-2.0 * i / HEAD_WIDTH)), row)
    return row[0:1]


def angle_tables(rows, padded, pos_ref):
    start = (lax.axis_index("seq") * lax.axis_size("head") + lax.axis_index("head")) * rows
    sublane = lax.broadcasted_iota(jnp.int32, (8, HEAD_WIDTH), 0)
    pieces = []
    for base in range(0, padded, 8):
        piece = jnp.zeros((8, HEAD_WIDTH), jnp.int32)
        for offset in range(min(8, rows - base)):
            piece = jnp.where(sublane == offset, pos_ref[start + (base + offset)], piece)
        pieces.append(piece)
    angle = jnp.concatenate(pieces, 0).astype(jnp.float32) * inverse_freq_row()
    lane = lax.broadcasted_iota(jnp.int32, angle.shape, 1)
    return jnp.cos(angle), jnp.sin(angle) * jnp.where(lane < HEAD_WIDTH // 2, -1.0, 1.0)


def rope(vectors, cosine, sine):
    return vectors * cosine + pltpu.roll(vectors, HEAD_WIDTH // 2, 1) * sine


def rope_back(vectors, cosine, sine):
    return vectors * cosine - pltpu.roll(vectors, HEAD_WIDTH // 2, 1) * sine


def head_cols(index):
    return slice(index * HEAD_WIDTH, (index + 1) * HEAD_WIDTH)


def prepare_keys(rows, pos_ref, key_ref, value_ref, whole_ref, *kv_refs):
    cosine, sine = angle_tables(rows, key_ref.shape[0], pos_ref)
    for head in range(KEY_VALUE_HEADS):
        chunk, place = divmod(head, HEADS_PER_CHUNK)
        rotated = rope(key_ref[:, head_cols(head)].astype(jnp.float32), cosine, sine)
        columns = {
            place: rotated.astype(jnp.bfloat16),
            HEADS_PER_CHUNK + place: value_ref[:, head_cols(head)],
        }
        for column, x in columns.items():
            kv_refs[chunk][0, :, head_cols(column)] = x
            whole_ref[:, head_cols(2 * chunk * HEADS_PER_CHUNK + column)] = x


def stack(*refs):
    *block_refs, stack_ref = refs
    place = 0
    for ref in block_refs:
        for i in range(ref.shape[0]):
            stack_ref[place] = ref[i]
            place += 1


def prepare_queries(rows, pos_ref, query_ref, grad_ref, *out_refs):
    q_ref, qt_ref, g_ref, gt_ref, cos_ref, sin_ref, cos_t_ref, sin_t_ref = out_refs

    @pl.when(pl.program_id(0) == 0)
    def _():
        cosine, sine = angle_tables(rows, query_ref.shape[0], pos_ref)
        cos_ref[...] = cosine
        sin_ref[...] = sine
        half = HEAD_WIDTH // 2
        cos_t_ref[...] = jnp.concatenate([cosine] * GROUP, 0).T[half:] * SCORE_SCALE
        sin_t_ref[...] = jnp.concatenate([sine] * GROUP, 0).T[half:] * SCORE_SCALE

    cosine, sine = cos_ref[...], sin_ref[...]
    queries = jnp.concatenate(
        [
            rope(query_ref[:, head_cols(h)].astype(jnp.float32), cosine, sine)
            for h in range(GROUP)
        ],
        0,
    )
    grads = jnp.concatenate(
        [grad_ref[:, head_cols(h)].astype(jnp.float32) for h in range(GROUP)], 0
    )
    q_ref[0] = queries.astype(jnp.bfloat16)
    qt_ref[0] = queries.T.astype(jnp.bfloat16)
    g_ref[0] = grads.astype(jnp.bfloat16)
    gt_ref[0] = grads.T.astype(jnp.bfloat16)


def dot(left, right):
    return jnp.dot(left, right, preferred_element_type=jnp.float32)


def blocks_of(refs):
    return [
        block
        for ref in refs
        for block in ([ref] if len(ref.shape) == 2 else [ref.at[i] for i in range(ref.shape[0])])
    ]


def attend(seq_count, head_count, rows, pieces, order, has_alias, counts_ref, *refs):
    blocks = seq_count * head_count
    kv_refs = [ref for _, ref in sorted(zip(order, blocks_of(refs[:pieces])), key=lambda x: x[0])]
    q_ref, qt_ref, g_ref, gt_ref, cos_ref, sin_ref = refs[pieces : pieces + 6]
    outs = refs[pieces + 6 + 2 * has_alias :]
    out_ref, grad_ref = outs[:2]
    part_refs = outs[2 : 2 + seq_count]
    bias_ref, live_ref = outs[2 + seq_count :]
    padded = kv_refs[0].shape[0]
    query_rows = GROUP * padded
    step = pl.program_id(0)
    seq_index, head_index = lax.axis_index("seq"), lax.axis_index("head")
    my_rank = seq_index * head_count + head_index

    @pl.when(step == 0)
    def _():
        key_row = lax.broadcasted_iota(jnp.int32, (padded, query_rows), 0)
        query_row = lax.rem(lax.broadcasted_iota(jnp.int32, (padded, query_rows), 1), padded)
        for block in range(blocks):
            seq_offset, head_offset = divmod(block, head_count)
            seq_from = jnp.bitwise_xor(seq_index, seq_offset)
            head_from = jnp.bitwise_xor(head_index, head_offset)
            rank = seq_from * head_count + head_from
            limit = jnp.minimum(counts_ref[seq_from] - head_from * rows, rows)
            limit = jnp.where(rank <= my_rank, limit, 0)
            allowed = key_row < limit
            if block == 0:
                allowed = allowed & (key_row <= query_row)
                live_ref[...] = (query_row[:8] < limit).astype(jnp.float32)
            bias_ref[block * padded : (block + 1) * padded, :] = jnp.where(allowed, 0.0, -1e30)

    def lanes(first, place):
        start = pl.multiple_of((first + step * STEP_HEADS + place) * HEAD_WIDTH, HEAD_WIDTH)
        return pl.ds(start, HEAD_WIDTH)

    def gathered(first, place):
        cols = lanes(first, place)
        wide = jnp.concatenate([ref[:, cols].astype(jnp.float32) for ref in kv_refs], 0)
        low = wide.astype(jnp.bfloat16)
        return low, low.T

    heads = range(STEP_HEADS)
    keys, values = [gathered(0, p) for p in heads], [gathered(HEADS_PER_CHUNK, p) for p in heads]
    bias, live = bias_ref[...], live_ref[0:1, :]
    scores = [dot(keys[p][0], qt_ref[p]) * SCORE_SCALE + bias for p in heads]
    dprobs, probs, probs_low = [], [], []
    for p in heads:
        weights = jnp.exp(scores[p] - jnp.max(scores[p], 0, keepdims=True))
        probs.append(weights * (live / jnp.sum(weights, 0, keepdims=True)))
        probs_low.append(probs[p].astype(jnp.bfloat16))
        dprobs.append(dot(values[p][0], gt_ref[p]))
    outs_t, value_parts, dscores = [], [], []
    for p in heads:
        outs_t.append(dot(values[p][1], probs_low[p]))
        value_parts.append(dot(probs_low[p], g_ref[p]))
        out_low = outs_t[p].astype(jnp.bfloat16).astype(jnp.float32)
        delta = jnp.sum(gt_ref[p].astype(jnp.float32) * out_low, 0, keepdims=True)
        dscores.append((probs[p] * (dprobs[p] - delta)).astype(jnp.bfloat16))
    grads_t = [dot(keys[p][1], dscores[p]) for p in heads]
    key_parts = [dot(dscores[p], q_ref[p]) * SCORE_SCALE for p in heads]

    cosine, sine = cos_ref[...], sin_ref[...]
    half = HEAD_WIDTH // 2
    for p in heads:
        first, second = grads_t[p][:half], grads_t[p][half:]
        turned = [first * cosine + second * sine, second * cosine - first * sine]
        grad_low = jnp.concatenate(turned, 0).astype(jnp.bfloat16)
        out_heads = outs_t[p].astype(jnp.bfloat16).T.astype(jnp.float32)
        grad_heads = grad_low.T.astype(jnp.float32)
        for h in range(GROUP):
            piece, cols = slice(h * padded, (h + 1) * padded), head_cols(p * GROUP + h)
            out_ref[:, cols] = out_heads[piece].astype(jnp.bfloat16)
            grad_ref[:, cols] = grad_heads[piece].astype(jnp.bfloat16)
        for block in range(blocks):
            seq_offset, head_offset = divmod(block, head_count)
            piece = slice(block * padded, (block + 1) * padded)
            part_ref = part_refs[seq_offset]
            part_ref[head_offset, :, lanes(0, p)] = key_parts[p][piece].astype(jnp.bfloat16)
            part_ref[head_offset, :, lanes(HEADS_PER_CHUNK, p)] = value_parts[p][piece].astype(
                jnp.bfloat16
            )


def combine_near(seq_count, *refs):
    part_refs, base_ref, send_refs = refs[:seq_count], refs[seq_count], refs[seq_count + 1 :]
    for offset in range(len(send_refs) + 1):
        total = sum(ref[offset].astype(jnp.float32) for ref in part_refs)
        if offset == 0:
            base_ref[...] = total
        else:
            send_refs[offset - 1][...] = total.astype(jnp.bfloat16)


def combine_ranks(*refs):
    *part_refs, send_ref = refs
    for offset in range(send_ref.shape[0]):
        total = sum(ref[offset].astype(jnp.float32) for ref in part_refs)
        send_ref[jnp.bitwise_xor(lax.axis_index("head"), offset)] = total.astype(jnp.bfloat16)


def finish(inputs, cos_ref, sin_ref, *refs):
    cosine, sine = cos_ref[...], sin_ref[...]
    key_ref, value_ref = refs[-2:]
    for chunk in range(CHUNKS):
        mine = blocks_of(refs[sum(inputs[:chunk]) : sum(inputs[: chunk + 1])])
        for place in range(HEADS_PER_CHUNK):
            here, there = head_cols(place), head_cols(HEADS_PER_CHUNK + place)
            key_total = sum(ref[:, here].astype(jnp.float32) for ref in mine)
            value_total = sum(ref[:, there].astype(jnp.float32) for ref in mine)
            cols = head_cols(chunk * HEADS_PER_CHUNK + place)
            key_ref[:, cols] = rope_back(key_total, cosine, sine).astype(jnp.bfloat16)
            value_ref[:, cols] = value_total.astype(jnp.bfloat16)


def params(mebibytes):
    return pltpu.CompilerParams(vmem_limit_bytes=mebibytes << 20)


def cost(microseconds):
    return pl.CostEstimate(
        flops=microseconds * 1153 * 10**6,
        bytes_accessed=microseconds * 3690 * 10**3,
        transcendentals=0,
    )


def shards(queries, routed_keys, routed_values, output_gradient, positions, counts):
    seq_count = lax.axis_size("seq")
    head_count = lax.axis_size("head")
    blocks = seq_count * head_count
    rows = queries.shape[0]
    padded = -(-rows // 8) * 8
    if padded != rows:
        extra = ((0, padded - rows), (0, 0))
        queries, routed_keys, routed_values, output_gradient = (
            jnp.pad(x, extra) for x in (queries, routed_keys, routed_values, output_gradient)
        )
    query_rows = GROUP * padded
    shape = jax.ShapeDtypeStruct
    bf16, f32 = jnp.bfloat16, jnp.float32
    ranks = [(s, z) for s in range(seq_count) for z in range(head_count)]

    def rank_of(s, z):
        return s * head_count + z

    def along_head(x, offset, upward, held=(0,)):
        pairs = []
        for s, z in ranks:
            other = z ^ offset
            if s < seq_count - 1 or any(((z ^ h) < other) == upward for h in held):
                pairs.append((rank_of(s, z), rank_of(s, other)))
        return lax.ppermute(x, ("seq", "head"), pairs)

    def along_seq(x, offset, upward):
        pairs = [
            (rank_of(s, z), rank_of(s ^ offset, z))
            for s, z in ranks
            if (s < (s ^ offset)) == upward
        ]
        return lax.ppermute(x, ("seq", "head"), pairs)

    table = shape((padded, HEAD_WIDTH), f32)
    table_t = shape((HEAD_WIDTH // 2, query_rows), f32)
    piece = shape((padded, 2 * CHUNK_COLS), bf16)
    whole, *own = pl.pallas_call(
        functools.partial(prepare_keys, rows),
        out_shape=[shape((padded, CHUNKS * 2 * CHUNK_COLS), bf16)]
        + [shape((1, padded, 2 * CHUNK_COLS), bf16)] * CHUNKS,
        in_specs=[SMEM, VMEM, VMEM],
        out_specs=[VMEM] * (CHUNKS + 1),
        compiler_params=params(56),
        name="prepare_keys",
    )(positions, routed_keys, routed_values)

    wide = GROUP * HEAD_WIDTH
    row_block = pl.BlockSpec((padded, wide), lambda g: (0, g))
    table_block = pl.BlockSpec((padded, HEAD_WIDTH), lambda g: (0, 0))
    tall_block = pl.BlockSpec((1, query_rows, HEAD_WIDTH), lambda g: (g, 0, 0))
    flat_block = pl.BlockSpec((1, HEAD_WIDTH, query_rows), lambda g: (g, 0, 0))
    tall = shape((KEY_VALUE_HEADS, query_rows, HEAD_WIDTH), bf16)
    flat = shape((KEY_VALUE_HEADS, HEAD_WIDTH, query_rows), bf16)
    table_t_block = pl.BlockSpec(table_t.shape, lambda g: (0, 0))
    *stacked, cosine, sine, cosine_t, sine_t = pl.pallas_call(
        functools.partial(prepare_queries, rows),
        grid=(KEY_VALUE_HEADS,),
        out_shape=[tall, flat, tall, flat, table, table, table_t, table_t],
        in_specs=[SMEM, row_block, row_block],
        out_specs=[tall_block, flat_block, tall_block, flat_block]
        + [table_block, table_block, table_t_block, table_t_block],
        cost_estimate=cost(7),
        compiler_params=params(16),
        name="prepare_queries",
    )(positions, queries, output_gradient)

    later = range(1, seq_count)
    bits = [1 << b for b in reversed(range((head_count - 1).bit_length()))]

    def stacked_blocks(xs):
        if len(xs) == 1:
            return xs[0]
        return pl.pallas_call(
            stack,
            out_shape=shape((sum(x.shape[0] for x in xs), *xs[0].shape[1:]), bf16),
            in_specs=[VMEM] * len(xs),
            out_specs=VMEM,
            compiler_params=params(8),
            name="stack",
        )(*xs)

    far = {a: along_seq(whole, a, True) for a in later}
    near, crossed = [], []
    for chunk in range(CHUNKS):
        held, received, passed = [0], [], []
        for bit in bits:
            x = along_head(stacked_blocks([own[chunk], *received]), bit, True, held)
            if chunk == 0 and bit == bits[0]:
                x, own[1:], cosine_t, far = lax.optimization_barrier(
                    (x, own[1:], cosine_t, far)
                )
            if chunk == 0:
                if bit == bits[-1]:
                    x, passed = lax.optimization_barrier((x, passed))
                passed.append({a: along_seq(x, a, True) for a in later})
            elif bit == bits[0]:
                x, near[-1][-1] = lax.optimization_barrier((x, near[-1][-1]))
            received.append(x)
            held += [h ^ bit for h in held]
        near.append(received)
        if chunk:
            passed = [{a: along_seq(stacked_blocks(received), a, True) for a in later}]
        crossed.append(passed)
    order = [a * head_count + h for a in range(seq_count) for h in held]

    wide_outs = ()
    parts = []
    for chunk in range(CHUNKS):
        first = chunk * HEADS_PER_CHUNK // STEP_HEADS
        has_alias = int(chunk > 0)
        tall_part, flat_part = (
            pl.BlockSpec((STEP_HEADS, *x.shape[1:]), lambda g, f=first: (f + g, 0, 0))
            for x in (tall, flat)
        )
        row_part = pl.BlockSpec((padded, STEP_HEADS * wide), lambda g, f=first: (0, f + g))
        gathered = [whole, *near[chunk]]
        for a in later:
            gathered += [far[a]] + [part[a] for part in crossed[chunk]]
        inputs = len(gathered)
        kv_whole = pl.BlockSpec((padded, 2 * CHUNK_COLS), lambda g, c=chunk: (0, c))
        kv_specs = [
            kv_whole if len(x.shape) == 2 else pl.BlockSpec(x.shape, lambda g: (0, 0, 0))
            for x in gathered
        ]
        part_block = pl.BlockSpec((head_count, padded, 2 * CHUNK_COLS), lambda g: (0, 0, 0))
        out = pl.pallas_call(
            functools.partial(attend, seq_count, head_count, rows, inputs, order, has_alias),
            grid=(HEADS_PER_CHUNK // STEP_HEADS,),
            out_shape=[shape((padded, QUERY_HEADS * HEAD_WIDTH), bf16)] * 2
            + [shape((head_count, padded, 2 * CHUNK_COLS), bf16)] * seq_count,
            in_specs=[SMEM]
            + kv_specs
            + [tall_part, flat_part, tall_part, flat_part, table_t_block, table_t_block]
            + [pl.BlockSpec(memory_space=pl.ANY)] * (2 * has_alias),
            out_specs=[row_part, row_part] + [part_block] * seq_count,
            scratch_shapes=[
                pltpu.VMEM((blocks * padded, query_rows), f32),
                pltpu.VMEM((8, query_rows), f32),
            ],
            input_output_aliases={inputs + 7: 0, inputs + 8: 1} if has_alias else {},
            cost_estimate=cost(10),
            compiler_params=params(32),
            name="attend",
        )(counts, *gathered, *stacked, cosine_t, sine_t, *wide_outs)
        wide_outs = out[:2]
        parts.append([out[2]] + [along_seq(out[2 + a], a, False) for a in later])

    summed = []
    for mine in parts[:-1]:
        base, *sends = pl.pallas_call(
            functools.partial(combine_near, seq_count),
            out_shape=[shape((padded, 2 * CHUNK_COLS), f32)] + [piece] * (head_count - 1),
            in_specs=[VMEM] * seq_count,
            out_specs=[VMEM] * head_count,
            cost_estimate=cost(2),
            compiler_params=params(8),
            name="combine_near",
        )(*mine)
        parts[-1][-1], base = lax.optimization_barrier((parts[-1][-1], base))
        summed.append([base] + [along_head(x, j + 1, False) for j, x in enumerate(sends)])
    sums = pl.pallas_call(
        combine_ranks,
        out_shape=shape((head_count, padded, 2 * CHUNK_COLS), bf16),
        in_specs=[VMEM] * seq_count,
        out_specs=VMEM,
        cost_estimate=cost(2),
        compiler_params=params(8),
        name="combine_ranks",
    )(*parts[-1])
    summed.append([lax.all_to_all(sums, "head", split_axis=0, concat_axis=0, tiled=True)])

    narrow = shape((padded, KEY_VALUE_HEADS * HEAD_WIDTH), bf16)
    key_grad, value_grad = pl.pallas_call(
        functools.partial(finish, [len(xs) for xs in summed]),
        out_shape=[narrow, narrow],
        in_specs=[VMEM] * (2 + sum(len(xs) for xs in summed)),
        out_specs=[VMEM, VMEM],
        cost_estimate=cost(2),
        compiler_params=params(8),
        name="finish",
    )(cosine, sine, *(x for xs in summed for x in xs))
    results = (*wide_outs, key_grad, value_grad)
    if padded != rows:
        results = tuple(x[:rows] for x in results)
    return results


def solution(mesh):
    rows = P(("dp", "seq", "head"), None)
    return jax.shard_map(
        shards,
        mesh=mesh,
        in_specs=(rows, rows, rows, rows, P("dp"), P("dp")),
        out_specs=(rows, rows, rows, rows),
        check_vma=False,
    )
```

```python
import functools

import jax
import jax.numpy as jnp
import numpy as np
from jax import lax
from jax.experimental import pallas as pl
from jax.experimental.pallas import tpu as pltpu
from jax.sharding import PartitionSpec as P

QUERY_HEADS = 64
KEY_VALUE_HEADS = 8
HEAD_WIDTH = 128
GROUP = QUERY_HEADS // KEY_VALUE_HEADS
ROPE_BASE = 500000.0
SCORE_SCALE = 1.0 / float(np.sqrt(HEAD_WIDTH))
SCORE_TO_LOG2 = SCORE_SCALE * 1.4426950408889634
CHUNKS = 2
HEADS_PER_CHUNK = KEY_VALUE_HEADS // CHUNKS
CHUNK_COLS = HEADS_PER_CHUNK * HEAD_WIDTH
STEP_HEADS = 2
VMEM = pl.BlockSpec(memory_space=pltpu.VMEM)
SMEM = pl.BlockSpec(memory_space=pltpu.SMEM)


def inverse_freq_row():
    half = HEAD_WIDTH // 2
    place = lax.rem(lax.broadcasted_iota(jnp.int32, (8, HEAD_WIDTH), 1), half)
    row = jnp.ones((8, HEAD_WIDTH), jnp.float32)
    for i in range(1, half):
        row = jnp.where(place == i, np.float32(ROPE_BASE ** (-2.0 * i / HEAD_WIDTH)), row)
    return row[0:1]


def angle_tables(rows, padded, pos_ref):
    start = (lax.axis_index("seq") * lax.axis_size("head") + lax.axis_index("head")) * rows
    sublane = lax.broadcasted_iota(jnp.int32, (8, HEAD_WIDTH), 0)
    pieces = []
    for base in range(0, padded, 8):
        piece = jnp.zeros((8, HEAD_WIDTH), jnp.int32)
        for offset in range(min(8, rows - base)):
            piece = jnp.where(sublane == offset, pos_ref[start + (base + offset)], piece)
        pieces.append(piece)
    angle = jnp.concatenate(pieces, 0).astype(jnp.float32) * inverse_freq_row()
    lane = lax.broadcasted_iota(jnp.int32, angle.shape, 1)
    return jnp.cos(angle), jnp.sin(angle) * jnp.where(lane < HEAD_WIDTH // 2, -1.0, 1.0)


def rope(vectors, cosine, sine):
    return vectors * cosine + pltpu.roll(vectors, HEAD_WIDTH // 2, 1) * sine


def rope_back(vectors, cosine, sine):
    return vectors * cosine - pltpu.roll(vectors, HEAD_WIDTH // 2, 1) * sine


def head_cols(index):
    return slice(index * HEAD_WIDTH, (index + 1) * HEAD_WIDTH)


def prepare_keys(rows, pos_ref, key_ref, value_ref, kv_ref):
    cosine, sine = angle_tables(rows, key_ref.shape[0], pos_ref)
    for head in range(KEY_VALUE_HEADS):
        chunk, place = divmod(head, HEADS_PER_CHUNK)
        place += 2 * chunk * HEADS_PER_CHUNK
        rotated = rope(key_ref[:, head_cols(head)].astype(jnp.float32), cosine, sine)
        kv_ref[:, head_cols(place)] = rotated.astype(jnp.bfloat16)
        kv_ref[:, head_cols(HEADS_PER_CHUNK + place)] = value_ref[:, head_cols(head)]


def stack(chunk, *refs):
    *block_refs, stack_ref = refs
    place = 0
    for ref in block_refs:
        if len(ref.shape) == 2:
            stack_ref[place] = ref[:, 2 * chunk * CHUNK_COLS : 2 * (chunk + 1) * CHUNK_COLS]
            place += 1
        else:
            for i in range(ref.shape[0]):
                stack_ref[place + i] = ref[i]
            place += ref.shape[0]


def prepare_queries(rows, pos_ref, query_ref, grad_ref, *out_refs):
    q_ref, qt_ref, g_ref, gt_ref, cos_ref, sin_ref, cos_t_ref, sin_t_ref = out_refs

    @pl.when(pl.program_id(0) == 0)
    def _():
        cosine, sine = angle_tables(rows, query_ref.shape[0], pos_ref)
        cos_ref[...] = cosine
        sin_ref[...] = sine
        half = HEAD_WIDTH // 2
        cos_t_ref[...] = jnp.concatenate([cosine] * GROUP, 0).T[half:] * SCORE_SCALE
        sin_t_ref[...] = jnp.concatenate([sine] * GROUP, 0).T[half:] * SCORE_SCALE

    cosine, sine = cos_ref[...], sin_ref[...]
    queries = jnp.concatenate(
        [
            rope(query_ref[:, head_cols(h)].astype(jnp.float32), cosine, sine)
            for h in range(GROUP)
        ],
        0,
    )
    grads = jnp.concatenate(
        [grad_ref[:, head_cols(h)].astype(jnp.float32) for h in range(GROUP)], 0
    )
    q_ref[0] = queries.astype(jnp.bfloat16)
    qt_ref[0] = queries.T.astype(jnp.bfloat16)
    g_ref[0] = grads.astype(jnp.bfloat16)
    gt_ref[0] = grads.T.astype(jnp.bfloat16)


def dot(left, right):
    return jnp.dot(left, right, preferred_element_type=jnp.float32)


def attend(seq_count, head_count, rows, pieces, order, has_alias, counts_ref, *refs):
    blocks = seq_count * head_count
    kv_refs = [None] * blocks
    places = iter(order)
    for ref in refs[:pieces]:
        for block in [ref] if len(ref.shape) == 2 else [ref.at[i] for i in range(ref.shape[0])]:
            kv_refs[next(places)] = block
    q_ref, qt_ref, g_ref, gt_ref, cos_ref, sin_ref = refs[pieces : pieces + 6]
    outs = refs[pieces + 6 + 2 * has_alias :]
    out_ref, grad_ref = outs[:2]
    part_refs = outs[2 : 2 + seq_count]
    bias_ref, live_ref = outs[2 + seq_count :]
    padded = kv_refs[0].shape[0]
    query_rows = GROUP * padded
    step = pl.program_id(0)
    seq_index, head_index = lax.axis_index("seq"), lax.axis_index("head")
    my_rank = seq_index * head_count + head_index

    @pl.when(step == 0)
    def _():
        key_row = lax.broadcasted_iota(jnp.int32, (padded, query_rows), 0)
        query_row = lax.rem(lax.broadcasted_iota(jnp.int32, (padded, query_rows), 1), padded)
        for block in range(blocks):
            seq_offset, head_offset = divmod(block, head_count)
            seq_from = jnp.bitwise_xor(seq_index, seq_offset)
            head_from = jnp.bitwise_xor(head_index, head_offset)
            rank = seq_from * head_count + head_from
            limit = jnp.minimum(counts_ref[seq_from] - head_from * rows, rows)
            limit = jnp.where(rank <= my_rank, limit, 0)
            allowed = key_row < limit
            if block == 0:
                allowed = allowed & (key_row <= query_row)
                live_ref[...] = (query_row[:8] < limit).astype(jnp.float32)
            bias_ref[block * padded : (block + 1) * padded, :] = jnp.where(allowed, 0.0, -1e30)

    def lanes(first, place):
        start = pl.multiple_of((first + step * STEP_HEADS + place) * HEAD_WIDTH, HEAD_WIDTH)
        return pl.ds(start, HEAD_WIDTH)

    def gathered(first, place):
        cols = lanes(first, place)
        wide = jnp.concatenate([ref[:, cols].astype(jnp.float32) for ref in kv_refs], 0)
        low = wide.astype(jnp.bfloat16)
        return low, low.T

    heads = range(STEP_HEADS)
    keys, values = [gathered(0, p) for p in heads], [gathered(HEADS_PER_CHUNK, p) for p in heads]
    bias, live = bias_ref[...], live_ref[0:1, :]
    scores = [dot(keys[p][0], qt_ref[p]) * SCORE_TO_LOG2 + bias for p in heads]
    dprobs, probs, probs_low = [], [], []
    for p in heads:
        weights = jnp.exp2(scores[p] - jnp.max(scores[p], 0, keepdims=True))
        probs.append(weights * (live / jnp.sum(weights, 0, keepdims=True)))
        probs_low.append(probs[p].astype(jnp.bfloat16))
        dprobs.append(dot(values[p][0], gt_ref[p]))
    outs_t, value_parts, dscores = [], [], []
    for p in heads:
        outs_t.append(dot(values[p][1], probs_low[p]))
        value_parts.append(dot(probs_low[p], g_ref[p]))
        out_low = outs_t[p].astype(jnp.bfloat16).astype(jnp.float32)
        delta = jnp.sum(gt_ref[p].astype(jnp.float32) * out_low, 0, keepdims=True)
        dscores.append((probs[p] * (dprobs[p] - delta)).astype(jnp.bfloat16))
    grads_t = [dot(keys[p][1], dscores[p]) for p in heads]
    key_parts = [dot(dscores[p], q_ref[p]) * SCORE_SCALE for p in heads]

    cosine, sine = cos_ref[...], sin_ref[...]
    half = HEAD_WIDTH // 2
    for p in heads:
        first, second = grads_t[p][:half], grads_t[p][half:]
        turned = [first * cosine + second * sine, second * cosine - first * sine]
        grad_low = jnp.concatenate(turned, 0).astype(jnp.bfloat16)
        out_heads = outs_t[p].astype(jnp.bfloat16).T.astype(jnp.float32)
        grad_heads = grad_low.T.astype(jnp.float32)
        for h in range(GROUP):
            piece, cols = slice(h * padded, (h + 1) * padded), head_cols(p * GROUP + h)
            out_ref[:, cols] = out_heads[piece].astype(jnp.bfloat16)
            grad_ref[:, cols] = grad_heads[piece].astype(jnp.bfloat16)
        for block in range(blocks):
            seq_offset, head_offset = divmod(block, head_count)
            piece = slice(block * padded, (block + 1) * padded)
            part_ref = part_refs[seq_offset]
            part_ref[head_offset, :, lanes(0, p)] = key_parts[p][piece].astype(jnp.bfloat16)
            part_ref[head_offset, :, lanes(HEADS_PER_CHUNK, p)] = value_parts[p][piece].astype(
                jnp.bfloat16
            )


def combine(seq_count, head_count, *refs):
    part_refs, base_ref, send_refs = refs[:seq_count], refs[seq_count], refs[seq_count + 1 :]
    for offset in range(head_count):
        total = part_refs[0][offset].astype(jnp.float32)
        for ref in part_refs[1:]:
            total = total + ref[offset].astype(jnp.float32)
        if offset == 0:
            base_ref[...] = total
        else:
            send_refs[offset - 1][...] = total.astype(jnp.bfloat16)


def finish(head_count, *refs):
    cosine, sine = refs[0][...], refs[1][...]
    key_ref, value_ref = refs[-2:]
    for chunk in range(CHUNKS):
        mine = refs[2 + chunk * head_count : 2 + (chunk + 1) * head_count]
        for place in range(HEADS_PER_CHUNK):
            here, there = head_cols(place), head_cols(HEADS_PER_CHUNK + place)
            key_total, value_total = mine[0][:, here], mine[0][:, there]
            for ref in mine[1:]:
                key_total = key_total + ref[:, here].astype(jnp.float32)
                value_total = value_total + ref[:, there].astype(jnp.float32)
            cols = head_cols(chunk * HEADS_PER_CHUNK + place)
            key_ref[:, cols] = rope_back(key_total, cosine, sine).astype(jnp.bfloat16)
            value_ref[:, cols] = value_total.astype(jnp.bfloat16)


def params(mebibytes):
    return pltpu.CompilerParams(vmem_limit_bytes=mebibytes << 20)


def cost(microseconds):
    return pl.CostEstimate(
        flops=microseconds * 1153 * 10**6,
        bytes_accessed=microseconds * 3690 * 10**3,
        transcendentals=0,
    )


def shards(queries, routed_keys, routed_values, output_gradient, positions, counts):
    seq_count = lax.axis_size("seq")
    head_count = lax.axis_size("head")
    blocks = seq_count * head_count
    rows = queries.shape[0]
    padded = -(-rows // 8) * 8
    if padded != rows:
        extra = ((0, padded - rows), (0, 0))
        queries, routed_keys, routed_values, output_gradient = (
            jnp.pad(x, extra) for x in (queries, routed_keys, routed_values, output_gradient)
        )
    query_rows = GROUP * padded
    shape = jax.ShapeDtypeStruct
    bf16, f32 = jnp.bfloat16, jnp.float32
    ranks = [(s, z) for s in range(seq_count) for z in range(head_count)]

    def rank_of(s, z):
        return s * head_count + z

    def along_head(x, offset, upward, held=0):
        pairs = []
        for s, z in ranks:
            other = z ^ offset
            if s < seq_count - 1 or ((z ^ held) < other) == upward:
                pairs.append((rank_of(s, z), rank_of(s, other)))
        return lax.ppermute(x, ("seq", "head"), pairs)

    def along_seq(x, offset, upward):
        pairs = [
            (rank_of(s, z), rank_of(s ^ offset, z))
            for s, z in ranks
            if (s < (s ^ offset)) == upward
        ]
        return lax.ppermute(x, ("seq", "head"), pairs)

    table = shape((padded, HEAD_WIDTH), f32)
    table_t = shape((HEAD_WIDTH // 2, query_rows), f32)
    piece = shape((padded, 2 * CHUNK_COLS), bf16)
    own = pl.pallas_call(
        functools.partial(prepare_keys, rows),
        out_shape=shape((padded, CHUNKS * 2 * CHUNK_COLS), bf16),
        in_specs=[SMEM, VMEM, VMEM],
        out_specs=VMEM,
        compiler_params=params(56),
        name="prepare_keys",
    )(positions, routed_keys, routed_values)

    wide = GROUP * HEAD_WIDTH
    row_block = pl.BlockSpec((padded, wide), lambda g: (0, g))
    table_block = pl.BlockSpec((padded, HEAD_WIDTH), lambda g: (0, 0))
    tall_block = pl.BlockSpec((1, query_rows, HEAD_WIDTH), lambda g: (g, 0, 0))
    flat_block = pl.BlockSpec((1, HEAD_WIDTH, query_rows), lambda g: (g, 0, 0))
    tall = shape((KEY_VALUE_HEADS, query_rows, HEAD_WIDTH), bf16)
    flat = shape((KEY_VALUE_HEADS, HEAD_WIDTH, query_rows), bf16)
    table_t_block = pl.BlockSpec(table_t.shape, lambda g: (0, 0))
    *stacked, cosine, sine, cosine_t, sine_t = pl.pallas_call(
        functools.partial(prepare_queries, rows),
        grid=(KEY_VALUE_HEADS,),
        out_shape=[tall, flat, tall, flat, table, table, table_t, table_t],
        in_specs=[SMEM, row_block, row_block],
        out_specs=[tall_block, flat_block, tall_block, flat_block]
        + [table_block, table_block, table_t_block, table_t_block],
        cost_estimate=cost(7),
        compiler_params=params(16),
        name="prepare_queries",
    )(positions, queries, output_gradient)

    bits = [1 << b for b in reversed(range((head_count - 1).bit_length()))]
    later = range(1, seq_count)
    whole = {0: own, **{j: along_head(own, j, True) for j in sorted({bits[0], 1})}}
    far = {a: along_seq(own, a, True) for a in later}
    whole, cosine_t, far = lax.optimization_barrier((whole, cosine_t, far))

    def stacked_blocks(chunk, xs):
        if len(xs) == 1 and len(xs[0].shape) == 3:
            return xs[0]
        count = sum(1 if len(x.shape) == 2 else x.shape[0] for x in xs)
        return pl.pallas_call(
            functools.partial(stack, chunk),
            out_shape=shape((count, padded, 2 * CHUNK_COLS), bf16),
            in_specs=[VMEM] * len(xs),
            out_specs=VMEM,
            compiler_params=params(8),
            name="stack",
        )(*xs)

    def cross(chunk, xs):
        held = stacked_blocks(chunk, xs)
        return {a: along_seq(held, a, True) for a in later}

    near, crossed = [], []
    for chunk in range(CHUNKS):
        blocks_here = dict(whole)
        for bit in bits[1:]:
            for j, x in list(blocks_here.items()):
                if j ^ bit not in blocks_here:
                    held = stacked_blocks(chunk, [x])
                    blocks_here[j ^ bit] = along_head(held, bit, True, j)
        direct = [x for j, x in blocks_here.items() if j in whole and j]
        derived = [x for j, x in blocks_here.items() if j not in whole]
        if chunk == 0:
            crossed.append([cross(chunk, direct), cross(chunk, derived)])
        else:
            derived, crossed[0][0] = lax.optimization_barrier((derived, crossed[0][0]))
            crossed.append([cross(chunk, direct + derived)])
        near.append([*whole.values(), *derived])
    offsets = list(blocks_here)
    order = [a * head_count + j for a in range(seq_count) for j in offsets]

    wide_outs = ()
    parts = []
    for chunk in range(CHUNKS):
        first = chunk * HEADS_PER_CHUNK // STEP_HEADS
        has_alias = int(chunk > 0)
        tall_part, flat_part = (
            pl.BlockSpec((STEP_HEADS, *x.shape[1:]), lambda g, f=first: (f + g, 0, 0))
            for x in (tall, flat)
        )
        row_part = pl.BlockSpec((padded, STEP_HEADS * wide), lambda g, f=first: (0, f + g))
        gathered = list(near[chunk])
        for a in later:
            gathered += [far[a]] + [part[a] for part in crossed[chunk]]
        inputs = len(gathered)
        kv_whole = pl.BlockSpec((padded, 2 * CHUNK_COLS), lambda g, c=chunk: (0, c))
        kv_specs = [
            kv_whole if len(x.shape) == 2 else pl.BlockSpec(x.shape, lambda g: (0, 0, 0))
            for x in gathered
        ]
        part_block = pl.BlockSpec((head_count, padded, 2 * CHUNK_COLS), lambda g: (0, 0, 0))
        out = pl.pallas_call(
            functools.partial(attend, seq_count, head_count, rows, inputs, order, has_alias),
            grid=(HEADS_PER_CHUNK // STEP_HEADS,),
            out_shape=[shape((padded, QUERY_HEADS * HEAD_WIDTH), bf16)] * 2
            + [shape((head_count, padded, 2 * CHUNK_COLS), bf16)] * seq_count,
            in_specs=[SMEM]
            + kv_specs
            + [tall_part, flat_part, tall_part, flat_part, table_t_block, table_t_block]
            + [pl.BlockSpec(memory_space=pl.ANY)] * (2 * has_alias),
            out_specs=[row_part, row_part] + [part_block] * seq_count,
            scratch_shapes=[
                pltpu.VMEM((blocks * padded, query_rows), f32),
                pltpu.VMEM((8, query_rows), f32),
            ],
            input_output_aliases={inputs + 7: 0, inputs + 8: 1} if has_alias else {},
            cost_estimate=cost(10),
            compiler_params=params(32),
            name="attend",
        )(counts, *gathered, *stacked, cosine_t, sine_t, *wide_outs)
        wide_outs = out[:2]
        parts.append([out[2]] + [along_seq(out[2 + a], a, False) for a in later])

    summed = []
    for mine in parts:
        if summed:
            mine[-1], summed[-head_count] = lax.optimization_barrier(
                (mine[-1], summed[-head_count])
            )
        base, *sends = pl.pallas_call(
            functools.partial(combine, seq_count, head_count),
            out_shape=[shape((padded, 2 * CHUNK_COLS), f32)] + [piece] * (head_count - 1),
            in_specs=[VMEM] * seq_count,
            out_specs=[VMEM] * head_count,
            cost_estimate=cost(2),
            compiler_params=params(8),
            name="combine",
        )(*mine)
        summed += [base] + [along_head(x, j + 1, False) for j, x in enumerate(sends)]

    narrow = shape((padded, KEY_VALUE_HEADS * HEAD_WIDTH), bf16)
    key_grad, value_grad = pl.pallas_call(
        functools.partial(finish, head_count),
        out_shape=[narrow, narrow],
        in_specs=[VMEM] * (2 + CHUNKS * head_count),
        out_specs=[VMEM, VMEM],
        cost_estimate=cost(2),
        compiler_params=params(8),
        name="finish",
    )(cosine, sine, *summed)
    results = (*wide_outs, key_grad, value_grad)
    if padded != rows:
        results = tuple(x[:rows] for x in results)
    return results


def solution(mesh):
    rows = P(("dp", "seq", "head"), None)
    return jax.shard_map(
        shards,
        mesh=mesh,
        in_specs=(rows, rows, rows, rows, P("dp"), P("dp")),
        out_specs=(rows, rows, rows, rows),
        check_vma=False,
    )
```

```python
import functools

import jax
import jax.numpy as jnp
import numpy as np
from jax import lax
from jax.experimental import pallas as pl
from jax.experimental.pallas import tpu as pltpu
from jax.sharding import PartitionSpec as P

QUERY_HEADS = 64
KEY_VALUE_HEADS = 8
HEAD_WIDTH = 128
GROUP = QUERY_HEADS // KEY_VALUE_HEADS
ROPE_BASE = 500000.0
SCORE_SCALE = 1.0 / float(np.sqrt(HEAD_WIDTH))
SCORE_TO_LOG2 = SCORE_SCALE * 1.4426950408889634
CHUNKS = 2
HEADS_PER_CHUNK = KEY_VALUE_HEADS // CHUNKS
CHUNK_COLS = HEADS_PER_CHUNK * HEAD_WIDTH
STEP_HEADS = 2
VMEM = pl.BlockSpec(memory_space=pltpu.VMEM)
SMEM = pl.BlockSpec(memory_space=pltpu.SMEM)


def inverse_freq_row():
    half = HEAD_WIDTH // 2
    place = lax.rem(lax.broadcasted_iota(jnp.int32, (8, HEAD_WIDTH), 1), half)
    row = jnp.ones((8, HEAD_WIDTH), jnp.float32)
    for i in range(1, half):
        row = jnp.where(place == i, np.float32(ROPE_BASE ** (-2.0 * i / HEAD_WIDTH)), row)
    return row[0:1]


def angle_tables(rows, padded, pos_ref):
    start = (lax.axis_index("seq") * lax.axis_size("head") + lax.axis_index("head")) * rows
    sublane = lax.broadcasted_iota(jnp.int32, (8, HEAD_WIDTH), 0)
    pieces = []
    for base in range(0, padded, 8):
        piece = jnp.zeros((8, HEAD_WIDTH), jnp.int32)
        for offset in range(min(8, rows - base)):
            piece = jnp.where(sublane == offset, pos_ref[start + (base + offset)], piece)
        pieces.append(piece)
    angle = jnp.concatenate(pieces, 0).astype(jnp.float32) * inverse_freq_row()
    lane = lax.broadcasted_iota(jnp.int32, angle.shape, 1)
    return jnp.cos(angle), jnp.sin(angle) * jnp.where(lane < HEAD_WIDTH // 2, -1.0, 1.0)


def rope(vectors, cosine, sine):
    return vectors * cosine + pltpu.roll(vectors, HEAD_WIDTH // 2, 1) * sine


def rope_back(vectors, cosine, sine):
    return vectors * cosine - pltpu.roll(vectors, HEAD_WIDTH // 2, 1) * sine


def head_cols(index):
    return slice(index * HEAD_WIDTH, (index + 1) * HEAD_WIDTH)


def prepare_keys(rows, pos_ref, key_ref, value_ref, kv_ref):
    cosine, sine = angle_tables(rows, key_ref.shape[0], pos_ref)
    for head in range(KEY_VALUE_HEADS):
        chunk, place = divmod(head, HEADS_PER_CHUNK)
        place += 2 * chunk * HEADS_PER_CHUNK
        rotated = rope(key_ref[:, head_cols(head)].astype(jnp.float32), cosine, sine)
        kv_ref[:, head_cols(place)] = rotated.astype(jnp.bfloat16)
        kv_ref[:, head_cols(HEADS_PER_CHUNK + place)] = value_ref[:, head_cols(head)]


def stack(chunks, *refs):
    *block_refs, stack_ref = refs
    for place, (chunk, ref) in enumerate(zip(chunks, block_refs)):
        stack_ref[place] = ref[:, 2 * chunk * CHUNK_COLS : 2 * (chunk + 1) * CHUNK_COLS]


def prepare_queries(rows, pos_ref, query_ref, grad_ref, *out_refs):
    q_ref, qt_ref, g_ref, gt_ref, cos_ref, sin_ref, cos_t_ref, sin_t_ref = out_refs

    @pl.when(pl.program_id(0) == 0)
    def _():
        cosine, sine = angle_tables(rows, query_ref.shape[0], pos_ref)
        cos_ref[...] = cosine
        sin_ref[...] = sine
        half = HEAD_WIDTH // 2
        cos_t_ref[...] = jnp.concatenate([cosine] * GROUP, 0).T[half:] * SCORE_SCALE
        sin_t_ref[...] = jnp.concatenate([sine] * GROUP, 0).T[half:] * SCORE_SCALE

    cosine, sine = cos_ref[...], sin_ref[...]
    queries = jnp.concatenate(
        [
            rope(query_ref[:, head_cols(h)].astype(jnp.float32), cosine, sine)
            for h in range(GROUP)
        ],
        0,
    )
    grads = jnp.concatenate(
        [grad_ref[:, head_cols(h)].astype(jnp.float32) for h in range(GROUP)], 0
    )
    q_ref[0] = queries.astype(jnp.bfloat16)
    qt_ref[0] = queries.T.astype(jnp.bfloat16)
    g_ref[0] = grads.astype(jnp.bfloat16)
    gt_ref[0] = grads.T.astype(jnp.bfloat16)


def dot(left, right):
    return jnp.dot(left, right, preferred_element_type=jnp.float32)


def attend(seq_count, head_count, rows, has_alias, counts_ref, *refs):
    blocks = seq_count * head_count
    kv_refs = [ref if len(ref.shape) == 2 else ref.at[0] for ref in refs[:blocks]]
    q_ref, qt_ref, g_ref, gt_ref, cos_ref, sin_ref = refs[blocks : blocks + 6]
    outs = refs[blocks + 6 + 2 * has_alias :]
    out_ref, grad_ref = outs[:2]
    part_refs = outs[2 : 2 + seq_count]
    bias_ref, live_ref = outs[2 + seq_count :]
    padded = kv_refs[0].shape[0]
    query_rows = GROUP * padded
    step = pl.program_id(0)
    seq_index, head_index = lax.axis_index("seq"), lax.axis_index("head")
    my_rank = seq_index * head_count + head_index

    @pl.when(step == 0)
    def _():
        key_row = lax.broadcasted_iota(jnp.int32, (padded, query_rows), 0)
        query_row = lax.rem(lax.broadcasted_iota(jnp.int32, (padded, query_rows), 1), padded)
        for block in range(blocks):
            seq_offset, head_offset = divmod(block, head_count)
            seq_from = jnp.bitwise_xor(seq_index, seq_offset)
            head_from = jnp.bitwise_xor(head_index, head_offset)
            rank = seq_from * head_count + head_from
            limit = jnp.minimum(counts_ref[seq_from] - head_from * rows, rows)
            limit = jnp.where(rank <= my_rank, limit, 0)
            allowed = key_row < limit
            if block == 0:
                allowed = allowed & (key_row <= query_row)
                live_ref[...] = (query_row[:8] < limit).astype(jnp.float32)
            bias_ref[block * padded : (block + 1) * padded, :] = jnp.where(allowed, 0.0, -1e30)

    def lanes(first, place):
        start = pl.multiple_of((first + step * STEP_HEADS + place) * HEAD_WIDTH, HEAD_WIDTH)
        return pl.ds(start, HEAD_WIDTH)

    def gathered(first, place):
        cols = lanes(first, place)
        wide = jnp.concatenate([ref[:, cols].astype(jnp.float32) for ref in kv_refs], 0)
        low = wide.astype(jnp.bfloat16)
        return low, low.T

    heads = range(STEP_HEADS)
    keys, values = [gathered(0, p) for p in heads], [gathered(HEADS_PER_CHUNK, p) for p in heads]
    bias, live = bias_ref[...], live_ref[0:1, :]
    scores = [dot(keys[p][0], qt_ref[p]) * SCORE_TO_LOG2 + bias for p in heads]
    dprobs, probs, probs_low = [], [], []
    for p in heads:
        weights = jnp.exp2(scores[p] - jnp.max(scores[p], 0, keepdims=True))
        probs.append(weights * (live / jnp.sum(weights, 0, keepdims=True)))
        probs_low.append(probs[p].astype(jnp.bfloat16))
        dprobs.append(dot(values[p][0], gt_ref[p]))
    outs_t, value_parts, dscores = [], [], []
    for p in heads:
        outs_t.append(dot(values[p][1], probs_low[p]))
        value_parts.append(dot(probs_low[p], g_ref[p]))
        out_low = outs_t[p].astype(jnp.bfloat16).astype(jnp.float32)
        delta = jnp.sum(gt_ref[p].astype(jnp.float32) * out_low, 0, keepdims=True)
        dscores.append((probs[p] * (dprobs[p] - delta)).astype(jnp.bfloat16))
    grads_t = [dot(keys[p][1], dscores[p]) for p in heads]
    key_parts = [dot(dscores[p], q_ref[p]) * SCORE_SCALE for p in heads]

    cosine, sine = cos_ref[...], sin_ref[...]
    half = HEAD_WIDTH // 2
    for p in heads:
        first, second = grads_t[p][:half], grads_t[p][half:]
        turned = [first * cosine + second * sine, second * cosine - first * sine]
        grad_low = jnp.concatenate(turned, 0).astype(jnp.bfloat16)
        out_heads = outs_t[p].astype(jnp.bfloat16).T.astype(jnp.float32)
        grad_heads = grad_low.T.astype(jnp.float32)
        for h in range(GROUP):
            piece, cols = slice(h * padded, (h + 1) * padded), head_cols(p * GROUP + h)
            out_ref[:, cols] = out_heads[piece].astype(jnp.bfloat16)
            grad_ref[:, cols] = grad_heads[piece].astype(jnp.bfloat16)
        for block in range(blocks):
            seq_offset, head_offset = divmod(block, head_count)
            piece = slice(block * padded, (block + 1) * padded)
            part_ref = part_refs[seq_offset]
            part_ref[head_offset, :, lanes(0, p)] = key_parts[p][piece].astype(jnp.bfloat16)
            part_ref[head_offset, :, lanes(HEADS_PER_CHUNK, p)] = value_parts[p][piece].astype(
                jnp.bfloat16
            )


def combine(seq_count, head_count, *refs):
    part_refs, base_ref, send_refs = refs[:seq_count], refs[seq_count], refs[seq_count + 1 :]
    for offset in range(head_count):
        total = part_refs[0][offset].astype(jnp.float32)
        for ref in part_refs[1:]:
            total = total + ref[offset].astype(jnp.float32)
        if offset == 0:
            base_ref[...] = total
        else:
            send_refs[offset - 1][...] = total.astype(jnp.bfloat16)


def finish(head_count, *refs):
    cosine, sine = refs[0][...], refs[1][...]
    key_ref, value_ref = refs[-2:]
    for chunk in range(CHUNKS):
        mine = refs[2 + chunk * head_count : 2 + (chunk + 1) * head_count]
        for place in range(HEADS_PER_CHUNK):
            here, there = head_cols(place), head_cols(HEADS_PER_CHUNK + place)
            key_total, value_total = mine[0][:, here], mine[0][:, there]
            for ref in mine[1:]:
                key_total = key_total + ref[:, here].astype(jnp.float32)
                value_total = value_total + ref[:, there].astype(jnp.float32)
            cols = head_cols(chunk * HEADS_PER_CHUNK + place)
            key_ref[:, cols] = rope_back(key_total, cosine, sine).astype(jnp.bfloat16)
            value_ref[:, cols] = value_total.astype(jnp.bfloat16)


def params(mebibytes):
    return pltpu.CompilerParams(vmem_limit_bytes=mebibytes << 20)


def cost(microseconds):
    return pl.CostEstimate(
        flops=microseconds * 1153 * 10**6,
        bytes_accessed=microseconds * 3690 * 10**3,
        transcendentals=0,
    )


def shards(queries, routed_keys, routed_values, output_gradient, positions, counts):
    seq_count = lax.axis_size("seq")
    head_count = lax.axis_size("head")
    blocks = seq_count * head_count
    rows = queries.shape[0]
    padded = -(-rows // 8) * 8
    if padded != rows:
        extra = ((0, padded - rows), (0, 0))
        queries, routed_keys, routed_values, output_gradient = (
            jnp.pad(x, extra) for x in (queries, routed_keys, routed_values, output_gradient)
        )
    query_rows = GROUP * padded
    shape = jax.ShapeDtypeStruct
    bf16, f32 = jnp.bfloat16, jnp.float32
    ranks = [(s, z) for s in range(seq_count) for z in range(head_count)]

    def rank_of(s, z):
        return s * head_count + z

    def along_head(x, offset, upward, held=0):
        pairs = []
        for s, z in ranks:
            other = z ^ offset
            if s < seq_count - 1 or ((z ^ held) < other) == upward:
                pairs.append((rank_of(s, z), rank_of(s, other)))
        return lax.ppermute(x, ("seq", "head"), pairs)

    def along_seq(x, offset, upward):
        pairs = [
            (rank_of(s, z), rank_of(s ^ offset, z))
            for s, z in ranks
            if (s < (s ^ offset)) == upward
        ]
        return lax.ppermute(x, ("seq", "head"), pairs)

    table = shape((padded, HEAD_WIDTH), f32)
    table_t = shape((HEAD_WIDTH // 2, query_rows), f32)
    piece = shape((padded, 2 * CHUNK_COLS), bf16)
    own = pl.pallas_call(
        functools.partial(prepare_keys, rows),
        out_shape=shape((padded, CHUNKS * 2 * CHUNK_COLS), bf16),
        in_specs=[SMEM, VMEM, VMEM],
        out_specs=VMEM,
        compiler_params=params(56),
        name="prepare_keys",
    )(positions, routed_keys, routed_values)

    wide = GROUP * HEAD_WIDTH
    row_block = pl.BlockSpec((padded, wide), lambda g: (0, g))
    table_block = pl.BlockSpec((padded, HEAD_WIDTH), lambda g: (0, 0))
    tall_block = pl.BlockSpec((1, query_rows, HEAD_WIDTH), lambda g: (g, 0, 0))
    flat_block = pl.BlockSpec((1, HEAD_WIDTH, query_rows), lambda g: (g, 0, 0))
    tall = shape((KEY_VALUE_HEADS, query_rows, HEAD_WIDTH), bf16)
    flat = shape((KEY_VALUE_HEADS, HEAD_WIDTH, query_rows), bf16)
    table_t_block = pl.BlockSpec(table_t.shape, lambda g: (0, 0))
    *stacked, cosine, sine, cosine_t, sine_t = pl.pallas_call(
        functools.partial(prepare_queries, rows),
        grid=(KEY_VALUE_HEADS,),
        out_shape=[tall, flat, tall, flat, table, table, table_t, table_t],
        in_specs=[SMEM, row_block, row_block],
        out_specs=[tall_block, flat_block, tall_block, flat_block]
        + [table_block, table_block, table_t_block, table_t_block],
        cost_estimate=cost(7),
        compiler_params=params(16),
        name="prepare_queries",
    )(positions, queries, output_gradient)

    bits = [1 << b for b in reversed(range((head_count - 1).bit_length()))]
    later = range(1, seq_count)
    near = {0: own, **{j: along_head(own, j, True) for j in sorted({bits[0], 1})}}
    far = {a: along_seq(own, a, True) for a in later}
    near[1], cosine_t, far = lax.optimization_barrier((near[1], cosine_t, far))

    def cross(*pieces):
        held = pl.pallas_call(
            functools.partial(stack, [chunk for _, chunk in pieces]),
            out_shape=shape((len(pieces), padded, 2 * CHUNK_COLS), bf16),
            in_specs=[VMEM] * len(pieces),
            out_specs=VMEM,
            compiler_params=params(8),
            name="stack",
        )(*(near[j] for j, _ in pieces))
        for a in later:
            moved = along_seq(held, a, True)
            crossed.update({(a, *piece): (moved, i) for i, piece in enumerate(pieces)})

    crossed = {}
    cross((1, 0))
    if bits[0] > 1:
        first = {a: crossed[a, 1, 0][0] for a in later}
        near[bits[0]], first = lax.optimization_barrier((near[bits[0]], first))
        crossed = {(a, 1, 0): (first[a], 0) for a in later}
    for bit in bits[1:]:
        near.update(
            {j ^ bit: along_head(x, bit, True, j) for j, x in near.items() if j ^ bit not in near}
        )
    rest = range(2, head_count)
    for j in rest[:1]:
        cross((j, 0), *((1, chunk) for chunk in range(1, CHUNKS)))
    for j in rest[1:]:
        cross((j, 0))
    for chunk in range(1, CHUNKS):
        cross(*((j, chunk) for j in (rest or [1])))

    wide_outs = ()
    parts = []
    for chunk in range(CHUNKS):
        first = chunk * HEADS_PER_CHUNK // STEP_HEADS
        has_alias = int(chunk > 0)
        tall_part, flat_part = (
            pl.BlockSpec((STEP_HEADS, *x.shape[1:]), lambda g, f=first: (f + g, 0, 0))
            for x in (tall, flat)
        )
        row_part = pl.BlockSpec((padded, STEP_HEADS * wide), lambda g, f=first: (0, f + g))
        gathered = [(near[j], None) for j in range(head_count)]
        for a in later:
            gathered.append((far[a], None))
            gathered += [crossed[a, j, chunk] for j in range(1, head_count)]
        inputs = len(gathered)
        kv_whole = pl.BlockSpec((padded, 2 * CHUNK_COLS), lambda g, c=chunk: (0, c))
        kv_specs = [
            kv_whole
            if place is None
            else pl.BlockSpec((1, padded, 2 * CHUNK_COLS), lambda g, i=place: (i, 0, 0))
            for _, place in gathered
        ]
        part_block = pl.BlockSpec((head_count, padded, 2 * CHUNK_COLS), lambda g: (0, 0, 0))
        out = pl.pallas_call(
            functools.partial(attend, seq_count, head_count, rows, has_alias),
            grid=(HEADS_PER_CHUNK // STEP_HEADS,),
            out_shape=[shape((padded, QUERY_HEADS * HEAD_WIDTH), bf16)] * 2
            + [shape((head_count, padded, 2 * CHUNK_COLS), bf16)] * seq_count,
            in_specs=[SMEM]
            + kv_specs
            + [tall_part, flat_part, tall_part, flat_part, table_t_block, table_t_block]
            + [pl.BlockSpec(memory_space=pl.ANY)] * (2 * has_alias),
            out_specs=[row_part, row_part] + [part_block] * seq_count,
            scratch_shapes=[
                pltpu.VMEM((blocks * padded, query_rows), f32),
                pltpu.VMEM((8, query_rows), f32),
            ],
            input_output_aliases={inputs + 7: 0, inputs + 8: 1} if has_alias else {},
            cost_estimate=cost(10),
            compiler_params=params(32),
            name="attend",
        )(counts, *(x for x, _ in gathered), *stacked, cosine_t, sine_t, *wide_outs)
        wide_outs = out[:2]
        parts.append([out[2]] + [along_seq(out[2 + a], a, False) for a in later])

    summed = []
    for mine in parts:
        if summed:
            mine[-1], summed[-head_count] = lax.optimization_barrier(
                (mine[-1], summed[-head_count])
            )
        base, *sends = pl.pallas_call(
            functools.partial(combine, seq_count, head_count),
            out_shape=[shape((padded, 2 * CHUNK_COLS), f32)] + [piece] * (head_count - 1),
            in_specs=[VMEM] * seq_count,
            out_specs=[VMEM] * head_count,
            cost_estimate=cost(2),
            compiler_params=params(8),
            name="combine",
        )(*mine)
        summed += [base] + [along_head(x, j + 1, False) for j, x in enumerate(sends)]

    narrow = shape((padded, KEY_VALUE_HEADS * HEAD_WIDTH), bf16)
    key_grad, value_grad = pl.pallas_call(
        functools.partial(finish, head_count),
        out_shape=[narrow, narrow],
        in_specs=[VMEM] * (2 + CHUNKS * head_count),
        out_specs=[VMEM, VMEM],
        cost_estimate=cost(2),
        compiler_params=params(8),
        name="finish",
    )(cosine, sine, *summed)
    results = (*wide_outs, key_grad, value_grad)
    if padded != rows:
        results = tuple(x[:rows] for x in results)
    return results


def solution(mesh):
    rows = P(("dp", "seq", "head"), None)
    return jax.shard_map(
        shards,
        mesh=mesh,
        in_specs=(rows, rows, rows, rows, P("dp"), P("dp")),
        out_specs=(rows, rows, rows, rows),
        check_vma=False,
    )
```

```python
import functools

import jax
import jax.numpy as jnp
import numpy as np
from jax import lax
from jax.experimental import pallas as pl
from jax.experimental.pallas import tpu as pltpu
from jax.sharding import PartitionSpec as P

QUERY_HEADS = 64
KEY_VALUE_HEADS = 8
HEAD_WIDTH = 128
GROUP = QUERY_HEADS // KEY_VALUE_HEADS
ROPE_BASE = 500000.0
SCORE_SCALE = 1.0 / float(np.sqrt(HEAD_WIDTH))
SCORE_TO_LOG2 = SCORE_SCALE * 1.4426950408889634
CHUNKS = 2
HEADS_PER_CHUNK = KEY_VALUE_HEADS // CHUNKS
CHUNK_COLS = HEADS_PER_CHUNK * HEAD_WIDTH
STEP_HEADS = 2
VMEM = pl.BlockSpec(memory_space=pltpu.VMEM)
SMEM = pl.BlockSpec(memory_space=pltpu.SMEM)


def inverse_freq_row():
    half = HEAD_WIDTH // 2
    place = lax.rem(lax.broadcasted_iota(jnp.int32, (8, HEAD_WIDTH), 1), half)
    row = jnp.ones((8, HEAD_WIDTH), jnp.float32)
    for i in range(1, half):
        row = jnp.where(place == i, np.float32(ROPE_BASE ** (-2.0 * i / HEAD_WIDTH)), row)
    return row[0:1]


def angle_tables(rows, padded, pos_ref):
    start = (lax.axis_index("seq") * lax.axis_size("head") + lax.axis_index("head")) * rows
    sublane = lax.broadcasted_iota(jnp.int32, (8, HEAD_WIDTH), 0)
    pieces = []
    for base in range(0, padded, 8):
        piece = jnp.zeros((8, HEAD_WIDTH), jnp.int32)
        for offset in range(min(8, rows - base)):
            piece = jnp.where(sublane == offset, pos_ref[start + (base + offset)], piece)
        pieces.append(piece)
    angle = jnp.concatenate(pieces, 0).astype(jnp.float32) * inverse_freq_row()
    lane = lax.broadcasted_iota(jnp.int32, angle.shape, 1)
    return jnp.cos(angle), jnp.sin(angle) * jnp.where(lane < HEAD_WIDTH // 2, -1.0, 1.0)


def rope(vectors, cosine, sine):
    return vectors * cosine + pltpu.roll(vectors, HEAD_WIDTH // 2, 1) * sine


def rope_back(vectors, cosine, sine):
    return vectors * cosine - pltpu.roll(vectors, HEAD_WIDTH // 2, 1) * sine


def head_cols(index):
    return slice(index * HEAD_WIDTH, (index + 1) * HEAD_WIDTH)


def prepare_keys(rows, pos_ref, key_ref, value_ref, kv_ref):
    cosine, sine = angle_tables(rows, key_ref.shape[0], pos_ref)
    for head in range(KEY_VALUE_HEADS):
        chunk, place = divmod(head, HEADS_PER_CHUNK)
        place += 2 * chunk * HEADS_PER_CHUNK
        rotated = rope(key_ref[:, head_cols(head)].astype(jnp.float32), cosine, sine)
        kv_ref[:, head_cols(place)] = rotated.astype(jnp.bfloat16)
        kv_ref[:, head_cols(HEADS_PER_CHUNK + place)] = value_ref[:, head_cols(head)]


def stack(chunk, *refs):
    *block_refs, stack_ref = refs
    for place, ref in enumerate(block_refs):
        stack_ref[place] = ref[:, 2 * chunk * CHUNK_COLS : 2 * (chunk + 1) * CHUNK_COLS]


def prepare_queries(rows, pos_ref, query_ref, grad_ref, *out_refs):
    q_ref, qt_ref, g_ref, gt_ref, cos_ref, sin_ref, cos_t_ref, sin_t_ref = out_refs

    @pl.when(pl.program_id(0) == 0)
    def _():
        cosine, sine = angle_tables(rows, query_ref.shape[0], pos_ref)
        cos_ref[...] = cosine
        sin_ref[...] = sine
        half = HEAD_WIDTH // 2
        cos_t_ref[...] = jnp.concatenate([cosine] * GROUP, 0).T[half:] * SCORE_SCALE
        sin_t_ref[...] = jnp.concatenate([sine] * GROUP, 0).T[half:] * SCORE_SCALE

    cosine, sine = cos_ref[...], sin_ref[...]
    queries = jnp.concatenate(
        [
            rope(query_ref[:, head_cols(h)].astype(jnp.float32), cosine, sine)
            for h in range(GROUP)
        ],
        0,
    )
    grads = jnp.concatenate(
        [grad_ref[:, head_cols(h)].astype(jnp.float32) for h in range(GROUP)], 0
    )
    q_ref[0] = queries.astype(jnp.bfloat16)
    qt_ref[0] = queries.T.astype(jnp.bfloat16)
    g_ref[0] = grads.astype(jnp.bfloat16)
    gt_ref[0] = grads.T.astype(jnp.bfloat16)


def dot(left, right):
    return jnp.dot(left, right, preferred_element_type=jnp.float32)


def attend(seq_count, head_count, rows, chunk, pieces, counts_ref, *refs):
    blocks = seq_count * head_count
    kv_refs = []
    for ref in refs[:pieces]:
        if len(ref.shape) == 2:
            kv_refs.append(ref.at[:, 2 * chunk * CHUNK_COLS : 2 * (chunk + 1) * CHUNK_COLS])
        else:
            kv_refs += [ref.at[i] for i in range(ref.shape[0])]
    q_ref, qt_ref, g_ref, gt_ref, cos_ref, sin_ref = refs[pieces : pieces + 6]
    outs = refs[pieces + 6 + 2 * int(chunk > 0) :]
    out_ref, grad_ref = outs[:2]
    part_refs = outs[2 : 2 + seq_count]
    bias_ref, live_ref = outs[2 + seq_count :]
    padded = kv_refs[0].shape[0]
    query_rows = GROUP * padded
    seq_index, head_index = lax.axis_index("seq"), lax.axis_index("head")
    my_rank = seq_index * head_count + head_index

    key_row = lax.broadcasted_iota(jnp.int32, (padded, query_rows), 0)
    query_row = lax.rem(lax.broadcasted_iota(jnp.int32, (padded, query_rows), 1), padded)
    for block in range(blocks):
        seq_offset, head_offset = divmod(block, head_count)
        seq_from = jnp.bitwise_xor(seq_index, seq_offset)
        head_from = jnp.bitwise_xor(head_index, head_offset)
        rank = seq_from * head_count + head_from
        limit = jnp.minimum(counts_ref[seq_from] - head_from * rows, rows)
        limit = jnp.where(rank <= my_rank, limit, 0)
        allowed = key_row < limit
        if block == 0:
            allowed = allowed & (key_row <= query_row)
            live_ref[...] = (query_row[:8] < limit).astype(jnp.float32)
        bias_ref[block * padded : (block + 1) * padded, :] = jnp.where(allowed, 0.0, -1e30)

    @pl.loop(0, HEADS_PER_CHUNK // STEP_HEADS)
    def _(step):
        first_head = chunk * HEADS_PER_CHUNK + step * STEP_HEADS

        def lanes(first, place):
            start = pl.multiple_of((first + step * STEP_HEADS + place) * HEAD_WIDTH, HEAD_WIDTH)
            return pl.ds(start, HEAD_WIDTH)

        def query_lanes(place, head):
            start = (step * STEP_HEADS + place) * GROUP * HEAD_WIDTH + head * HEAD_WIDTH
            start = pl.multiple_of(start, HEAD_WIDTH)
            return pl.ds(start, HEAD_WIDTH)

        def gathered(first, place):
            cols = lanes(first, place)
            wide = jnp.concatenate([ref[:, cols].astype(jnp.float32) for ref in kv_refs], 0)
            low = wide.astype(jnp.bfloat16)
            return low, low.T

        heads = range(STEP_HEADS)
        keys, values = [gathered(0, p) for p in heads], [gathered(HEADS_PER_CHUNK, p) for p in heads]
        bias, live = bias_ref[...], live_ref[0:1, :]
        scores = [dot(keys[p][0], qt_ref[first_head + p]) * SCORE_TO_LOG2 + bias for p in heads]
        dprobs, probs, probs_low = [], [], []
        for p in heads:
            weights = jnp.exp2(scores[p] - jnp.max(scores[p], 0, keepdims=True))
            probs.append(weights * (live / jnp.sum(weights, 0, keepdims=True)))
            probs_low.append(probs[p].astype(jnp.bfloat16))
            dprobs.append(dot(values[p][0], gt_ref[first_head + p]))
        outs_t, value_parts, dscores = [], [], []
        for p in heads:
            outs_t.append(dot(values[p][1], probs_low[p]))
            value_parts.append(dot(probs_low[p], g_ref[first_head + p]))
            out_low = outs_t[p].astype(jnp.bfloat16).astype(jnp.float32)
            delta = jnp.sum(gt_ref[first_head + p].astype(jnp.float32) * out_low, 0, keepdims=True)
            dscores.append((probs[p] * (dprobs[p] - delta)).astype(jnp.bfloat16))
        grads_t = [dot(keys[p][1], dscores[p]) for p in heads]
        key_parts = [dot(dscores[p], q_ref[first_head + p]) * SCORE_SCALE for p in heads]

        cosine, sine = cos_ref[...], sin_ref[...]
        half = HEAD_WIDTH // 2
        for p in heads:
            first, second = grads_t[p][:half], grads_t[p][half:]
            turned = [first * cosine + second * sine, second * cosine - first * sine]
            grad_low = jnp.concatenate(turned, 0).astype(jnp.bfloat16)
            out_heads = outs_t[p].astype(jnp.bfloat16).T.astype(jnp.float32)
            grad_heads = grad_low.T.astype(jnp.float32)
            for h in range(GROUP):
                piece, cols = slice(h * padded, (h + 1) * padded), query_lanes(p, h)
                out_ref[:, cols] = out_heads[piece].astype(jnp.bfloat16)
                grad_ref[:, cols] = grad_heads[piece].astype(jnp.bfloat16)
            for block in range(blocks):
                seq_offset, head_offset = divmod(block, head_count)
                piece = slice(block * padded, (block + 1) * padded)
                part_ref = part_refs[seq_offset]
                part_ref[head_offset, :, lanes(0, p)] = key_parts[p][piece].astype(jnp.bfloat16)
                part_ref[head_offset, :, lanes(HEADS_PER_CHUNK, p)] = value_parts[p][piece].astype(
                    jnp.bfloat16
                )


def combine(seq_count, head_count, *refs):
    part_refs, base_ref, send_refs = refs[:seq_count], refs[seq_count], refs[seq_count + 1 :]
    for offset in range(head_count):
        total = part_refs[0][offset].astype(jnp.float32)
        for ref in part_refs[1:]:
            total = total + ref[offset].astype(jnp.float32)
        if offset == 0:
            base_ref[...] = total
        else:
            send_refs[offset - 1][...] = total.astype(jnp.bfloat16)


def finish(head_count, *refs):
    cosine, sine = refs[0][...], refs[1][...]
    key_ref, value_ref = refs[-2:]
    for chunk in range(CHUNKS):
        mine = refs[2 + chunk * head_count : 2 + (chunk + 1) * head_count]
        for place in range(HEADS_PER_CHUNK):
            here, there = head_cols(place), head_cols(HEADS_PER_CHUNK + place)
            key_total, value_total = mine[0][:, here], mine[0][:, there]
            for ref in mine[1:]:
                key_total = key_total + ref[:, here].astype(jnp.float32)
                value_total = value_total + ref[:, there].astype(jnp.float32)
            cols = head_cols(chunk * HEADS_PER_CHUNK + place)
            key_ref[:, cols] = rope_back(key_total, cosine, sine).astype(jnp.bfloat16)
            value_ref[:, cols] = value_total.astype(jnp.bfloat16)


def params(mebibytes):
    return pltpu.CompilerParams(vmem_limit_bytes=mebibytes << 20)


def cost(microseconds):
    return pl.CostEstimate(
        flops=microseconds * 1153 * 10**6,
        bytes_accessed=microseconds * 3690 * 10**3,
        transcendentals=0,
    )


def shards(queries, routed_keys, routed_values, output_gradient, positions, counts):
    seq_count = lax.axis_size("seq")
    head_count = lax.axis_size("head")
    blocks = seq_count * head_count
    rows = queries.shape[0]
    padded = -(-rows // 8) * 8
    if padded != rows:
        extra = ((0, padded - rows), (0, 0))
        queries, routed_keys, routed_values, output_gradient = (
            jnp.pad(x, extra) for x in (queries, routed_keys, routed_values, output_gradient)
        )
    query_rows = GROUP * padded
    shape = jax.ShapeDtypeStruct
    bf16, f32 = jnp.bfloat16, jnp.float32
    ranks = [(s, z) for s in range(seq_count) for z in range(head_count)]

    def rank_of(s, z):
        return s * head_count + z

    def along_head(x, offset, upward, held=0):
        pairs = []
        for s, z in ranks:
            other = z ^ offset
            if s < seq_count - 1 or ((z ^ held) < other) == upward:
                pairs.append((rank_of(s, z), rank_of(s, other)))
        return lax.ppermute(x, ("seq", "head"), pairs)

    def along_seq(x, offset, upward):
        pairs = [
            (rank_of(s, z), rank_of(s ^ offset, z))
            for s, z in ranks
            if (s < (s ^ offset)) == upward
        ]
        return lax.ppermute(x, ("seq", "head"), pairs)

    table = shape((padded, HEAD_WIDTH), f32)
    table_t = shape((HEAD_WIDTH // 2, query_rows), f32)
    piece = shape((padded, 2 * CHUNK_COLS), bf16)
    own = pl.pallas_call(
        functools.partial(prepare_keys, rows),
        out_shape=shape((padded, CHUNKS * 2 * CHUNK_COLS), bf16),
        in_specs=[SMEM, VMEM, VMEM],
        out_specs=VMEM,
        compiler_params=params(56),
        name="prepare_keys",
    )(positions, routed_keys, routed_values)

    wide = GROUP * HEAD_WIDTH
    row_block = pl.BlockSpec((padded, wide), lambda g: (0, g))
    table_block = pl.BlockSpec((padded, HEAD_WIDTH), lambda g: (0, 0))
    tall_block = pl.BlockSpec((1, query_rows, HEAD_WIDTH), lambda g: (g, 0, 0))
    flat_block = pl.BlockSpec((1, HEAD_WIDTH, query_rows), lambda g: (g, 0, 0))
    tall = shape((KEY_VALUE_HEADS, query_rows, HEAD_WIDTH), bf16)
    flat = shape((KEY_VALUE_HEADS, HEAD_WIDTH, query_rows), bf16)
    table_t_block = pl.BlockSpec(table_t.shape, lambda g: (0, 0))
    *stacked, cosine, sine, cosine_t, sine_t = pl.pallas_call(
        functools.partial(prepare_queries, rows),
        grid=(KEY_VALUE_HEADS,),
        out_shape=[tall, flat, tall, flat, table, table, table_t, table_t],
        in_specs=[SMEM, row_block, row_block],
        out_specs=[tall_block, flat_block, tall_block, flat_block]
        + [table_block, table_block, table_t_block, table_t_block],
        cost_estimate=cost(7),
        compiler_params=params(16),
        name="prepare_queries",
    )(positions, queries, output_gradient)

    bits = [1 << b for b in reversed(range((head_count - 1).bit_length()))]
    later = range(1, seq_count)
    last = head_count - 1
    near = {0: own, **{j: along_head(own, j, True) for j in sorted({bits[0], 1}, reverse=True)}}
    far = {a: along_seq(own, a, True) for a in later}
    near, cosine_t, far = lax.optimization_barrier((near, cosine_t, far))
    for bit in bits[1:]:
        near.update(
            {j ^ bit: along_head(x, bit, True, j) for j, x in near.items() if j ^ bit not in near}
        )

    def cross(chunk, offsets):
        held = pl.pallas_call(
            functools.partial(stack, chunk),
            out_shape=shape((len(offsets), padded, 2 * CHUNK_COLS), bf16),
            in_specs=[VMEM] * len(offsets),
            out_specs=VMEM,
            compiler_params=params(8),
            name="stack",
        )(*(near[j] for j in offsets))
        return {a: along_seq(held, a, True) for a in later}

    crossed = [[cross(0, range(1, last)), cross(0, [last])]]
    near[last], crossed[0][0] = lax.optimization_barrier((near[last], crossed[0][0]))
    crossed += [[cross(chunk, range(1, head_count))] for chunk in range(1, CHUNKS)]

    wide_outs = ()
    parts = []
    for chunk in range(CHUNKS):
        has_alias = int(chunk > 0)
        gathered = [near[j] for j in range(head_count)]
        for a in later:
            gathered += [far[a]] + [part[a] for part in crossed[chunk]]
        inputs = len(gathered)
        out = pl.pallas_call(
            functools.partial(attend, seq_count, head_count, rows, chunk, inputs),
            out_shape=[shape((padded, QUERY_HEADS * HEAD_WIDTH), bf16)] * 2
            + [shape((head_count, padded, 2 * CHUNK_COLS), bf16)] * seq_count,
            in_specs=[SMEM]
            + [VMEM] * (inputs + 6)
            + [pl.BlockSpec(memory_space=pl.ANY)] * (2 * has_alias),
            out_specs=[pl.BlockSpec((padded, HEADS_PER_CHUNK * wide), lambda i, c=chunk: (0, c))] * 2
            + [VMEM] * seq_count,
            grid=(1,),
            scratch_shapes=[
                pltpu.VMEM((blocks * padded, query_rows), f32),
                pltpu.VMEM((8, query_rows), f32),
            ],
            input_output_aliases={inputs + 7: 0, inputs + 8: 1} if has_alias else {},
            cost_estimate=cost(10),
            compiler_params=params(32),
            name="attend",
        )(counts, *gathered, *stacked, cosine_t, sine_t, *wide_outs)
        wide_outs = out[:2]
        parts.append([out[2]] + [along_seq(out[2 + a], a, False) for a in later])

    summed = []
    for mine in parts:
        if summed:
            mine[-1], summed[-head_count] = lax.optimization_barrier(
                (mine[-1], summed[-head_count])
            )
        base, *sends = pl.pallas_call(
            functools.partial(combine, seq_count, head_count),
            out_shape=[shape((padded, 2 * CHUNK_COLS), f32)] + [piece] * (head_count - 1),
            in_specs=[VMEM] * seq_count,
            out_specs=[VMEM] * head_count,
            cost_estimate=cost(2),
            compiler_params=params(8),
            name="combine",
        )(*mine)
        summed += [base] + [along_head(x, j + 1, False) for j, x in enumerate(sends)]

    narrow = shape((padded, KEY_VALUE_HEADS * HEAD_WIDTH), bf16)
    key_grad, value_grad = pl.pallas_call(
        functools.partial(finish, head_count),
        out_shape=[narrow, narrow],
        in_specs=[VMEM] * (2 + CHUNKS * head_count),
        out_specs=[VMEM, VMEM],
        cost_estimate=cost(2),
        compiler_params=params(8),
        name="finish",
    )(cosine, sine, *summed)
    results = (*wide_outs, key_grad, value_grad)
    if padded != rows:
        results = tuple(x[:rows] for x in results)
    return results


def solution(mesh):
    rows = P(("dp", "seq", "head"), None)
    return jax.shard_map(
        shards,
        mesh=mesh,
        in_specs=(rows, rows, rows, rows, P("dp"), P("dp")),
        out_specs=(rows, rows, rows, rows),
        check_vma=False,
    )
```

```python
import functools

import jax
import jax.numpy as jnp
import numpy as np
from jax import lax
from jax.experimental import pallas as pl
from jax.experimental.pallas import tpu as pltpu
from jax.sharding import PartitionSpec as P

QUERY_HEADS = 64
KEY_VALUE_HEADS = 8
HEAD_WIDTH = 128
GROUP = QUERY_HEADS // KEY_VALUE_HEADS
ROPE_BASE = 500000.0
SCORE_SCALE = 1.0 / float(np.sqrt(HEAD_WIDTH))
SCORE_TO_LOG2 = SCORE_SCALE * 1.4426950408889634
CHUNKS = 2
HEADS_PER_CHUNK = KEY_VALUE_HEADS // CHUNKS
CHUNK_COLS = HEADS_PER_CHUNK * HEAD_WIDTH
STEP_HEADS = 2
VMEM = pl.BlockSpec(memory_space=pltpu.VMEM)
SMEM = pl.BlockSpec(memory_space=pltpu.SMEM)


def inverse_freq_row():
    half = HEAD_WIDTH // 2
    place = lax.rem(lax.broadcasted_iota(jnp.int32, (8, HEAD_WIDTH), 1), half)
    row = jnp.ones((8, HEAD_WIDTH), jnp.float32)
    for i in range(1, half):
        row = jnp.where(place == i, np.float32(ROPE_BASE ** (-2.0 * i / HEAD_WIDTH)), row)
    return row[0:1]


def angle_tables(rows, padded, pos_ref):
    start = (lax.axis_index("seq") * lax.axis_size("head") + lax.axis_index("head")) * rows
    sublane = lax.broadcasted_iota(jnp.int32, (8, HEAD_WIDTH), 0)
    pieces = []
    for base in range(0, padded, 8):
        piece = jnp.zeros((8, HEAD_WIDTH), jnp.int32)
        for offset in range(min(8, rows - base)):
            piece = jnp.where(sublane == offset, pos_ref[start + (base + offset)], piece)
        pieces.append(piece)
    angle = jnp.concatenate(pieces, 0).astype(jnp.float32) * inverse_freq_row()
    lane = lax.broadcasted_iota(jnp.int32, angle.shape, 1)
    return jnp.cos(angle), jnp.sin(angle) * jnp.where(lane < HEAD_WIDTH // 2, -1.0, 1.0)


def rope(vectors, cosine, sine):
    return vectors * cosine + pltpu.roll(vectors, HEAD_WIDTH // 2, 1) * sine


def rope_back(vectors, cosine, sine):
    return vectors * cosine - pltpu.roll(vectors, HEAD_WIDTH // 2, 1) * sine


def head_cols(index):
    return slice(index * HEAD_WIDTH, (index + 1) * HEAD_WIDTH)


def prepare_keys(rows, pos_ref, key_ref, value_ref, kv_ref):
    cosine, sine = angle_tables(rows, key_ref.shape[0], pos_ref)
    for head in range(KEY_VALUE_HEADS):
        chunk, place = divmod(head, HEADS_PER_CHUNK)
        place += 2 * chunk * HEADS_PER_CHUNK
        rotated = rope(key_ref[:, head_cols(head)].astype(jnp.float32), cosine, sine)
        kv_ref[:, head_cols(place)] = rotated.astype(jnp.bfloat16)
        kv_ref[:, head_cols(HEADS_PER_CHUNK + place)] = value_ref[:, head_cols(head)]


def stack(chunk, *refs):
    *block_refs, stack_ref = refs
    for place, ref in enumerate(block_refs):
        stack_ref[place] = ref[:, 2 * chunk * CHUNK_COLS : 2 * (chunk + 1) * CHUNK_COLS]


def prepare_queries(rows, pos_ref, query_ref, grad_ref, *out_refs):
    q_ref, qt_ref, g_ref, gt_ref, cos_ref, sin_ref, cos_t_ref, sin_t_ref = out_refs

    @pl.when(pl.program_id(0) == 0)
    def _():
        cosine, sine = angle_tables(rows, query_ref.shape[0], pos_ref)
        cos_ref[...] = cosine
        sin_ref[...] = sine
        half = HEAD_WIDTH // 2
        cos_t_ref[...] = jnp.concatenate([cosine] * GROUP, 0).T[half:] * SCORE_SCALE
        sin_t_ref[...] = jnp.concatenate([sine] * GROUP, 0).T[half:] * SCORE_SCALE

    cosine, sine = cos_ref[...], sin_ref[...]
    queries = jnp.concatenate(
        [
            rope(query_ref[:, head_cols(h)].astype(jnp.float32), cosine, sine)
            for h in range(GROUP)
        ],
        0,
    )
    grads = jnp.concatenate(
        [grad_ref[:, head_cols(h)].astype(jnp.float32) for h in range(GROUP)], 0
    )
    q_ref[0] = queries.astype(jnp.bfloat16)
    qt_ref[0] = queries.T.astype(jnp.bfloat16)
    g_ref[0] = grads.astype(jnp.bfloat16)
    gt_ref[0] = grads.T.astype(jnp.bfloat16)


def dot(left, right):
    return jnp.dot(left, right, preferred_element_type=jnp.float32)


def attend(seq_count, head_count, rows, pieces, has_alias, counts_ref, *refs):
    blocks = seq_count * head_count
    kv_refs = []
    for ref in refs[:pieces]:
        kv_refs += [ref] if len(ref.shape) == 2 else [ref.at[i] for i in range(ref.shape[0])]
    q_ref, qt_ref, g_ref, gt_ref, cos_ref, sin_ref = refs[pieces : pieces + 6]
    outs = refs[pieces + 6 + 2 * has_alias :]
    out_ref, grad_ref = outs[:2]
    part_refs = outs[2 : 2 + seq_count]
    bias_ref, live_ref = outs[2 + seq_count :]
    padded = kv_refs[0].shape[0]
    query_rows = GROUP * padded
    step = pl.program_id(0)
    seq_index, head_index = lax.axis_index("seq"), lax.axis_index("head")
    my_rank = seq_index * head_count + head_index

    @pl.when(step == 0)
    def _():
        key_row = lax.broadcasted_iota(jnp.int32, (padded, query_rows), 0)
        query_row = lax.rem(lax.broadcasted_iota(jnp.int32, (padded, query_rows), 1), padded)
        for block in range(blocks):
            seq_offset, head_offset = divmod(block, head_count)
            seq_from = jnp.bitwise_xor(seq_index, seq_offset)
            head_from = jnp.bitwise_xor(head_index, head_offset)
            rank = seq_from * head_count + head_from
            limit = jnp.minimum(counts_ref[seq_from] - head_from * rows, rows)
            limit = jnp.where(rank <= my_rank, limit, 0)
            allowed = key_row < limit
            if block == 0:
                allowed = allowed & (key_row <= query_row)
                live_ref[...] = (query_row[:8] < limit).astype(jnp.float32)
            bias_ref[block * padded : (block + 1) * padded, :] = jnp.where(allowed, 0.0, -1e30)

    def lanes(first, place):
        start = pl.multiple_of((first + step * STEP_HEADS + place) * HEAD_WIDTH, HEAD_WIDTH)
        return pl.ds(start, HEAD_WIDTH)

    def gathered(first, place):
        cols = lanes(first, place)
        wide = jnp.concatenate([ref[:, cols].astype(jnp.float32) for ref in kv_refs], 0)
        low = wide.astype(jnp.bfloat16)
        return low, low.T

    heads = range(STEP_HEADS)
    keys, values = [gathered(0, p) for p in heads], [gathered(HEADS_PER_CHUNK, p) for p in heads]
    bias, live = bias_ref[...], live_ref[0:1, :]
    scores = [dot(keys[p][0], qt_ref[p]) * SCORE_TO_LOG2 + bias for p in heads]
    probs_low = []
    for p in heads:
        weights = jnp.exp2(scores[p] - jnp.max(scores[p], 0, keepdims=True))
        factor = live / jnp.sum(weights, 0, keepdims=True)
        probs_low.append((weights * factor).astype(jnp.bfloat16))
    outs_t, value_parts, dscores = [], [], []
    for p in heads:
        outs_t.append(dot(values[p][1], probs_low[p]))
        value_parts.append(dot(probs_low[p], g_ref[p]))
        out_low = outs_t[p].astype(jnp.bfloat16).astype(jnp.float32)
        delta = jnp.sum(gt_ref[p].astype(jnp.float32) * out_low, 0, keepdims=True)
        dscores.append(probs_low[p] * (dot(values[p][0], gt_ref[p]) - delta).astype(jnp.bfloat16))
    grads_t = [dot(keys[p][1], dscores[p]) for p in heads]
    key_parts = [dot(dscores[p], q_ref[p]) * SCORE_SCALE for p in heads]

    cosine, sine = cos_ref[...], sin_ref[...]
    half = HEAD_WIDTH // 2
    for p in heads:
        first, second = grads_t[p][:half], grads_t[p][half:]
        turned = [first * cosine + second * sine, second * cosine - first * sine]
        grad_low = jnp.concatenate(turned, 0).astype(jnp.bfloat16)
        out_heads = outs_t[p].astype(jnp.bfloat16).T.astype(jnp.float32)
        grad_heads = grad_low.T.astype(jnp.float32)
        for h in range(GROUP):
            piece, cols = slice(h * padded, (h + 1) * padded), head_cols(p * GROUP + h)
            out_ref[:, cols] = out_heads[piece].astype(jnp.bfloat16)
            grad_ref[:, cols] = grad_heads[piece].astype(jnp.bfloat16)
        for block in range(blocks):
            seq_offset, head_offset = divmod(block, head_count)
            piece = slice(block * padded, (block + 1) * padded)
            part_ref = part_refs[seq_offset]
            part_ref[head_offset, :, lanes(0, p)] = key_parts[p][piece].astype(jnp.bfloat16)
            part_ref[head_offset, :, lanes(HEADS_PER_CHUNK, p)] = value_parts[p][piece].astype(
                jnp.bfloat16
            )


def combine(seq_count, head_count, *refs):
    part_refs, base_ref, send_refs = refs[:seq_count], refs[seq_count], refs[seq_count + 1 :]
    for offset in range(head_count):
        total = part_refs[0][offset].astype(jnp.float32)
        for ref in part_refs[1:]:
            total = total + ref[offset].astype(jnp.float32)
        if offset == 0:
            base_ref[...] = total
        else:
            send_refs[offset - 1][...] = total.astype(jnp.bfloat16)


def finish(head_count, *refs):
    cosine, sine = refs[0][...], refs[1][...]
    key_ref, value_ref = refs[-2:]
    for chunk in range(CHUNKS):
        mine = refs[2 + chunk * head_count : 2 + (chunk + 1) * head_count]
        for place in range(HEADS_PER_CHUNK):
            here, there = head_cols(place), head_cols(HEADS_PER_CHUNK + place)
            key_total, value_total = mine[0][:, here], mine[0][:, there]
            for ref in mine[1:]:
                key_total = key_total + ref[:, here].astype(jnp.float32)
                value_total = value_total + ref[:, there].astype(jnp.float32)
            cols = head_cols(chunk * HEADS_PER_CHUNK + place)
            key_ref[:, cols] = rope_back(key_total, cosine, sine).astype(jnp.bfloat16)
            value_ref[:, cols] = value_total.astype(jnp.bfloat16)


def params(mebibytes):
    return pltpu.CompilerParams(vmem_limit_bytes=mebibytes << 20)


def cost(microseconds):
    return pl.CostEstimate(
        flops=microseconds * 1153 * 10**6,
        bytes_accessed=microseconds * 3690 * 10**3,
        transcendentals=0,
    )


def shards(queries, routed_keys, routed_values, output_gradient, positions, counts):
    seq_count = lax.axis_size("seq")
    head_count = lax.axis_size("head")
    blocks = seq_count * head_count
    rows = queries.shape[0]
    padded = -(-rows // 8) * 8
    if padded != rows:
        extra = ((0, padded - rows), (0, 0))
        queries, routed_keys, routed_values, output_gradient = (
            jnp.pad(x, extra) for x in (queries, routed_keys, routed_values, output_gradient)
        )
    query_rows = GROUP * padded
    shape = jax.ShapeDtypeStruct
    bf16, f32 = jnp.bfloat16, jnp.float32
    ranks = [(s, z) for s in range(seq_count) for z in range(head_count)]

    def rank_of(s, z):
        return s * head_count + z

    def along_head(x, offset, upward, held=0):
        pairs = []
        for s, z in ranks:
            other = z ^ offset
            if s < seq_count - 1 or ((z ^ held) < other) == upward:
                pairs.append((rank_of(s, z), rank_of(s, other)))
        return lax.ppermute(x, ("seq", "head"), pairs)

    def along_seq(x, offset, upward):
        pairs = [
            (rank_of(s, z), rank_of(s ^ offset, z))
            for s, z in ranks
            if (s < (s ^ offset)) == upward
        ]
        return lax.ppermute(x, ("seq", "head"), pairs)

    table = shape((padded, HEAD_WIDTH), f32)
    table_t = shape((HEAD_WIDTH // 2, query_rows), f32)
    piece = shape((padded, 2 * CHUNK_COLS), bf16)
    own = pl.pallas_call(
        functools.partial(prepare_keys, rows),
        out_shape=shape((padded, CHUNKS * 2 * CHUNK_COLS), bf16),
        in_specs=[SMEM, VMEM, VMEM],
        out_specs=VMEM,
        compiler_params=params(56),
        name="prepare_keys",
    )(positions, routed_keys, routed_values)

    wide = GROUP * HEAD_WIDTH
    row_block = pl.BlockSpec((padded, wide), lambda g: (0, g))
    table_block = pl.BlockSpec((padded, HEAD_WIDTH), lambda g: (0, 0))
    tall_block = pl.BlockSpec((1, query_rows, HEAD_WIDTH), lambda g: (g, 0, 0))
    flat_block = pl.BlockSpec((1, HEAD_WIDTH, query_rows), lambda g: (g, 0, 0))
    tall = shape((KEY_VALUE_HEADS, query_rows, HEAD_WIDTH), bf16)
    flat = shape((KEY_VALUE_HEADS, HEAD_WIDTH, query_rows), bf16)
    table_t_block = pl.BlockSpec(table_t.shape, lambda g: (0, 0))
    *stacked, cosine, sine, cosine_t, sine_t = pl.pallas_call(
        functools.partial(prepare_queries, rows),
        grid=(KEY_VALUE_HEADS,),
        out_shape=[tall, flat, tall, flat, table, table, table_t, table_t],
        in_specs=[SMEM, row_block, row_block],
        out_specs=[tall_block, flat_block, tall_block, flat_block]
        + [table_block, table_block, table_t_block, table_t_block],
        cost_estimate=cost(7),
        compiler_params=params(16),
        name="prepare_queries",
    )(positions, queries, output_gradient)

    bits = [1 << b for b in reversed(range((head_count - 1).bit_length()))]
    later = range(1, seq_count)
    last = head_count - 1
    near = {0: own, **{j: along_head(own, j, True) for j in sorted({bits[0], 1}, reverse=True)}}
    far = {a: along_seq(own, a, True) for a in later}
    near, cosine_t, far = lax.optimization_barrier((near, cosine_t, far))
    for bit in bits[1:]:
        near.update(
            {j ^ bit: along_head(x, bit, True, j) for j, x in near.items() if j ^ bit not in near}
        )

    def cross(chunk, offsets):
        held = pl.pallas_call(
            functools.partial(stack, chunk),
            out_shape=shape((len(offsets), padded, 2 * CHUNK_COLS), bf16),
            in_specs=[VMEM] * len(offsets),
            out_specs=VMEM,
            compiler_params=params(8),
            name="stack",
        )(*(near[j] for j in offsets))
        return {a: along_seq(held, a, True) for a in later}

    crossed = [[cross(0, range(1, last)), cross(0, [last])]]
    near[last], crossed[0][0] = lax.optimization_barrier((near[last], crossed[0][0]))
    crossed += [[cross(chunk, range(1, head_count))] for chunk in range(1, CHUNKS)]

    wide_outs = ()
    parts = []
    for chunk in range(CHUNKS):
        first = chunk * HEADS_PER_CHUNK // STEP_HEADS
        has_alias = int(chunk > 0)
        tall_part, flat_part = (
            pl.BlockSpec((STEP_HEADS, *x.shape[1:]), lambda g, f=first: (f + g, 0, 0))
            for x in (tall, flat)
        )
        row_part = pl.BlockSpec((padded, STEP_HEADS * wide), lambda g, f=first: (0, f + g))
        gathered = [near[j] for j in range(head_count)]
        for a in later:
            gathered += [far[a]] + [part[a] for part in crossed[chunk]]
        inputs = len(gathered)
        kv_whole = pl.BlockSpec((padded, 2 * CHUNK_COLS), lambda g, c=chunk: (0, c))
        kv_specs = [
            kv_whole if len(x.shape) == 2 else pl.BlockSpec(x.shape, lambda g: (0, 0, 0))
            for x in gathered
        ]
        part_block = pl.BlockSpec((head_count, padded, 2 * CHUNK_COLS), lambda g: (0, 0, 0))
        out = pl.pallas_call(
            functools.partial(attend, seq_count, head_count, rows, inputs, has_alias),
            grid=(HEADS_PER_CHUNK // STEP_HEADS,),
            out_shape=[shape((padded, QUERY_HEADS * HEAD_WIDTH), bf16)] * 2
            + [shape((head_count, padded, 2 * CHUNK_COLS), bf16)] * seq_count,
            in_specs=[SMEM]
            + kv_specs
            + [tall_part, flat_part, tall_part, flat_part, table_t_block, table_t_block]
            + [pl.BlockSpec(memory_space=pl.ANY)] * (2 * has_alias),
            out_specs=[row_part, row_part] + [part_block] * seq_count,
            scratch_shapes=[
                pltpu.VMEM((blocks * padded, query_rows), f32),
                pltpu.VMEM((8, query_rows), f32),
            ],
            input_output_aliases={inputs + 7: 0, inputs + 8: 1} if has_alias else {},
            cost_estimate=cost(10),
            compiler_params=params(32),
            name="attend",
        )(counts, *gathered, *stacked, cosine_t, sine_t, *wide_outs)
        wide_outs = out[:2]
        parts.append([out[2]] + [along_seq(out[2 + a], a, False) for a in later])

    summed = []
    for mine in parts:
        if summed:
            mine[-1], summed[-head_count] = lax.optimization_barrier(
                (mine[-1], summed[-head_count])
            )
        base, *sends = pl.pallas_call(
            functools.partial(combine, seq_count, head_count),
            out_shape=[shape((padded, 2 * CHUNK_COLS), f32)] + [piece] * (head_count - 1),
            in_specs=[VMEM] * seq_count,
            out_specs=[VMEM] * head_count,
            cost_estimate=cost(2),
            compiler_params=params(8),
            name="combine",
        )(*mine)
        summed += [base] + [along_head(x, j + 1, False) for j, x in enumerate(sends)]

    narrow = shape((padded, KEY_VALUE_HEADS * HEAD_WIDTH), bf16)
    key_grad, value_grad = pl.pallas_call(
        functools.partial(finish, head_count),
        out_shape=[narrow, narrow],
        in_specs=[VMEM] * (2 + CHUNKS * head_count),
        out_specs=[VMEM, VMEM],
        cost_estimate=cost(2),
        compiler_params=params(8),
        name="finish",
    )(cosine, sine, *summed)
    results = (*wide_outs, key_grad, value_grad)
    if padded != rows:
        results = tuple(x[:rows] for x in results)
    return results


def solution(mesh):
    rows = P(("dp", "seq", "head"), None)
    return jax.shard_map(
        shards,
        mesh=mesh,
        in_specs=(rows, rows, rows, rows, P("dp"), P("dp")),
        out_specs=(rows, rows, rows, rows),
        check_vma=False,
    )
```

```python
import functools

import jax
import jax.numpy as jnp
import numpy as np
from jax import lax
from jax.experimental import pallas as pl
from jax.experimental.pallas import tpu as pltpu
from jax.sharding import PartitionSpec as P

QUERY_HEADS = 64
KEY_VALUE_HEADS = 8
HEAD_WIDTH = 128
GROUP = QUERY_HEADS // KEY_VALUE_HEADS
ROPE_BASE = 500000.0
SCORE_SCALE = 1.0 / float(np.sqrt(HEAD_WIDTH))
SCORE_TO_LOG2 = SCORE_SCALE * 1.4426950408889634
CHUNKS = 2
HEADS_PER_CHUNK = KEY_VALUE_HEADS // CHUNKS
CHUNK_COLS = HEADS_PER_CHUNK * HEAD_WIDTH
STEP_HEADS = 2
VMEM = pl.BlockSpec(memory_space=pltpu.VMEM)
SMEM = pl.BlockSpec(memory_space=pltpu.SMEM)


def inverse_freq_row():
    half = HEAD_WIDTH // 2
    place = lax.rem(lax.broadcasted_iota(jnp.int32, (8, HEAD_WIDTH), 1), half)
    row = jnp.ones((8, HEAD_WIDTH), jnp.float32)
    for i in range(1, half):
        row = jnp.where(place == i, np.float32(ROPE_BASE ** (-2.0 * i / HEAD_WIDTH)), row)
    return row[0:1]


def angle_tables(rows, padded, pos_ref):
    start = (lax.axis_index("seq") * lax.axis_size("head") + lax.axis_index("head")) * rows
    sublane = lax.broadcasted_iota(jnp.int32, (8, HEAD_WIDTH), 0)
    pieces = []
    for base in range(0, padded, 8):
        piece = jnp.zeros((8, HEAD_WIDTH), jnp.int32)
        for offset in range(min(8, rows - base)):
            piece = jnp.where(sublane == offset, pos_ref[start + (base + offset)], piece)
        pieces.append(piece)
    angle = jnp.concatenate(pieces, 0).astype(jnp.float32) * inverse_freq_row()
    lane = lax.broadcasted_iota(jnp.int32, angle.shape, 1)
    return jnp.cos(angle), jnp.sin(angle) * jnp.where(lane < HEAD_WIDTH // 2, -1.0, 1.0)


def rope(vectors, cosine, sine):
    return vectors * cosine + pltpu.roll(vectors, HEAD_WIDTH // 2, 1) * sine


def rope_back(vectors, cosine, sine):
    return vectors * cosine - pltpu.roll(vectors, HEAD_WIDTH // 2, 1) * sine


def head_cols(index):
    return slice(index * HEAD_WIDTH, (index + 1) * HEAD_WIDTH)


def prepare_keys(rows, pos_ref, key_ref, value_ref, kv_ref):
    cosine, sine = angle_tables(rows, key_ref.shape[0], pos_ref)
    for head in range(KEY_VALUE_HEADS):
        chunk, place = divmod(head, HEADS_PER_CHUNK)
        place += 2 * chunk * HEADS_PER_CHUNK
        rotated = rope(key_ref[:, head_cols(head)].astype(jnp.float32), cosine, sine)
        kv_ref[:, head_cols(place)] = rotated.astype(jnp.bfloat16)
        kv_ref[:, head_cols(HEADS_PER_CHUNK + place)] = value_ref[:, head_cols(head)]


def stack(chunk, *refs):
    *block_refs, stack_ref = refs
    for place, ref in enumerate(block_refs):
        stack_ref[place] = ref[:, 2 * chunk * CHUNK_COLS : 2 * (chunk + 1) * CHUNK_COLS]


def prepare_queries(rows, pos_ref, query_ref, grad_ref, *out_refs):
    q_ref, qt_ref, g_ref, gt_ref, cos_ref, sin_ref, cos_t_ref, sin_t_ref = out_refs

    @pl.when(pl.program_id(0) == 0)
    def _():
        cosine, sine = angle_tables(rows, query_ref.shape[0], pos_ref)
        cos_ref[...] = cosine
        sin_ref[...] = sine
        half = HEAD_WIDTH // 2
        cos_t_ref[...] = jnp.concatenate([cosine] * GROUP, 0).T[half:] * SCORE_SCALE
        sin_t_ref[...] = jnp.concatenate([sine] * GROUP, 0).T[half:] * SCORE_SCALE

    cosine, sine = cos_ref[...], sin_ref[...]
    queries = jnp.concatenate(
        [
            rope(query_ref[:, head_cols(h)].astype(jnp.float32), cosine, sine)
            for h in range(GROUP)
        ],
        0,
    )
    grads = jnp.concatenate(
        [grad_ref[:, head_cols(h)].astype(jnp.float32) for h in range(GROUP)], 0
    )
    q_ref[0] = queries.astype(jnp.bfloat16)
    qt_ref[0] = queries.T.astype(jnp.bfloat16)
    g_ref[0] = grads.astype(jnp.bfloat16)
    gt_ref[0] = grads.T.astype(jnp.bfloat16)


def dot(left, right):
    return jnp.dot(left, right, preferred_element_type=jnp.float32)


def attend(seq_count, head_count, rows, pieces, has_alias, counts_ref, *refs):
    blocks = seq_count * head_count
    kv_refs = []
    for ref in refs[:pieces]:
        kv_refs += [ref] if len(ref.shape) == 2 else [ref.at[i] for i in range(ref.shape[0])]
    q_ref, qt_ref, g_ref, gt_ref, cos_ref, sin_ref = refs[pieces : pieces + 6]
    outs = refs[pieces + 6 + 2 * has_alias :]
    out_ref, grad_ref = outs[:2]
    part_refs = outs[2 : 2 + seq_count]
    bias_ref, live_ref = outs[2 + seq_count :]
    padded = kv_refs[0].shape[0]
    query_rows = GROUP * padded
    step = pl.program_id(0)
    seq_index, head_index = lax.axis_index("seq"), lax.axis_index("head")
    my_rank = seq_index * head_count + head_index

    @pl.when(step == 0)
    def _():
        key_row = lax.broadcasted_iota(jnp.int32, (padded, query_rows), 0)
        query_row = lax.rem(lax.broadcasted_iota(jnp.int32, (padded, query_rows), 1), padded)
        for block in range(blocks):
            seq_offset, head_offset = divmod(block, head_count)
            seq_from = jnp.bitwise_xor(seq_index, seq_offset)
            head_from = jnp.bitwise_xor(head_index, head_offset)
            rank = seq_from * head_count + head_from
            limit = jnp.minimum(counts_ref[seq_from] - head_from * rows, rows)
            limit = jnp.where(rank <= my_rank, limit, 0)
            allowed = key_row < limit
            if block == 0:
                allowed = allowed & (key_row <= query_row)
                live_ref[...] = (query_row[:8] < limit).astype(jnp.float32)
            bias_ref[block * padded : (block + 1) * padded, :] = jnp.where(allowed, 0.0, -1e30)

    def lanes(first, place):
        start = pl.multiple_of((first + step * STEP_HEADS + place) * HEAD_WIDTH, HEAD_WIDTH)
        return pl.ds(start, HEAD_WIDTH)

    def gathered(first, place):
        cols = lanes(first, place)
        wide = jnp.concatenate([ref[:, cols].astype(jnp.float32) for ref in kv_refs], 0)
        low = wide.astype(jnp.bfloat16)
        return low, low.T

    heads = range(STEP_HEADS)
    keys, values = [gathered(0, p) for p in heads], [gathered(HEADS_PER_CHUNK, p) for p in heads]
    bias, live = bias_ref[...], live_ref[0:1, :]
    scores = [dot(keys[p][0], qt_ref[p]) * SCORE_TO_LOG2 + bias for p in heads]
    probs_low = []
    for p in heads:
        weights = jnp.exp2(scores[p] - jnp.max(scores[p], 0, keepdims=True))
        factor = live / jnp.sum(weights, 0, keepdims=True)
        probs_low.append((weights * factor).astype(jnp.bfloat16))
    outs_t, value_parts, dscores = [], [], []
    for p in heads:
        outs_t.append(dot(values[p][1], probs_low[p]))
        value_parts.append(dot(probs_low[p], g_ref[p]))
        out_low = outs_t[p].astype(jnp.bfloat16).astype(jnp.float32)
        delta = jnp.sum(gt_ref[p].astype(jnp.float32) * out_low, 0, keepdims=True)
        dscores.append(probs_low[p] * (dot(values[p][0], gt_ref[p]) - delta).astype(jnp.bfloat16))
    grads_t = [dot(keys[p][1], dscores[p]) for p in heads]
    key_parts = [dot(dscores[p], q_ref[p]) * SCORE_SCALE for p in heads]

    cosine, sine = cos_ref[...], sin_ref[...]
    half = HEAD_WIDTH // 2
    for p in heads:
        first, second = grads_t[p][:half], grads_t[p][half:]
        turned = [first * cosine + second * sine, second * cosine - first * sine]
        grad_low = jnp.concatenate(turned, 0).astype(jnp.bfloat16)
        out_heads = outs_t[p].astype(jnp.bfloat16).T.astype(jnp.float32)
        grad_heads = grad_low.T.astype(jnp.float32)
        for h in range(GROUP):
            piece, cols = slice(h * padded, (h + 1) * padded), head_cols(p * GROUP + h)
            out_ref[:, cols] = out_heads[piece].astype(jnp.bfloat16)
            grad_ref[:, cols] = grad_heads[piece].astype(jnp.bfloat16)
        for block in range(blocks):
            seq_offset, head_offset = divmod(block, head_count)
            piece = slice(block * padded, (block + 1) * padded)
            part_ref = part_refs[seq_offset]
            part_ref[head_offset, :, lanes(0, p)] = key_parts[p][piece].astype(jnp.bfloat16)
            part_ref[head_offset, :, lanes(HEADS_PER_CHUNK, p)] = value_parts[p][piece].astype(
                jnp.bfloat16
            )


def combine(seq_count, head_count, *refs):
    part_refs, base_ref, send_refs = refs[:seq_count], refs[seq_count], refs[seq_count + 1 :]
    for offset in range(head_count):
        total = part_refs[0][offset].astype(jnp.float32)
        for ref in part_refs[1:]:
            total = total + ref[offset].astype(jnp.float32)
        if offset == 0:
            base_ref[...] = total
        else:
            send_refs[offset - 1][...] = total.astype(jnp.bfloat16)


def finish(head_count, *refs):
    cosine, sine = refs[0][...], refs[1][...]
    key_ref, value_ref = refs[-2:]
    for chunk in range(CHUNKS):
        mine = refs[2 + chunk * head_count : 2 + (chunk + 1) * head_count]
        for place in range(HEADS_PER_CHUNK):
            here, there = head_cols(place), head_cols(HEADS_PER_CHUNK + place)
            key_total, value_total = mine[0][:, here], mine[0][:, there]
            for ref in mine[1:]:
                key_total = key_total + ref[:, here].astype(jnp.float32)
                value_total = value_total + ref[:, there].astype(jnp.float32)
            cols = head_cols(chunk * HEADS_PER_CHUNK + place)
            key_ref[:, cols] = rope_back(key_total, cosine, sine).astype(jnp.bfloat16)
            value_ref[:, cols] = value_total.astype(jnp.bfloat16)


def params(mebibytes):
    return pltpu.CompilerParams(vmem_limit_bytes=mebibytes << 20)


def cost(microseconds):
    return pl.CostEstimate(
        flops=microseconds * 1153 * 10**6,
        bytes_accessed=microseconds * 3690 * 10**3,
        transcendentals=0,
    )


def shards(queries, routed_keys, routed_values, output_gradient, positions, counts):
    seq_count = lax.axis_size("seq")
    head_count = lax.axis_size("head")
    blocks = seq_count * head_count
    rows = queries.shape[0]
    padded = -(-rows // 8) * 8
    if padded != rows:
        extra = ((0, padded - rows), (0, 0))
        queries, routed_keys, routed_values, output_gradient = (
            jnp.pad(x, extra) for x in (queries, routed_keys, routed_values, output_gradient)
        )
    query_rows = GROUP * padded
    shape = jax.ShapeDtypeStruct
    bf16, f32 = jnp.bfloat16, jnp.float32
    ranks = [(s, z) for s in range(seq_count) for z in range(head_count)]

    def rank_of(s, z):
        return s * head_count + z

    def along_head(x, offset, upward, held=0):
        pairs = []
        for s, z in ranks:
            other = z ^ offset
            if s < seq_count - 1 or ((z ^ held) < other) == upward:
                pairs.append((rank_of(s, z), rank_of(s, other)))
        return lax.ppermute(x, ("seq", "head"), pairs)

    def along_seq(x, offset, upward):
        pairs = [
            (rank_of(s, z), rank_of(s ^ offset, z))
            for s, z in ranks
            if (s < (s ^ offset)) == upward
        ]
        return lax.ppermute(x, ("seq", "head"), pairs)

    table = shape((padded, HEAD_WIDTH), f32)
    table_t = shape((HEAD_WIDTH // 2, query_rows), f32)
    piece = shape((padded, 2 * CHUNK_COLS), bf16)
    own = pl.pallas_call(
        functools.partial(prepare_keys, rows),
        out_shape=shape((padded, CHUNKS * 2 * CHUNK_COLS), bf16),
        in_specs=[SMEM, VMEM, VMEM],
        out_specs=VMEM,
        compiler_params=params(56),
        name="prepare_keys",
    )(positions, routed_keys, routed_values)

    wide = GROUP * HEAD_WIDTH
    row_block = pl.BlockSpec((padded, wide), lambda g: (0, g))
    table_block = pl.BlockSpec((padded, HEAD_WIDTH), lambda g: (0, 0))
    tall_block = pl.BlockSpec((1, query_rows, HEAD_WIDTH), lambda g: (g, 0, 0))
    flat_block = pl.BlockSpec((1, HEAD_WIDTH, query_rows), lambda g: (g, 0, 0))
    tall = shape((KEY_VALUE_HEADS, query_rows, HEAD_WIDTH), bf16)
    flat = shape((KEY_VALUE_HEADS, HEAD_WIDTH, query_rows), bf16)
    table_t_block = pl.BlockSpec(table_t.shape, lambda g: (0, 0))
    *stacked, cosine, sine, cosine_t, sine_t = pl.pallas_call(
        functools.partial(prepare_queries, rows),
        grid=(KEY_VALUE_HEADS,),
        out_shape=[tall, flat, tall, flat, table, table, table_t, table_t],
        in_specs=[SMEM, row_block, row_block],
        out_specs=[tall_block, flat_block, tall_block, flat_block]
        + [table_block, table_block, table_t_block, table_t_block],
        cost_estimate=cost(7),
        compiler_params=params(16),
        name="prepare_queries",
    )(positions, queries, output_gradient)

    bits = [1 << b for b in reversed(range((head_count - 1).bit_length()))]
    later = range(1, seq_count)
    last = head_count - 1
    near = {0: own, **{j: along_head(own, j, True) for j in sorted({bits[0], 1}, reverse=True)}}
    far = {a: along_seq(own, a, True) for a in later}
    near, cosine_t, far = lax.optimization_barrier((near, cosine_t, far))
    for bit in bits[1:]:
        near.update(
            {j ^ bit: along_head(x, bit, True, j) for j, x in near.items() if j ^ bit not in near}
        )

    def cross(chunk, offsets):
        held = pl.pallas_call(
            functools.partial(stack, chunk),
            out_shape=shape((len(offsets), padded, 2 * CHUNK_COLS), bf16),
            in_specs=[VMEM] * len(offsets),
            out_specs=VMEM,
            compiler_params=params(8),
            name="stack",
        )(*(near[j] for j in offsets))
        return {a: along_seq(held, a, True) for a in later}

    crossed = [[cross(0, range(1, last)), cross(0, [last])]]
    near[last], crossed[0][0] = lax.optimization_barrier((near[last], crossed[0][0]))
    crossed += [[cross(chunk, range(1, head_count))] for chunk in range(1, CHUNKS)]

    wide_outs = ()
    parts = []
    for chunk in range(CHUNKS):
        first = chunk * HEADS_PER_CHUNK // STEP_HEADS
        has_alias = int(chunk > 0)
        tall_part, flat_part = (
            pl.BlockSpec((STEP_HEADS, *x.shape[1:]), lambda g, f=first: (f + g, 0, 0))
            for x in (tall, flat)
        )
        row_part = pl.BlockSpec((padded, STEP_HEADS * wide), lambda g, f=first: (0, f + g))
        gathered = [near[j] for j in range(head_count)]
        for a in later:
            gathered += [far[a]] + [part[a] for part in crossed[chunk]]
        inputs = len(gathered)
        kv_whole = pl.BlockSpec((padded, 2 * CHUNK_COLS), lambda g, c=chunk: (0, c))
        kv_specs = [
            kv_whole if len(x.shape) == 2 else pl.BlockSpec(x.shape, lambda g: (0, 0, 0))
            for x in gathered
        ]
        part_block = pl.BlockSpec((head_count, padded, 2 * CHUNK_COLS), lambda g: (0, 0, 0))
        out = pl.pallas_call(
            functools.partial(attend, seq_count, head_count, rows, inputs, has_alias),
            grid=(HEADS_PER_CHUNK // STEP_HEADS,),
            out_shape=[shape((padded, QUERY_HEADS * HEAD_WIDTH), bf16)] * 2
            + [shape((head_count, padded, 2 * CHUNK_COLS), bf16)] * seq_count,
            in_specs=[SMEM]
            + kv_specs
            + [tall_part, flat_part, tall_part, flat_part, table_t_block, table_t_block]
            + [pl.BlockSpec(memory_space=pl.ANY)] * (2 * has_alias),
            out_specs=[row_part, row_part] + [part_block] * seq_count,
            scratch_shapes=[
                pltpu.VMEM((blocks * padded, query_rows), f32),
                pltpu.VMEM((8, query_rows), f32),
            ],
            input_output_aliases={inputs + 7: 0, inputs + 8: 1} if has_alias else {},
            cost_estimate=cost(10),
            compiler_params=params(32),
            name="attend",
        )(counts, *gathered, *stacked, cosine_t, sine_t, *wide_outs)
        wide_outs = out[:2]
        parts.append([out[2]] + [along_seq(out[2 + a], a, False) for a in later])

    summed = []
    for mine in parts:
        if summed:
            mine[-1], summed[-head_count] = lax.optimization_barrier(
                (mine[-1], summed[-head_count])
            )
        base, *sends = pl.pallas_call(
            functools.partial(combine, seq_count, head_count),
            out_shape=[shape((padded, 2 * CHUNK_COLS), f32)] + [piece] * (head_count - 1),
            in_specs=[VMEM] * seq_count,
            out_specs=[VMEM] * head_count,
            cost_estimate=cost(2),
            compiler_params=params(8),
            name="combine",
        )(*mine)
        order = [*enumerate(sends, 1)]
        if mine is parts[-1]:
            order.reverse()
        summed += [base] + [along_head(x, j, False) for j, x in order]

    narrow = shape((padded, KEY_VALUE_HEADS * HEAD_WIDTH), bf16)
    key_grad, value_grad = pl.pallas_call(
        functools.partial(finish, head_count),
        out_shape=[narrow, narrow],
        in_specs=[VMEM] * (2 + CHUNKS * head_count),
        out_specs=[VMEM, VMEM],
        cost_estimate=cost(2),
        compiler_params=params(8),
        name="finish",
    )(cosine, sine, *summed)
    results = (*wide_outs, key_grad, value_grad)
    if padded != rows:
        results = tuple(x[:rows] for x in results)
    return results


def solution(mesh):
    rows = P(("dp", "seq", "head"), None)
    return jax.shard_map(
        shards,
        mesh=mesh,
        in_specs=(rows, rows, rows, rows, P("dp"), P("dp")),
        out_specs=(rows, rows, rows, rows),
        check_vma=False,
    )
```

```python
import functools

import jax
import jax.numpy as jnp
import numpy as np
from jax import lax
from jax.experimental import pallas as pl
from jax.experimental.pallas import tpu as pltpu
from jax.sharding import PartitionSpec as P

QUERY_HEADS = 64
KEY_VALUE_HEADS = 8
HEAD_WIDTH = 128
GROUP = QUERY_HEADS // KEY_VALUE_HEADS
ROPE_BASE = 500000.0
SCORE_SCALE = 1.0 / float(np.sqrt(HEAD_WIDTH))
SCORE_TO_LOG2 = SCORE_SCALE * 1.4426950408889634
CHUNKS = 2
HEADS_PER_CHUNK = KEY_VALUE_HEADS // CHUNKS
CHUNK_COLS = HEADS_PER_CHUNK * HEAD_WIDTH
STEP_HEADS = 2
VMEM = pl.BlockSpec(memory_space=pltpu.VMEM)
SMEM = pl.BlockSpec(memory_space=pltpu.SMEM)


def inverse_freq_row():
    half = HEAD_WIDTH // 2
    place = lax.rem(lax.broadcasted_iota(jnp.int32, (8, HEAD_WIDTH), 1), half)
    row = jnp.ones((8, HEAD_WIDTH), jnp.float32)
    for i in range(1, half):
        row = jnp.where(place == i, np.float32(ROPE_BASE ** (-2.0 * i / HEAD_WIDTH)), row)
    return row[0:1]


def angle_tables(rows, padded, pos_ref):
    start = (lax.axis_index("seq") * lax.axis_size("head") + lax.axis_index("head")) * rows
    sublane = lax.broadcasted_iota(jnp.int32, (8, HEAD_WIDTH), 0)
    pieces = []
    for base in range(0, padded, 8):
        piece = jnp.zeros((8, HEAD_WIDTH), jnp.int32)
        for offset in range(min(8, rows - base)):
            piece = jnp.where(sublane == offset, pos_ref[start + (base + offset)], piece)
        pieces.append(piece)
    angle = jnp.concatenate(pieces, 0).astype(jnp.float32) * inverse_freq_row()
    lane = lax.broadcasted_iota(jnp.int32, angle.shape, 1)
    return jnp.cos(angle), jnp.sin(angle) * jnp.where(lane < HEAD_WIDTH // 2, -1.0, 1.0)


def rope(vectors, cosine, sine):
    return vectors * cosine + pltpu.roll(vectors, HEAD_WIDTH // 2, 1) * sine


def rope_back(vectors, cosine, sine):
    return vectors * cosine - pltpu.roll(vectors, HEAD_WIDTH // 2, 1) * sine


def head_cols(index):
    return slice(index * HEAD_WIDTH, (index + 1) * HEAD_WIDTH)


def prepare_keys(rows, pos_ref, key_ref, value_ref, kv_ref):
    cosine, sine = angle_tables(rows, key_ref.shape[0], pos_ref)
    for head in range(KEY_VALUE_HEADS):
        chunk, place = divmod(head, HEADS_PER_CHUNK)
        place += 2 * chunk * HEADS_PER_CHUNK
        rotated = rope(key_ref[:, head_cols(head)].astype(jnp.float32), cosine, sine)
        kv_ref[:, head_cols(place)] = rotated.astype(jnp.bfloat16)
        kv_ref[:, head_cols(HEADS_PER_CHUNK + place)] = value_ref[:, head_cols(head)]


def stack(chunk, *refs):
    *block_refs, stack_ref = refs
    for place, ref in enumerate(block_refs):
        stack_ref[place] = ref[:, 2 * chunk * CHUNK_COLS : 2 * (chunk + 1) * CHUNK_COLS]


def prepare_queries(rows, pos_ref, query_ref, grad_ref, *out_refs):
    q_ref, qt_ref, g_ref, gt_ref, cos_ref, sin_ref, cos_t_ref, sin_t_ref = out_refs

    @pl.when(pl.program_id(0) == 0)
    def _():
        cosine, sine = angle_tables(rows, query_ref.shape[0], pos_ref)
        cos_ref[...] = cosine
        sin_ref[...] = sine
        half = HEAD_WIDTH // 2
        cos_t_ref[...] = jnp.concatenate([cosine] * GROUP, 0).T[half:] * SCORE_SCALE
        sin_t_ref[...] = jnp.concatenate([sine] * GROUP, 0).T[half:] * SCORE_SCALE

    cosine, sine = cos_ref[...], sin_ref[...]
    queries = jnp.concatenate(
        [
            rope(query_ref[:, head_cols(h)].astype(jnp.float32), cosine, sine)
            for h in range(GROUP)
        ],
        0,
    )
    grads = jnp.concatenate(
        [grad_ref[:, head_cols(h)].astype(jnp.float32) for h in range(GROUP)], 0
    )
    q_ref[0] = queries.astype(jnp.bfloat16)
    qt_ref[0] = queries.T.astype(jnp.bfloat16)
    g_ref[0] = grads.astype(jnp.bfloat16)
    gt_ref[0] = grads.T.astype(jnp.bfloat16)


def dot(left, right):
    return jnp.dot(left, right, preferred_element_type=jnp.float32)


def attend(seq_count, head_count, rows, pieces, has_alias, counts_ref, *refs):
    blocks = seq_count * head_count
    kv_refs = []
    for ref in refs[:pieces]:
        kv_refs += [ref] if len(ref.shape) == 2 else [ref.at[i] for i in range(ref.shape[0])]
    q_ref, qt_ref, g_ref, gt_ref, cos_ref, sin_ref = refs[pieces : pieces + 6]
    outs = refs[pieces + 6 + 2 * has_alias :]
    out_ref, grad_ref = outs[:2]
    part_refs = outs[2 : 2 + seq_count]
    bias_ref, live_ref = outs[2 + seq_count :]
    padded = kv_refs[0].shape[0]
    query_rows = GROUP * padded
    step = pl.program_id(0)
    seq_index, head_index = lax.axis_index("seq"), lax.axis_index("head")
    my_rank = seq_index * head_count + head_index

    @pl.when(step == 0)
    def _():
        key_row = lax.broadcasted_iota(jnp.int32, (padded, query_rows), 0)
        query_row = lax.rem(lax.broadcasted_iota(jnp.int32, (padded, query_rows), 1), padded)
        for block in range(blocks):
            seq_offset, head_offset = divmod(block, head_count)
            seq_from = jnp.bitwise_xor(seq_index, seq_offset)
            head_from = jnp.bitwise_xor(head_index, head_offset)
            rank = seq_from * head_count + head_from
            limit = jnp.minimum(counts_ref[seq_from] - head_from * rows, rows)
            limit = jnp.where(rank <= my_rank, limit, 0)
            allowed = key_row < limit
            if block == 0:
                allowed = allowed & (key_row <= query_row)
                live_ref[...] = (query_row[:8] < limit).astype(jnp.float32)
            bias_ref[block * padded : (block + 1) * padded, :] = jnp.where(allowed, 0.0, -1e30)

    def lanes(first, place):
        start = pl.multiple_of((first + step * STEP_HEADS + place) * HEAD_WIDTH, HEAD_WIDTH)
        return pl.ds(start, HEAD_WIDTH)

    def gathered(first, place):
        cols = lanes(first, place)
        wide = jnp.concatenate([ref[:, cols].astype(jnp.float32) for ref in kv_refs], 0)
        low = wide.astype(jnp.bfloat16)
        return low, low.T

    heads = range(STEP_HEADS)
    keys, values = [gathered(0, p) for p in heads], [gathered(HEADS_PER_CHUNK, p) for p in heads]
    bias, live = bias_ref[...], live_ref[0:1, :]
    scores = [dot(keys[p][0], qt_ref[p]) * SCORE_TO_LOG2 + bias for p in heads]
    probs_low = []
    for p in heads:
        weights = jnp.exp2(scores[p] - jnp.max(scores[p], 0, keepdims=True))
        factor = live / jnp.sum(weights, 0, keepdims=True)
        probs_low.append((weights * factor).astype(jnp.bfloat16))
    outs_t, value_parts, dscores = [], [], []
    for p in heads:
        outs_t.append(dot(values[p][1], probs_low[p]))
        value_parts.append(dot(probs_low[p], g_ref[p]))
        out_low = outs_t[p].astype(jnp.bfloat16).astype(jnp.float32)
        delta = jnp.sum(gt_ref[p].astype(jnp.float32) * out_low, 0, keepdims=True)
        dscores.append(probs_low[p] * (dot(values[p][0], gt_ref[p]) - delta).astype(jnp.bfloat16))
    grads_t = [dot(keys[p][1], dscores[p]) for p in heads]
    key_parts = [dot(dscores[p], q_ref[p]) * SCORE_SCALE for p in heads]

    cosine, sine = cos_ref[...], sin_ref[...]
    half = HEAD_WIDTH // 2
    for p in heads:
        first, second = grads_t[p][:half], grads_t[p][half:]
        turned = [first * cosine + second * sine, second * cosine - first * sine]
        grad_low = jnp.concatenate(turned, 0).astype(jnp.bfloat16)
        out_heads = outs_t[p].astype(jnp.bfloat16).T.astype(jnp.float32)
        grad_heads = grad_low.T.astype(jnp.float32)
        for h in range(GROUP):
            piece, cols = slice(h * padded, (h + 1) * padded), head_cols(p * GROUP + h)
            out_ref[:, cols] = out_heads[piece].astype(jnp.bfloat16)
            grad_ref[:, cols] = grad_heads[piece].astype(jnp.bfloat16)
        for block in range(blocks):
            seq_offset, head_offset = divmod(block, head_count)
            piece = slice(block * padded, (block + 1) * padded)
            part_ref = part_refs[seq_offset]
            part_ref[head_offset, :, lanes(0, p)] = key_parts[p][piece].astype(jnp.bfloat16)
            part_ref[head_offset, :, lanes(HEADS_PER_CHUNK, p)] = value_parts[p][piece].astype(
                jnp.bfloat16
            )


def combine(seq_count, head_count, *refs):
    part_refs, base_ref, send_refs = refs[:seq_count], refs[seq_count], refs[seq_count + 1 :]
    for offset in range(head_count):
        total = part_refs[0][offset].astype(jnp.float32)
        for ref in part_refs[1:]:
            total = total + ref[offset].astype(jnp.float32)
        if offset == 0:
            base_ref[...] = total
        else:
            send_refs[offset - 1][...] = total.astype(jnp.bfloat16)


def finish(head_count, *refs):
    cosine, sine = refs[0][...], refs[1][...]
    key_ref, value_ref = refs[-2:]
    for chunk in range(CHUNKS):
        mine = refs[2 + chunk * head_count : 2 + (chunk + 1) * head_count]
        for place in range(HEADS_PER_CHUNK):
            here, there = head_cols(place), head_cols(HEADS_PER_CHUNK + place)
            key_total, value_total = mine[0][:, here], mine[0][:, there]
            for ref in mine[1:]:
                key_total = key_total + ref[:, here].astype(jnp.float32)
                value_total = value_total + ref[:, there].astype(jnp.float32)
            cols = head_cols(chunk * HEADS_PER_CHUNK + place)
            key_ref[:, cols] = rope_back(key_total, cosine, sine).astype(jnp.bfloat16)
            value_ref[:, cols] = value_total.astype(jnp.bfloat16)


def params(mebibytes):
    return pltpu.CompilerParams(vmem_limit_bytes=mebibytes << 20)


def cost(microseconds):
    return pl.CostEstimate(
        flops=microseconds * 1153 * 10**6,
        bytes_accessed=microseconds * 3690 * 10**3,
        transcendentals=0,
    )


def shards(queries, routed_keys, routed_values, output_gradient, positions, counts):
    seq_count = lax.axis_size("seq")
    head_count = lax.axis_size("head")
    blocks = seq_count * head_count
    rows = queries.shape[0]
    padded = -(-rows // 8) * 8
    if padded != rows:
        extra = ((0, padded - rows), (0, 0))
        queries, routed_keys, routed_values, output_gradient = (
            jnp.pad(x, extra) for x in (queries, routed_keys, routed_values, output_gradient)
        )
    query_rows = GROUP * padded
    shape = jax.ShapeDtypeStruct
    bf16, f32 = jnp.bfloat16, jnp.float32
    ranks = [(s, z) for s in range(seq_count) for z in range(head_count)]

    def rank_of(s, z):
        return s * head_count + z

    def along_head(x, offset, upward, held=0):
        pairs = []
        for s, z in ranks:
            other = z ^ offset
            if s < seq_count - 1 or ((z ^ held) < other) == upward:
                pairs.append((rank_of(s, z), rank_of(s, other)))
        return lax.ppermute(x, ("seq", "head"), pairs)

    def along_seq(x, offset, upward):
        pairs = [
            (rank_of(s, z), rank_of(s ^ offset, z))
            for s, z in ranks
            if (s < (s ^ offset)) == upward
        ]
        return lax.ppermute(x, ("seq", "head"), pairs)

    table = shape((padded, HEAD_WIDTH), f32)
    table_t = shape((HEAD_WIDTH // 2, query_rows), f32)
    piece = shape((padded, 2 * CHUNK_COLS), bf16)
    own = pl.pallas_call(
        functools.partial(prepare_keys, rows),
        out_shape=shape((padded, CHUNKS * 2 * CHUNK_COLS), bf16),
        in_specs=[SMEM, VMEM, VMEM],
        out_specs=VMEM,
        compiler_params=params(56),
        name="prepare_keys",
    )(positions, routed_keys, routed_values)

    wide = GROUP * HEAD_WIDTH
    row_block = pl.BlockSpec((padded, wide), lambda g: (0, g))
    table_block = pl.BlockSpec((padded, HEAD_WIDTH), lambda g: (0, 0))
    tall_block = pl.BlockSpec((1, query_rows, HEAD_WIDTH), lambda g: (g, 0, 0))
    flat_block = pl.BlockSpec((1, HEAD_WIDTH, query_rows), lambda g: (g, 0, 0))
    tall = shape((KEY_VALUE_HEADS, query_rows, HEAD_WIDTH), bf16)
    flat = shape((KEY_VALUE_HEADS, HEAD_WIDTH, query_rows), bf16)
    table_t_block = pl.BlockSpec(table_t.shape, lambda g: (0, 0))
    *stacked, cosine, sine, cosine_t, sine_t = pl.pallas_call(
        functools.partial(prepare_queries, rows),
        grid=(KEY_VALUE_HEADS,),
        out_shape=[tall, flat, tall, flat, table, table, table_t, table_t],
        in_specs=[SMEM, row_block, row_block],
        out_specs=[tall_block, flat_block, tall_block, flat_block]
        + [table_block, table_block, table_t_block, table_t_block],
        cost_estimate=cost(7),
        compiler_params=params(16),
        name="prepare_queries",
    )(positions, queries, output_gradient)

    bits = [1 << b for b in reversed(range((head_count - 1).bit_length()))]
    later = range(1, seq_count)
    last = head_count - 1
    near = {0: own, **{j: along_head(own, j, True) for j in sorted({bits[0], 1}, reverse=True)}}
    far = {a: along_seq(own, a, True) for a in later}
    near, cosine_t, far = lax.optimization_barrier((near, cosine_t, far))
    for bit in bits[1:]:
        near.update(
            {j ^ bit: along_head(x, bit, True, j) for j, x in near.items() if j ^ bit not in near}
        )

    def cross(chunk, offsets):
        held = pl.pallas_call(
            functools.partial(stack, chunk),
            out_shape=shape((len(offsets), padded, 2 * CHUNK_COLS), bf16),
            in_specs=[VMEM] * len(offsets),
            out_specs=VMEM,
            compiler_params=params(8),
            name="stack",
        )(*(near[j] for j in offsets))
        return {a: along_seq(held, a, True) for a in later}

    crossed = [[cross(0, range(1, last)), cross(0, [last])]]
    near[last], crossed[0] = lax.optimization_barrier((near[last], crossed[0]))
    crossed += [[cross(chunk, range(1, head_count))] for chunk in range(1, CHUNKS)]

    wide_outs = ()
    parts = []
    for chunk in range(CHUNKS):
        first = chunk * HEADS_PER_CHUNK // STEP_HEADS
        has_alias = int(chunk > 0)
        tall_part, flat_part = (
            pl.BlockSpec((STEP_HEADS, *x.shape[1:]), lambda g, f=first: (f + g, 0, 0))
            for x in (tall, flat)
        )
        row_part = pl.BlockSpec((padded, STEP_HEADS * wide), lambda g, f=first: (0, f + g))
        gathered = [near[j] for j in range(head_count)]
        for a in later:
            gathered += [far[a]] + [part[a] for part in crossed[chunk]]
        inputs = len(gathered)
        kv_whole = pl.BlockSpec((padded, 2 * CHUNK_COLS), lambda g, c=chunk: (0, c))
        kv_specs = [
            kv_whole if len(x.shape) == 2 else pl.BlockSpec(x.shape, lambda g: (0, 0, 0))
            for x in gathered
        ]
        part_block = pl.BlockSpec((head_count, padded, 2 * CHUNK_COLS), lambda g: (0, 0, 0))
        out = pl.pallas_call(
            functools.partial(attend, seq_count, head_count, rows, inputs, has_alias),
            grid=(HEADS_PER_CHUNK // STEP_HEADS,),
            out_shape=[shape((padded, QUERY_HEADS * HEAD_WIDTH), bf16)] * 2
            + [shape((head_count, padded, 2 * CHUNK_COLS), bf16)] * seq_count,
            in_specs=[SMEM]
            + kv_specs
            + [tall_part, flat_part, tall_part, flat_part, table_t_block, table_t_block]
            + [pl.BlockSpec(memory_space=pl.ANY)] * (2 * has_alias),
            out_specs=[row_part, row_part] + [part_block] * seq_count,
            scratch_shapes=[
                pltpu.VMEM((blocks * padded, query_rows), f32),
                pltpu.VMEM((8, query_rows), f32),
            ],
            input_output_aliases={inputs + 7: 0, inputs + 8: 1} if has_alias else {},
            cost_estimate=cost(10),
            compiler_params=params(32),
            name="attend",
        )(counts, *gathered, *stacked, cosine_t, sine_t, *wide_outs)
        wide_outs = out[:2]
        parts.append([out[2]] + [along_seq(out[2 + a], a, False) for a in later])

    summed = []
    for mine in parts:
        if summed:
            mine[-1], summed[-head_count] = lax.optimization_barrier(
                (mine[-1], summed[-head_count])
            )
        base, *sends = pl.pallas_call(
            functools.partial(combine, seq_count, head_count),
            out_shape=[shape((padded, 2 * CHUNK_COLS), f32)] + [piece] * (head_count - 1),
            in_specs=[VMEM] * seq_count,
            out_specs=[VMEM] * head_count,
            cost_estimate=cost(2),
            compiler_params=params(8),
            name="combine",
        )(*mine)
        summed += [base] + [along_head(x, j + 1, False) for j, x in enumerate(sends)]

    narrow = shape((padded, KEY_VALUE_HEADS * HEAD_WIDTH), bf16)
    key_grad, value_grad = pl.pallas_call(
        functools.partial(finish, head_count),
        out_shape=[narrow, narrow],
        in_specs=[VMEM] * (2 + CHUNKS * head_count),
        out_specs=[VMEM, VMEM],
        cost_estimate=cost(2),
        compiler_params=params(8),
        name="finish",
    )(cosine, sine, *summed)
    results = (*wide_outs, key_grad, value_grad)
    if padded != rows:
        results = tuple(x[:rows] for x in results)
    return results


def solution(mesh):
    rows = P(("dp", "seq", "head"), None)
    return jax.shard_map(
        shards,
        mesh=mesh,
        in_specs=(rows, rows, rows, rows, P("dp"), P("dp")),
        out_specs=(rows, rows, rows, rows),
        check_vma=False,
    )
```

```python
import functools

import jax
import jax.numpy as jnp
import numpy as np
from jax import lax
from jax.experimental import pallas as pl
from jax.experimental.pallas import tpu as pltpu
from jax.sharding import PartitionSpec as P

QUERY_HEADS = 64
KEY_VALUE_HEADS = 8
HEAD_WIDTH = 128
GROUP = QUERY_HEADS // KEY_VALUE_HEADS
ROPE_BASE = 500000.0
SCORE_SCALE = 1.0 / float(np.sqrt(HEAD_WIDTH))
SCORE_TO_LOG2 = SCORE_SCALE * 1.4426950408889634
CHUNKS = 2
HEADS_PER_CHUNK = KEY_VALUE_HEADS // CHUNKS
CHUNK_COLS = HEADS_PER_CHUNK * HEAD_WIDTH
STEP_HEADS = 2
VMEM = pl.BlockSpec(memory_space=pltpu.VMEM)
SMEM = pl.BlockSpec(memory_space=pltpu.SMEM)


def inverse_freq_row():
    half = HEAD_WIDTH // 2
    place = lax.rem(lax.broadcasted_iota(jnp.int32, (8, HEAD_WIDTH), 1), half)
    row = jnp.ones((8, HEAD_WIDTH), jnp.float32)
    for i in range(1, half):
        row = jnp.where(place == i, np.float32(ROPE_BASE ** (-2.0 * i / HEAD_WIDTH)), row)
    return row[0:1]


def angle_tables(rows, padded, pos_ref):
    start = (lax.axis_index("seq") * lax.axis_size("head") + lax.axis_index("head")) * rows
    sublane = lax.broadcasted_iota(jnp.int32, (8, HEAD_WIDTH), 0)
    pieces = []
    for base in range(0, padded, 8):
        piece = jnp.zeros((8, HEAD_WIDTH), jnp.int32)
        for offset in range(min(8, rows - base)):
            piece = jnp.where(sublane == offset, pos_ref[start + (base + offset)], piece)
        pieces.append(piece)
    angle = jnp.concatenate(pieces, 0).astype(jnp.float32) * inverse_freq_row()
    lane = lax.broadcasted_iota(jnp.int32, angle.shape, 1)
    return jnp.cos(angle), jnp.sin(angle) * jnp.where(lane < HEAD_WIDTH // 2, -1.0, 1.0)


def rope(vectors, cosine, sine):
    return vectors * cosine + pltpu.roll(vectors, HEAD_WIDTH // 2, 1) * sine


def rope_back(vectors, cosine, sine):
    return vectors * cosine - pltpu.roll(vectors, HEAD_WIDTH // 2, 1) * sine


def head_cols(index):
    return slice(index * HEAD_WIDTH, (index + 1) * HEAD_WIDTH)


def prepare_keys(rows, pos_ref, key_ref, value_ref, kv_ref):
    cosine, sine = angle_tables(rows, key_ref.shape[0], pos_ref)
    for head in range(KEY_VALUE_HEADS):
        chunk, place = divmod(head, HEADS_PER_CHUNK)
        place += 2 * chunk * HEADS_PER_CHUNK
        rotated = rope(key_ref[:, head_cols(head)].astype(jnp.float32), cosine, sine)
        kv_ref[:, head_cols(place)] = rotated.astype(jnp.bfloat16)
        kv_ref[:, head_cols(HEADS_PER_CHUNK + place)] = value_ref[:, head_cols(head)]


def stack(chunk, *refs):
    *block_refs, stack_ref = refs
    for place, ref in enumerate(block_refs):
        stack_ref[place] = ref[:, 2 * chunk * CHUNK_COLS : 2 * (chunk + 1) * CHUNK_COLS]


def prepare_queries(rows, pos_ref, query_ref, grad_ref, *out_refs):
    q_ref, qt_ref, g_ref, gt_ref, cos_ref, sin_ref, cos_t_ref, sin_t_ref = out_refs

    @pl.when(pl.program_id(0) == 0)
    def _():
        cosine, sine = angle_tables(rows, query_ref.shape[0], pos_ref)
        cos_ref[...] = cosine
        sin_ref[...] = sine
        half = HEAD_WIDTH // 2
        cos_t_ref[...] = jnp.concatenate([cosine] * GROUP, 0).T[half:] * SCORE_SCALE
        sin_t_ref[...] = jnp.concatenate([sine] * GROUP, 0).T[half:] * SCORE_SCALE

    cosine, sine = cos_ref[...], sin_ref[...]
    queries = jnp.concatenate(
        [
            rope(query_ref[:, head_cols(h)].astype(jnp.float32), cosine, sine)
            for h in range(GROUP)
        ],
        0,
    )
    grads = jnp.concatenate(
        [grad_ref[:, head_cols(h)].astype(jnp.float32) for h in range(GROUP)], 0
    )
    q_ref[0] = queries.astype(jnp.bfloat16)
    qt_ref[0] = queries.T.astype(jnp.bfloat16)
    g_ref[0] = grads.astype(jnp.bfloat16)
    gt_ref[0] = grads.T.astype(jnp.bfloat16)


def dot(left, right):
    return jnp.dot(left, right, preferred_element_type=jnp.float32)


def attend(seq_count, head_count, rows, pieces, has_alias, counts_ref, *refs):
    blocks = seq_count * head_count
    kv_refs = []
    for ref in refs[:pieces]:
        kv_refs += [ref] if len(ref.shape) == 2 else [ref.at[i] for i in range(ref.shape[0])]
    q_ref, qt_ref, g_ref, gt_ref, cos_ref, sin_ref = refs[pieces : pieces + 6]
    outs = refs[pieces + 6 + 2 * has_alias :]
    out_ref, grad_ref = outs[:2]
    part_refs = outs[2 : 2 + seq_count]
    bias_ref, live_ref = outs[2 + seq_count :]
    padded = kv_refs[0].shape[0]
    query_rows = GROUP * padded
    step = pl.program_id(0)
    seq_index, head_index = lax.axis_index("seq"), lax.axis_index("head")
    my_rank = seq_index * head_count + head_index

    @pl.when(step == 0)
    def _():
        key_row = lax.broadcasted_iota(jnp.int32, (padded, query_rows), 0)
        query_row = lax.rem(lax.broadcasted_iota(jnp.int32, (padded, query_rows), 1), padded)
        for block in range(blocks):
            seq_offset, head_offset = divmod(block, head_count)
            seq_from = jnp.bitwise_xor(seq_index, seq_offset)
            head_from = jnp.bitwise_xor(head_index, head_offset)
            rank = seq_from * head_count + head_from
            limit = jnp.minimum(counts_ref[seq_from] - head_from * rows, rows)
            limit = jnp.where(rank <= my_rank, limit, 0)
            allowed = key_row < limit
            if block == 0:
                allowed = allowed & (key_row <= query_row)
                live_ref[...] = (query_row[:8] < limit).astype(jnp.float32)
            bias_ref[block * padded : (block + 1) * padded, :] = jnp.where(allowed, 0.0, -1e30)

    def lanes(first, place):
        start = pl.multiple_of((first + step * STEP_HEADS + place) * HEAD_WIDTH, HEAD_WIDTH)
        return pl.ds(start, HEAD_WIDTH)

    def gathered(first, place):
        cols = lanes(first, place)
        wide = jnp.concatenate([ref[:, cols].astype(jnp.float32) for ref in kv_refs], 0)
        low = wide.astype(jnp.bfloat16)
        return low, low.T

    heads = range(STEP_HEADS)
    keys, values = [gathered(0, p) for p in heads], [gathered(HEADS_PER_CHUNK, p) for p in heads]
    bias, live = bias_ref[...], live_ref[0:1, :]
    scores = [dot(keys[p][0], qt_ref[p]) * SCORE_TO_LOG2 + bias for p in heads]
    probs_low = []
    for p in heads:
        weights = jnp.exp2(scores[p] - jnp.max(scores[p], 0, keepdims=True))
        factor = live / jnp.sum(weights, 0, keepdims=True)
        probs_low.append((weights * factor).astype(jnp.bfloat16))
    outs_t, value_parts, dscores = [], [], []
    for p in heads:
        outs_t.append(dot(values[p][1], probs_low[p]))
        value_parts.append(dot(probs_low[p], g_ref[p]))
        out_low = outs_t[p].astype(jnp.bfloat16).astype(jnp.float32)
        delta = jnp.sum(gt_ref[p].astype(jnp.float32) * out_low, 0, keepdims=True)
        dscores.append(probs_low[p] * (dot(values[p][0], gt_ref[p]) - delta).astype(jnp.bfloat16))
    grads_t = [dot(keys[p][1], dscores[p]) for p in heads]
    key_parts = [dot(dscores[p], q_ref[p]) * SCORE_SCALE for p in heads]

    cosine, sine = cos_ref[...], sin_ref[...]
    half = HEAD_WIDTH // 2
    for p in heads:
        first, second = grads_t[p][:half], grads_t[p][half:]
        turned = [first * cosine + second * sine, second * cosine - first * sine]
        grad_low = jnp.concatenate(turned, 0).astype(jnp.bfloat16)
        out_heads = outs_t[p].astype(jnp.bfloat16).T.astype(jnp.float32)
        grad_heads = grad_low.T.astype(jnp.float32)
        for h in range(GROUP):
            piece, cols = slice(h * padded, (h + 1) * padded), head_cols(p * GROUP + h)
            out_ref[:, cols] = out_heads[piece].astype(jnp.bfloat16)
            grad_ref[:, cols] = grad_heads[piece].astype(jnp.bfloat16)
        for block in range(blocks):
            seq_offset, head_offset = divmod(block, head_count)
            piece = slice(block * padded, (block + 1) * padded)
            part_ref = part_refs[seq_offset]
            part_ref[head_offset, :, lanes(0, p)] = key_parts[p][piece].astype(jnp.bfloat16)
            part_ref[head_offset, :, lanes(HEADS_PER_CHUNK, p)] = value_parts[p][piece].astype(
                jnp.bfloat16
            )


def combine(seq_count, head_count, *refs):
    part_refs, base_ref, send_refs = refs[:seq_count], refs[seq_count], refs[seq_count + 1 :]
    for offset in range(head_count):
        total = part_refs[0][offset].astype(jnp.float32)
        for ref in part_refs[1:]:
            total = total + ref[offset].astype(jnp.float32)
        if offset == 0:
            base_ref[...] = total
        else:
            send_refs[offset - 1][...] = total.astype(jnp.bfloat16)


def finish(head_count, *refs):
    cosine, sine = refs[0][...], refs[1][...]
    key_ref, value_ref = refs[-2:]
    for chunk in range(CHUNKS):
        mine = refs[2 + chunk * head_count : 2 + (chunk + 1) * head_count]
        for place in range(HEADS_PER_CHUNK):
            here, there = head_cols(place), head_cols(HEADS_PER_CHUNK + place)
            key_total, value_total = mine[0][:, here], mine[0][:, there]
            for ref in mine[1:]:
                key_total = key_total + ref[:, here].astype(jnp.float32)
                value_total = value_total + ref[:, there].astype(jnp.float32)
            cols = head_cols(chunk * HEADS_PER_CHUNK + place)
            key_ref[:, cols] = rope_back(key_total, cosine, sine).astype(jnp.bfloat16)
            value_ref[:, cols] = value_total.astype(jnp.bfloat16)


def params(mebibytes):
    return pltpu.CompilerParams(vmem_limit_bytes=mebibytes << 20)


def cost(microseconds):
    return pl.CostEstimate(
        flops=microseconds * 1153 * 10**6,
        bytes_accessed=microseconds * 3690 * 10**3,
        transcendentals=0,
    )


def shards(queries, routed_keys, routed_values, output_gradient, positions, counts):
    seq_count = lax.axis_size("seq")
    head_count = lax.axis_size("head")
    blocks = seq_count * head_count
    rows = queries.shape[0]
    padded = -(-rows // 8) * 8
    if padded != rows:
        extra = ((0, padded - rows), (0, 0))
        queries, routed_keys, routed_values, output_gradient = (
            jnp.pad(x, extra) for x in (queries, routed_keys, routed_values, output_gradient)
        )
    query_rows = GROUP * padded
    shape = jax.ShapeDtypeStruct
    bf16, f32 = jnp.bfloat16, jnp.float32
    ranks = [(s, z) for s in range(seq_count) for z in range(head_count)]

    def rank_of(s, z):
        return s * head_count + z

    def along_head(x, offset, upward, held=0):
        pairs = []
        for s, z in ranks:
            other = z ^ offset
            if s < seq_count - 1 or ((z ^ held) < other) == upward:
                pairs.append((rank_of(s, z), rank_of(s, other)))
        return lax.ppermute(x, ("seq", "head"), pairs)

    def along_seq(x, offset, upward):
        pairs = [
            (rank_of(s, z), rank_of(s ^ offset, z))
            for s, z in ranks
            if (s < (s ^ offset)) == upward
        ]
        return lax.ppermute(x, ("seq", "head"), pairs)

    table = shape((padded, HEAD_WIDTH), f32)
    table_t = shape((HEAD_WIDTH // 2, query_rows), f32)
    piece = shape((padded, 2 * CHUNK_COLS), bf16)
    own = pl.pallas_call(
        functools.partial(prepare_keys, rows),
        out_shape=shape((padded, CHUNKS * 2 * CHUNK_COLS), bf16),
        in_specs=[SMEM, VMEM, VMEM],
        out_specs=VMEM,
        compiler_params=params(56),
        name="prepare_keys",
    )(positions, routed_keys, routed_values)

    wide = GROUP * HEAD_WIDTH
    row_block = pl.BlockSpec((padded, wide), lambda g: (0, g))
    table_block = pl.BlockSpec((padded, HEAD_WIDTH), lambda g: (0, 0))
    tall_block = pl.BlockSpec((1, query_rows, HEAD_WIDTH), lambda g: (g, 0, 0))
    flat_block = pl.BlockSpec((1, HEAD_WIDTH, query_rows), lambda g: (g, 0, 0))
    tall = shape((KEY_VALUE_HEADS, query_rows, HEAD_WIDTH), bf16)
    flat = shape((KEY_VALUE_HEADS, HEAD_WIDTH, query_rows), bf16)
    table_t_block = pl.BlockSpec(table_t.shape, lambda g: (0, 0))
    *stacked, cosine, sine, cosine_t, sine_t = pl.pallas_call(
        functools.partial(prepare_queries, rows),
        grid=(KEY_VALUE_HEADS,),
        out_shape=[tall, flat, tall, flat, table, table, table_t, table_t],
        in_specs=[SMEM, row_block, row_block],
        out_specs=[tall_block, flat_block, tall_block, flat_block]
        + [table_block, table_block, table_t_block, table_t_block],
        cost_estimate=cost(7),
        compiler_params=params(16),
        name="prepare_queries",
    )(positions, queries, output_gradient)

    bits = [1 << b for b in reversed(range((head_count - 1).bit_length()))]
    later = range(1, seq_count)
    last = head_count - 1
    near = {j: along_head(own, j, True) for j in sorted({bits[0], 1}, reverse=True)}
    crossing, cosine_t = lax.optimization_barrier((own, cosine_t))
    far = {a: along_seq(crossing, a, True) for a in later}
    near[1], far, cosine_t = lax.optimization_barrier((near[1], far, cosine_t))
    near[0] = own
    for bit in bits[1:]:
        near.update(
            {j ^ bit: along_head(x, bit, True, j) for j, x in near.items() if j ^ bit not in near}
        )

    def cross(chunk, offsets):
        held = pl.pallas_call(
            functools.partial(stack, chunk),
            out_shape=shape((len(offsets), padded, 2 * CHUNK_COLS), bf16),
            in_specs=[VMEM] * len(offsets),
            out_specs=VMEM,
            compiler_params=params(8),
            name="stack",
        )(*(near[j] for j in offsets))
        return {a: along_seq(held, a, True) for a in later}

    crossed = [[cross(0, range(1, last)), cross(0, [last])]]
    near[last], crossed[0][0] = lax.optimization_barrier((near[last], crossed[0][0]))
    crossed += [[cross(chunk, range(1, head_count))] for chunk in range(1, CHUNKS)]

    wide_outs = ()
    parts = []
    for chunk in range(CHUNKS):
        first = chunk * HEADS_PER_CHUNK // STEP_HEADS
        has_alias = int(chunk > 0)
        tall_part, flat_part = (
            pl.BlockSpec((STEP_HEADS, *x.shape[1:]), lambda g, f=first: (f + g, 0, 0))
            for x in (tall, flat)
        )
        row_part = pl.BlockSpec((padded, STEP_HEADS * wide), lambda g, f=first: (0, f + g))
        gathered = [near[j] for j in range(head_count)]
        for a in later:
            gathered += [far[a]] + [part[a] for part in crossed[chunk]]
        inputs = len(gathered)
        kv_whole = pl.BlockSpec((padded, 2 * CHUNK_COLS), lambda g, c=chunk: (0, c))
        kv_specs = [
            kv_whole if len(x.shape) == 2 else pl.BlockSpec(x.shape, lambda g: (0, 0, 0))
            for x in gathered
        ]
        part_block = pl.BlockSpec((head_count, padded, 2 * CHUNK_COLS), lambda g: (0, 0, 0))
        out = pl.pallas_call(
            functools.partial(attend, seq_count, head_count, rows, inputs, has_alias),
            grid=(HEADS_PER_CHUNK // STEP_HEADS,),
            out_shape=[shape((padded, QUERY_HEADS * HEAD_WIDTH), bf16)] * 2
            + [shape((head_count, padded, 2 * CHUNK_COLS), bf16)] * seq_count,
            in_specs=[SMEM]
            + kv_specs
            + [tall_part, flat_part, tall_part, flat_part, table_t_block, table_t_block]
            + [pl.BlockSpec(memory_space=pl.ANY)] * (2 * has_alias),
            out_specs=[row_part, row_part] + [part_block] * seq_count,
            scratch_shapes=[
                pltpu.VMEM((blocks * padded, query_rows), f32),
                pltpu.VMEM((8, query_rows), f32),
            ],
            input_output_aliases={inputs + 7: 0, inputs + 8: 1} if has_alias else {},
            cost_estimate=cost(10),
            compiler_params=params(32),
            name="attend",
        )(counts, *gathered, *stacked, cosine_t, sine_t, *wide_outs)
        wide_outs = out[:2]
        parts.append([out[2]] + [along_seq(out[2 + a], a, False) for a in later])

    summed = []
    for mine in parts:
        if summed:
            mine[-1], summed[-head_count] = lax.optimization_barrier(
                (mine[-1], summed[-head_count])
            )
        base, *sends = pl.pallas_call(
            functools.partial(combine, seq_count, head_count),
            out_shape=[shape((padded, 2 * CHUNK_COLS), f32)] + [piece] * (head_count - 1),
            in_specs=[VMEM] * seq_count,
            out_specs=[VMEM] * head_count,
            cost_estimate=cost(2),
            compiler_params=params(8),
            name="combine",
        )(*mine)
        summed += [base] + [along_head(x, j + 1, False) for j, x in enumerate(sends)]

    narrow = shape((padded, KEY_VALUE_HEADS * HEAD_WIDTH), bf16)
    key_grad, value_grad = pl.pallas_call(
        functools.partial(finish, head_count),
        out_shape=[narrow, narrow],
        in_specs=[VMEM] * (2 + CHUNKS * head_count),
        out_specs=[VMEM, VMEM],
        cost_estimate=cost(2),
        compiler_params=params(8),
        name="finish",
    )(cosine, sine, *summed)
    results = (*wide_outs, key_grad, value_grad)
    if padded != rows:
        results = tuple(x[:rows] for x in results)
    return results


def solution(mesh):
    rows = P(("dp", "seq", "head"), None)
    return jax.shard_map(
        shards,
        mesh=mesh,
        in_specs=(rows, rows, rows, rows, P("dp"), P("dp")),
        out_specs=(rows, rows, rows, rows),
        check_vma=False,
    )
```

```python
import functools

import jax
import jax.numpy as jnp
import numpy as np
from jax import lax
from jax.experimental import pallas as pl
from jax.experimental.pallas import tpu as pltpu
from jax.sharding import PartitionSpec as P

QUERY_HEADS = 64
KEY_VALUE_HEADS = 8
HEAD_WIDTH = 128
GROUP = QUERY_HEADS // KEY_VALUE_HEADS
ROPE_BASE = 500000.0
SCORE_SCALE = 1.0 / float(np.sqrt(HEAD_WIDTH))
SCORE_TO_LOG2 = SCORE_SCALE * 1.4426950408889634
CHUNKS = 2
HEADS_PER_CHUNK = KEY_VALUE_HEADS // CHUNKS
CHUNK_COLS = HEADS_PER_CHUNK * HEAD_WIDTH
STEP_HEADS = 4
VMEM = pl.BlockSpec(memory_space=pltpu.VMEM)
SMEM = pl.BlockSpec(memory_space=pltpu.SMEM)


def inverse_freq_row():
    half = HEAD_WIDTH // 2
    place = lax.rem(lax.broadcasted_iota(jnp.int32, (8, HEAD_WIDTH), 1), half)
    row = jnp.ones((8, HEAD_WIDTH), jnp.float32)
    for i in range(1, half):
        row = jnp.where(place == i, np.float32(ROPE_BASE ** (-2.0 * i / HEAD_WIDTH)), row)
    return row[0:1]


def angle_tables(rows, padded, pos_ref):
    start = (lax.axis_index("seq") * lax.axis_size("head") + lax.axis_index("head")) * rows
    sublane = lax.broadcasted_iota(jnp.int32, (8, HEAD_WIDTH), 0)
    pieces = []
    for base in range(0, padded, 8):
        piece = jnp.zeros((8, HEAD_WIDTH), jnp.int32)
        for offset in range(min(8, rows - base)):
            piece = jnp.where(sublane == offset, pos_ref[start + (base + offset)], piece)
        pieces.append(piece)
    angle = jnp.concatenate(pieces, 0).astype(jnp.float32) * inverse_freq_row()
    lane = lax.broadcasted_iota(jnp.int32, angle.shape, 1)
    return jnp.cos(angle), jnp.sin(angle) * jnp.where(lane < HEAD_WIDTH // 2, -1.0, 1.0)


def rope(vectors, cosine, sine):
    return vectors * cosine + pltpu.roll(vectors, HEAD_WIDTH // 2, 1) * sine


def rope_back(vectors, cosine, sine):
    return vectors * cosine - pltpu.roll(vectors, HEAD_WIDTH // 2, 1) * sine


def head_cols(index):
    return slice(index * HEAD_WIDTH, (index + 1) * HEAD_WIDTH)


def prepare_keys(rows, pos_ref, key_ref, value_ref, kv_ref):
    cosine, sine = angle_tables(rows, key_ref.shape[0], pos_ref)
    for head in range(KEY_VALUE_HEADS):
        chunk, place = divmod(head, HEADS_PER_CHUNK)
        place += 2 * chunk * HEADS_PER_CHUNK
        rotated = rope(key_ref[:, head_cols(head)].astype(jnp.float32), cosine, sine)
        kv_ref[:, head_cols(place)] = rotated.astype(jnp.bfloat16)
        kv_ref[:, head_cols(HEADS_PER_CHUNK + place)] = value_ref[:, head_cols(head)]


def stack(chunk, *refs):
    *block_refs, stack_ref = refs
    for place, ref in enumerate(block_refs):
        stack_ref[place] = ref[:, 2 * chunk * CHUNK_COLS : 2 * (chunk + 1) * CHUNK_COLS]


def prepare_queries(rows, pos_ref, query_ref, grad_ref, *out_refs):
    q_ref, qt_ref, g_ref, gt_ref, cos_ref, sin_ref, cos_t_ref, sin_t_ref = out_refs

    @pl.when(pl.program_id(0) == 0)
    def _():
        cosine, sine = angle_tables(rows, query_ref.shape[0], pos_ref)
        cos_ref[...] = cosine
        sin_ref[...] = sine
        half = HEAD_WIDTH // 2
        cos_t_ref[...] = jnp.concatenate([cosine] * GROUP, 0).T[half:] * SCORE_SCALE
        sin_t_ref[...] = jnp.concatenate([sine] * GROUP, 0).T[half:] * SCORE_SCALE

    cosine, sine = cos_ref[...], sin_ref[...]
    queries = jnp.concatenate(
        [
            rope(query_ref[:, head_cols(h)].astype(jnp.float32), cosine, sine)
            for h in range(GROUP)
        ],
        0,
    )
    grads = jnp.concatenate(
        [grad_ref[:, head_cols(h)].astype(jnp.float32) for h in range(GROUP)], 0
    )
    q_ref[0] = queries.astype(jnp.bfloat16)
    qt_ref[0] = queries.T.astype(jnp.bfloat16)
    g_ref[0] = grads.astype(jnp.bfloat16)
    gt_ref[0] = grads.T.astype(jnp.bfloat16)


def dot(left, right):
    return jnp.dot(left, right, preferred_element_type=jnp.float32)


def attend(seq_count, head_count, rows, chunk, pieces, counts_ref, *refs):
    blocks = seq_count * head_count
    kv_refs = []
    for ref in refs[:pieces]:
        if len(ref.shape) == 2:
            kv_refs.append(ref.at[:, 2 * chunk * CHUNK_COLS : 2 * (chunk + 1) * CHUNK_COLS])
        else:
            kv_refs += [ref.at[i] for i in range(ref.shape[0])]
    q_ref, qt_ref, g_ref, gt_ref, cos_ref, sin_ref = refs[pieces : pieces + 6]
    outs = refs[pieces + 6 + 2 * int(chunk > 0) :]
    out_ref, grad_ref = outs[:2]
    part_refs = outs[2 : 2 + seq_count]
    bias_ref, live_ref = outs[2 + seq_count :]
    padded = kv_refs[0].shape[0]
    query_rows = GROUP * padded
    seq_index, head_index = lax.axis_index("seq"), lax.axis_index("head")
    my_rank = seq_index * head_count + head_index

    key_row = lax.broadcasted_iota(jnp.int32, (padded, query_rows), 0)
    query_row = lax.rem(lax.broadcasted_iota(jnp.int32, (padded, query_rows), 1), padded)
    for block in range(blocks):
        seq_offset, head_offset = divmod(block, head_count)
        seq_from = jnp.bitwise_xor(seq_index, seq_offset)
        head_from = jnp.bitwise_xor(head_index, head_offset)
        rank = seq_from * head_count + head_from
        limit = jnp.minimum(counts_ref[seq_from] - head_from * rows, rows)
        limit = jnp.where(rank <= my_rank, limit, 0)
        allowed = key_row < limit
        if block == 0:
            allowed = allowed & (key_row <= query_row)
            live_ref[...] = (query_row[:8] < limit).astype(jnp.float32)
        bias_ref[block * padded : (block + 1) * padded, :] = jnp.where(allowed, 0.0, -1e30)

    @pl.loop(0, HEADS_PER_CHUNK // STEP_HEADS)
    def _(step):
        first_head = chunk * HEADS_PER_CHUNK + step * STEP_HEADS

        def lanes(first, place):
            start = pl.multiple_of((first + step * STEP_HEADS + place) * HEAD_WIDTH, HEAD_WIDTH)
            return pl.ds(start, HEAD_WIDTH)

        def query_lanes(place, head):
            start = (step * STEP_HEADS + place) * GROUP * HEAD_WIDTH + head * HEAD_WIDTH
            start = pl.multiple_of(start, HEAD_WIDTH)
            return pl.ds(start, HEAD_WIDTH)

        def gathered(first, place):
            cols = lanes(first, place)
            wide = jnp.concatenate([ref[:, cols].astype(jnp.float32) for ref in kv_refs], 0)
            low = wide.astype(jnp.bfloat16)
            return low, low.T

        heads = range(STEP_HEADS)
        keys, values = [gathered(0, p) for p in heads], [gathered(HEADS_PER_CHUNK, p) for p in heads]
        bias, live = bias_ref[...], live_ref[0:1, :]
        scores = [dot(keys[p][0], qt_ref[first_head + p]) * SCORE_TO_LOG2 + bias for p in heads]
        probs_low = []
        for p in heads:
            weights = jnp.exp2(scores[p] - jnp.max(scores[p], 0, keepdims=True))
            factor = live / jnp.sum(weights, 0, keepdims=True)
            probs_low.append((weights * factor).astype(jnp.bfloat16))
        outs_t, value_parts, dscores = [], [], []
        for p in heads:
            grads_in = gt_ref[first_head + p]
            outs_t.append(dot(values[p][1], probs_low[p]))
            value_parts.append(dot(probs_low[p], g_ref[first_head + p]))
            out_low = outs_t[p].astype(jnp.bfloat16).astype(jnp.float32)
            delta = jnp.sum(grads_in.astype(jnp.float32) * out_low, 0, keepdims=True)
            dprob = dot(values[p][0], grads_in) - delta
            dscores.append(probs_low[p] * dprob.astype(jnp.bfloat16))
        grads_t = [dot(keys[p][1], dscores[p]) for p in heads]
        key_parts = [dot(dscores[p], q_ref[first_head + p]) * SCORE_SCALE for p in heads]

        cosine, sine = cos_ref[...], sin_ref[...]
        half = HEAD_WIDTH // 2
        for p in heads:
            first, second = grads_t[p][:half], grads_t[p][half:]
            turned = [first * cosine + second * sine, second * cosine - first * sine]
            grad_low = jnp.concatenate(turned, 0).astype(jnp.bfloat16)
            out_heads = outs_t[p].astype(jnp.bfloat16).T.astype(jnp.float32)
            grad_heads = grad_low.T.astype(jnp.float32)
            for h in range(GROUP):
                piece, cols = slice(h * padded, (h + 1) * padded), query_lanes(p, h)
                out_ref[:, cols] = out_heads[piece].astype(jnp.bfloat16)
                grad_ref[:, cols] = grad_heads[piece].astype(jnp.bfloat16)
            for block in range(blocks):
                seq_offset, head_offset = divmod(block, head_count)
                piece = slice(block * padded, (block + 1) * padded)
                part_ref = part_refs[seq_offset]
                part_ref[head_offset, :, lanes(0, p)] = key_parts[p][piece].astype(jnp.bfloat16)
                part_ref[head_offset, :, lanes(HEADS_PER_CHUNK, p)] = value_parts[p][piece].astype(
                    jnp.bfloat16
                )


def combine(seq_count, head_count, *refs):
    part_refs, base_ref, send_refs = refs[:seq_count], refs[seq_count], refs[seq_count + 1 :]
    for offset in range(head_count):
        total = part_refs[0][offset].astype(jnp.float32)
        for ref in part_refs[1:]:
            total = total + ref[offset].astype(jnp.float32)
        if offset == 0:
            base_ref[...] = total
        else:
            send_refs[offset - 1][...] = total.astype(jnp.bfloat16)


def finish(head_count, *refs):
    cosine, sine = refs[0][...], refs[1][...]
    key_ref, value_ref = refs[-2:]
    for chunk in range(CHUNKS):
        mine = refs[2 + chunk * head_count : 2 + (chunk + 1) * head_count]
        for place in range(HEADS_PER_CHUNK):
            here, there = head_cols(place), head_cols(HEADS_PER_CHUNK + place)
            key_total, value_total = mine[0][:, here], mine[0][:, there]
            for ref in mine[1:]:
                key_total = key_total + ref[:, here].astype(jnp.float32)
                value_total = value_total + ref[:, there].astype(jnp.float32)
            cols = head_cols(chunk * HEADS_PER_CHUNK + place)
            key_ref[:, cols] = rope_back(key_total, cosine, sine).astype(jnp.bfloat16)
            value_ref[:, cols] = value_total.astype(jnp.bfloat16)


def params(mebibytes):
    return pltpu.CompilerParams(vmem_limit_bytes=mebibytes << 20)


def cost(microseconds):
    return pl.CostEstimate(
        flops=microseconds * 1153 * 10**6,
        bytes_accessed=microseconds * 3690 * 10**3,
        transcendentals=0,
    )


def shards(queries, routed_keys, routed_values, output_gradient, positions, counts):
    seq_count = lax.axis_size("seq")
    head_count = lax.axis_size("head")
    blocks = seq_count * head_count
    rows = queries.shape[0]
    padded = -(-rows // 8) * 8
    if padded != rows:
        extra = ((0, padded - rows), (0, 0))
        queries, routed_keys, routed_values, output_gradient = (
            jnp.pad(x, extra) for x in (queries, routed_keys, routed_values, output_gradient)
        )
    query_rows = GROUP * padded
    shape = jax.ShapeDtypeStruct
    bf16, f32 = jnp.bfloat16, jnp.float32
    ranks = [(s, z) for s in range(seq_count) for z in range(head_count)]

    def rank_of(s, z):
        return s * head_count + z

    def along_head(x, offset, upward, held=0):
        pairs = []
        for s, z in ranks:
            other = z ^ offset
            if s < seq_count - 1 or ((z ^ held) < other) == upward:
                pairs.append((rank_of(s, z), rank_of(s, other)))
        return lax.ppermute(x, ("seq", "head"), pairs)

    def along_seq(x, offset, upward):
        pairs = [
            (rank_of(s, z), rank_of(s ^ offset, z))
            for s, z in ranks
            if (s < (s ^ offset)) == upward
        ]
        return lax.ppermute(x, ("seq", "head"), pairs)

    table = shape((padded, HEAD_WIDTH), f32)
    table_t = shape((HEAD_WIDTH // 2, query_rows), f32)
    piece = shape((padded, 2 * CHUNK_COLS), bf16)
    own = pl.pallas_call(
        functools.partial(prepare_keys, rows),
        out_shape=shape((padded, CHUNKS * 2 * CHUNK_COLS), bf16),
        in_specs=[SMEM, VMEM, VMEM],
        out_specs=VMEM,
        compiler_params=params(56),
        name="prepare_keys",
    )(positions, routed_keys, routed_values)

    wide = GROUP * HEAD_WIDTH
    row_block = pl.BlockSpec((padded, wide), lambda g: (0, g))
    table_block = pl.BlockSpec((padded, HEAD_WIDTH), lambda g: (0, 0))
    tall_block = pl.BlockSpec((1, query_rows, HEAD_WIDTH), lambda g: (g, 0, 0))
    flat_block = pl.BlockSpec((1, HEAD_WIDTH, query_rows), lambda g: (g, 0, 0))
    tall = shape((KEY_VALUE_HEADS, query_rows, HEAD_WIDTH), bf16)
    flat = shape((KEY_VALUE_HEADS, HEAD_WIDTH, query_rows), bf16)
    table_t_block = pl.BlockSpec(table_t.shape, lambda g: (0, 0))
    *stacked, cosine, sine, cosine_t, sine_t = pl.pallas_call(
        functools.partial(prepare_queries, rows),
        grid=(KEY_VALUE_HEADS,),
        out_shape=[tall, flat, tall, flat, table, table, table_t, table_t],
        in_specs=[SMEM, row_block, row_block],
        out_specs=[tall_block, flat_block, tall_block, flat_block]
        + [table_block, table_block, table_t_block, table_t_block],
        cost_estimate=cost(7),
        compiler_params=params(16),
        name="prepare_queries",
    )(positions, queries, output_gradient)

    bits = [1 << b for b in reversed(range((head_count - 1).bit_length()))]
    later = range(1, seq_count)
    last = head_count - 1
    near = {0: own, **{j: along_head(own, j, True) for j in sorted({bits[0], 1}, reverse=True)}}
    far = {a: along_seq(own, a, True) for a in later}
    near, cosine_t, far = lax.optimization_barrier((near, cosine_t, far))
    for bit in bits[1:]:
        near.update(
            {j ^ bit: along_head(x, bit, True, j) for j, x in near.items() if j ^ bit not in near}
        )

    def cross(chunk, offsets):
        held = pl.pallas_call(
            functools.partial(stack, chunk),
            out_shape=shape((len(offsets), padded, 2 * CHUNK_COLS), bf16),
            in_specs=[VMEM] * len(offsets),
            out_specs=VMEM,
            compiler_params=params(8),
            name="stack",
        )(*(near[j] for j in offsets))
        return {a: along_seq(held, a, True) for a in later}

    crossed = [[cross(0, range(1, last)), cross(0, [last])]]
    near[last], crossed[0][0] = lax.optimization_barrier((near[last], crossed[0][0]))
    crossed += [[cross(chunk, range(1, head_count))] for chunk in range(1, CHUNKS)]

    wide_outs = ()
    parts = []
    for chunk in range(CHUNKS):
        has_alias = int(chunk > 0)
        gathered = [near[j] for j in range(head_count)]
        for a in later:
            gathered += [far[a]] + [part[a] for part in crossed[chunk]]
        inputs = len(gathered)
        out = pl.pallas_call(
            functools.partial(attend, seq_count, head_count, rows, chunk, inputs),
            out_shape=[shape((padded, QUERY_HEADS * HEAD_WIDTH), bf16)] * 2
            + [shape((head_count, padded, 2 * CHUNK_COLS), bf16)] * seq_count,
            in_specs=[SMEM]
            + [VMEM] * (inputs + 6)
            + [pl.BlockSpec(memory_space=pl.ANY)] * (2 * has_alias),
            out_specs=[pl.BlockSpec((padded, HEADS_PER_CHUNK * wide), lambda i, c=chunk: (0, c))] * 2
            + [VMEM] * seq_count,
            grid=(1,),
            scratch_shapes=[
                pltpu.VMEM((blocks * padded, query_rows), f32),
                pltpu.VMEM((8, query_rows), f32),
            ],
            input_output_aliases={inputs + 7: 0, inputs + 8: 1} if has_alias else {},
            cost_estimate=cost(10),
            compiler_params=params(32),
            name="attend",
        )(counts, *gathered, *stacked, cosine_t, sine_t, *wide_outs)
        wide_outs = out[:2]
        parts.append([out[2]] + [along_seq(out[2 + a], a, False) for a in later])

    summed = []
    for mine in parts:
        if summed:
            mine[-1], summed[-head_count] = lax.optimization_barrier(
                (mine[-1], summed[-head_count])
            )
        base, *sends = pl.pallas_call(
            functools.partial(combine, seq_count, head_count),
            out_shape=[shape((padded, 2 * CHUNK_COLS), f32)] + [piece] * (head_count - 1),
            in_specs=[VMEM] * seq_count,
            out_specs=[VMEM] * head_count,
            cost_estimate=cost(2),
            compiler_params=params(8),
            name="combine",
        )(*mine)
        summed += [base] + [along_head(x, j + 1, False) for j, x in enumerate(sends)]

    narrow = shape((padded, KEY_VALUE_HEADS * HEAD_WIDTH), bf16)
    key_grad, value_grad = pl.pallas_call(
        functools.partial(finish, head_count),
        out_shape=[narrow, narrow],
        in_specs=[VMEM] * (2 + CHUNKS * head_count),
        out_specs=[VMEM, VMEM],
        cost_estimate=cost(2),
        compiler_params=params(8),
        name="finish",
    )(cosine, sine, *summed)
    results = (*wide_outs, key_grad, value_grad)
    if padded != rows:
        results = tuple(x[:rows] for x in results)
    return results


def solution(mesh):
    rows = P(("dp", "seq", "head"), None)
    return jax.shard_map(
        shards,
        mesh=mesh,
        in_specs=(rows, rows, rows, rows, P("dp"), P("dp")),
        out_specs=(rows, rows, rows, rows),
        check_vma=False,
    )
```
